32 devices in a mesh: mem: 8 (over y, x, core), tile: 4 (over z).
Axes of the slice: x: 2, y: 2, z: 4, core: 2. Of those that a mesh axis runs over, the one named last changes fastest.
Arguments:
- starting_ensemble: bfloat16 [16, 8, 32, 1120], P('mem', None, 'tile'), may hold values from -6 to 6
- patch_lifting: bfloat16 [1120, 768], P('mem'), may hold values from -0.1875 to 0.1875
- query_keyvalue_lift: bfloat16 [768, 2304], P(None, 'mem'), may hold values from -0.21875 to 0.21875
- output_combiner: bfloat16 [768, 768], P(None, 'mem'), may hold values from -0.21875 to 0.21875
- decoder_linear_map: bfloat16 [768, 1120], P(None, 'mem'), may hold values from -0.21875 to 0.21875
- cosine_logit_scale: float32 [12], replicated, may hold values from 2 to 30
- sensor_variable_loadings: bfloat16 [16, 70], replicated, may hold values from -0.75 to 0.75
- sensor_gridpoint: int32 [8, 4, 256], P('mem', 'tile'), may hold values from 0 to 127, as said below
- sensor_domain_index: int32 [8, 4, 256], P('mem', 'tile'), may hold values from 0 to 7, as said below
- sensor_channel_list: int32 [8, 4, 256], P('mem', 'tile'), may hold values from 0 to 15
- sensor_reading: float32 [8, 4, 256], P('mem', 'tile'), may hold values from -6 to 6
- sensor_noise_deviation: float32 [8, 4, 256], P('mem', 'tile'), may hold values from 0.5 to 2
Outputs:
- analysis: bfloat16 [16, 8, 32, 1120], P('mem', None, 'tile')
The draws below stay inside these ranges and needn't reach their ends.
Inputs may be any that keep to these rules, and one draw needn't show every extreme that they name: `sensor_gridpoint`: a point of the piece's 8 tokens. `sensor_domain_index`: differs by at most one from sensor_gridpoint // 16 of the same observation.
All inputs are finite; a program needn't handle non-finite values. Where the reference program divides by a largest or mean magnitude, that divisor is 1e-20 or more.
Results may differ from the reference program's by a relative error of at most 0.039.
Values may be sent and summed in bfloat16 or wider, within the bound.
A program may use at most 64 MiB of HBM per device.

```python
import math
import jax
import jax.numpy as jnp
from jax import lax

VARS = 70
PATCH = 16
FEAT = 1120
FOCUS_COUNT = 12
D = 768
PANE_SIDE = 8
ENS = 16
LAT = 8
LON_DEV = 8
LON = 32
TOKP = 8
OBS_DEV = 256
NCH = 16
NS_ITERS = 5
N_MEM = 8
N_TILE = 4


def obs_places(key):
    return jax.random.randint(key, (N_MEM, N_TILE, OBS_DEV), 0, TOKP * PATCH)


def draw_sensor_gridpoint(key, part):
    places = obs_places(key)
    return places.astype(jnp.int32)


def draw_sensor_domain_index(key, part):
    places = obs_places(key)
    key = jax.random.fold_in(key, 7)
    offset = jax.random.randint(key, places.shape, -1, 2)
    return jnp.clip(places // PATCH + offset, 0, TOKP - 1).astype(jnp.int32)


def place_ends(entries, stream_key, smallest, high):
    place = [jax.random.randint(jax.random.fold_in(stream_key, axis), (), 0, length) for axis, length in enumerate(entries.shape)]
    main_axis = entries.shape.index(max(entries.shape))
    next_to = place[:main_axis] + [(place[main_axis] + 1) % entries.shape[main_axis]] + place[main_axis + 1:]
    return entries.at[tuple(place)].set(smallest).at[tuple(next_to)].set(high)


def levels(key, shape, shards, least, top_value):
    loudness = 1.0
    for dim, parts in shards:
        steps = jax.random.uniform(jax.random.fold_in(jax.random.fold_in(key, 6), dim), (parts,), jnp.float32, least / len(shards), top_value / len(shards))
        loudness = loudness * jnp.repeat(jnp.exp(steps), shape[dim] // parts).reshape((-1,) + (1,) * (len(shape) - 1 - dim))
    return loudness


def centred(rng, extent, scale, most, cuts=(), kind=jnp.bfloat16):
    loudness = levels(rng, extent, cuts, -0.22, 0.18) if cuts else 1.0
    values = jax.random.normal(rng, extent, jnp.float32) * scale * loudness
    return jnp.minimum(jnp.maximum(values, -most), most).astype(kind)


def setup_inputs(seed: int = 0) -> dict:
    streams_of = jax.random.split(jax.random.key(seed), 13)
    starting_ensemble = centred(streams_of[0], (ENS, LAT, LON, FEAT), 1.0, 6.0, ((0, 8), (2, 4)))
    patch_lifting = centred(streams_of[1], (FEAT, D), FEAT ** -0.5, 0.1875, ((0, 8),))
    query_keyvalue_lift = centred(streams_of[2], (D, 3 * D), D ** -0.5, 0.21875, ((1, 8),))
    output_combiner = centred(streams_of[3], (D, D), D ** -0.5, 0.21875, ((1, 8),))
    decoder_linear_map = centred(streams_of[4], (D, FEAT), D ** -0.5, 0.21875, ((1, 8),))
    cosine_logit_scale = jnp.clip(jnp.exp(jax.random.uniform(streams_of[5], (FOCUS_COUNT,), jnp.float32, math.log(2.0), math.log(30.0))), 2.0, 30.0)
    sensor_variable_loadings = centred(streams_of[6], (NCH, VARS), VARS ** -0.5, 0.75)
    sensor_gridpoint = draw_sensor_gridpoint(jax.random.fold_in(streams_of[12], 71), 0)
    sensor_domain_index = draw_sensor_domain_index(jax.random.fold_in(streams_of[12], 71), 0)
    sensor_channel_list = place_ends(jax.random.randint(streams_of[9], (N_MEM, N_TILE, OBS_DEV), 0, NCH), jax.random.fold_in(streams_of[9], 1), 0, NCH - 1).astype(jnp.int32)
    sensor_reading = centred(streams_of[10], (N_MEM, N_TILE, OBS_DEV), 1.0, 6.0, ((0, 8), (1, 4)), jnp.float32)
    sensor_noise_deviation = jnp.clip(jnp.exp(math.log(2.0) - 1.3862944 * jax.random.uniform(streams_of[11], (N_MEM, N_TILE, OBS_DEV), jnp.float32) ** levels(streams_of[11], (N_MEM, N_TILE, OBS_DEV), ((0, 8), (1, 4)), -0.2, 0.2)), 0.5, 2.0)
    return {"starting_ensemble": starting_ensemble, "patch_lifting": patch_lifting, "query_keyvalue_lift": query_keyvalue_lift, "output_combiner": output_combiner, "decoder_linear_map": decoder_linear_map, "cosine_logit_scale": cosine_logit_scale, "sensor_variable_loadings": sensor_variable_loadings, "sensor_gridpoint": sensor_gridpoint, "sensor_domain_index": sensor_domain_index, "sensor_channel_list": sensor_channel_list, "sensor_reading": sensor_reading, "sensor_noise_deviation": sensor_noise_deviation}


eps_norm = 1e-05
normalizing_guard = 1e-06

def layer_norm(values):
    values = values.astype(jnp.float32)
    center = values - lax.optimization_barrier(jnp.mean(values, axis=-1, keepdims=True))
    spread = lax.optimization_barrier(jnp.mean(center * center, axis=-1, keepdims=True))
    return center * lax.rsqrt(spread + eps_norm)

def unit_rows(values):
    values = values.astype(jnp.float32)
    return (values * lax.rsqrt(lax.optimization_barrier(jnp.sum(values * values, axis=-1, keepdims=True)) + normalizing_guard)).astype(jnp.bfloat16)

def pane_cosine_mixer(padded_part, query_keyvalue_lift, cosine_logit_scale):
    rows, cols, attention_span = padded_part.shape
    focus_groups = cosine_logit_scale.shape[0]
    head_dim = attention_span // focus_groups
    qkv = jnp.dot(padded_part.reshape(-1, attention_span), query_keyvalue_lift, preferred_element_type=jnp.float32).astype(jnp.bfloat16)
    qkv = qkv.reshape(rows // PANE_SIDE, PANE_SIDE, cols // PANE_SIDE, PANE_SIDE, 3 * attention_span)
    qkv = qkv.transpose(0, 2, 1, 3, 4).reshape(-1, PANE_SIDE * PANE_SIDE, 3, focus_groups, head_dim)
    query = unit_rows(qkv[:, :, 0])
    key_rows = unit_rows(qkv[:, :, 1])
    value_rows = qkv[:, :, 2]
    affinity_logits = jnp.einsum('bihd,bjhd->bhij', query.astype(jnp.float32), key_rows.astype(jnp.float32))
    affinity_logits = affinity_logits * cosine_logit_scale[None, :, None, None]
    weights = jnp.exp(affinity_logits)
    probs = (weights / lax.optimization_barrier(jnp.sum(weights, axis=-1, keepdims=True))).astype(jnp.bfloat16)
    mixed_outcome = jnp.einsum('bhij,bjhd->bihd', probs.astype(jnp.float32), value_rows.astype(jnp.float32))
    mixed_outcome = mixed_outcome.astype(jnp.bfloat16).reshape(rows // PANE_SIDE, cols // PANE_SIDE, PANE_SIDE, PANE_SIDE, attention_span)
    return mixed_outcome.transpose(0, 2, 1, 3, 4).reshape(rows, cols, attention_span)

def hidden_ensemble_draw(ensemble_draw_vector_state, patch_lifting, query_keyvalue_lift, output_combiner, cosine_logit_scale):
    rows, cols, feats = ensemble_draw_vector_state.shape
    attention_span = patch_lifting.shape[1]
    hidden = jnp.dot(ensemble_draw_vector_state.reshape(-1, feats), patch_lifting, preferred_element_type=jnp.float32)
    hidden = hidden.astype(jnp.bfloat16).reshape(rows, cols, attention_span)
    normed = layer_norm(hidden).astype(jnp.bfloat16)
    rolled_sequence = jnp.roll(normed, -(PANE_SIDE // 2), axis=1)
    mixed_outcome = jnp.roll(pane_cosine_mixer(rolled_sequence, query_keyvalue_lift, cosine_logit_scale), PANE_SIDE // 2, axis=1)
    mixed = hidden.astype(jnp.float32) + jnp.dot(mixed_outcome.reshape(-1, attention_span), output_combiner, preferred_element_type=jnp.float32).reshape(rows, cols, attention_span)
    return layer_norm(mixed).astype(jnp.bfloat16)

def batched(left, right):
    return jnp.einsum('rij,rjk->rik', left, right, precision=lax.Precision.HIGHEST)

def local_analysis(embedded_patches, decoder_linear_map, sensor_gridpoint, sensor_domain_index, sensor_channel_list, sensor_reading, sensor_noise_deviation, sensor_variable_loadings):
    members, regions, attention_span = embedded_patches.shape
    feats = decoder_linear_map.shape[1]
    channels, variables = sensor_variable_loadings.shape
    points = feats // variables
    count = sensor_gridpoint.shape[0]
    prior_member_grids = jnp.dot(embedded_patches.reshape(-1, attention_span), decoder_linear_map, preferred_element_type=jnp.float32).astype(jnp.bfloat16)
    token = sensor_gridpoint // points
    point = sensor_gridpoint - token * points
    pick_point = (point[:, None] == jnp.arange(points, dtype=jnp.int32)[None, :]).astype(jnp.float32)
    pick_chan = (sensor_channel_list[:, None] == jnp.arange(channels, dtype=jnp.int32)[None, :]).astype(jnp.float32)
    rows_h = jnp.dot(pick_chan, sensor_variable_loadings.astype(jnp.float32), precision=lax.Precision.HIGHEST)
    measurement_mapping = (pick_point[:, :, None] * rows_h[:, None, :]).reshape(count, feats).astype(jnp.bfloat16)
    mapped_samples = jnp.einsum('df,lf->dl', prior_member_grids.astype(jnp.float32), measurement_mapping.astype(jnp.float32))
    mapped_samples = mapped_samples.reshape(members, regions, count)
    pick_token = (token[None, :] == jnp.arange(regions, dtype=jnp.int32)[:, None]).astype(jnp.float32)
    ens_obs = lax.optimization_barrier(jnp.sum(mapped_samples * pick_token[None], axis=1))
    mean_obs = lax.optimization_barrier(jnp.mean(ens_obs, axis=0))
    pert_obs = ens_obs - mean_obs[None, :]
    innovation = sensor_reading - mean_obs
    distance = (token - sensor_domain_index).astype(jnp.float32)
    obs_weight = jnp.exp(-0.5 * distance * distance) / (sensor_noise_deviation * sensor_noise_deviation)
    pick_region = (sensor_domain_index[:, None] == jnp.arange(regions, dtype=jnp.int32)[None, :]).astype(jnp.float32)
    weighted = pert_obs * obs_weight[None, :]
    gram = jnp.einsum('kj,jr,lj->rkl', weighted, pick_region, pert_obs, precision=lax.Precision.HIGHEST)
    drive = jnp.einsum('kj,jr,j->rk', weighted, pick_region, innovation, precision=lax.Precision.HIGHEST)
    eye = jnp.eye(members, dtype=jnp.float32)
    system = eye[None] + gram / (members - 1.0)
    bound = lax.optimization_barrier(jnp.max(lax.optimization_barrier(jnp.sum(jnp.abs(system), axis=2)), axis=1))
    iterate = system / bound[:, None, None]
    inverse_root = jnp.broadcast_to(eye, system.shape)
    for step in range(NS_ITERS):
        factor = 1.5 * eye[None] - 0.5 * batched(inverse_root, iterate)
        iterate = batched(iterate, factor)
        inverse_root = batched(factor, inverse_root)
    root = inverse_root * lax.rsqrt(bound)[:, None, None]
    inner = jnp.einsum('rkl,rl->rk', root, drive, precision=lax.Precision.HIGHEST)
    mean_weight = jnp.einsum('rkl,rl->rk', root, inner, precision=lax.Precision.HIGHEST) / (members - 1.0)
    transform_matrix = root + mean_weight[:, :, None]
    values = embedded_patches.astype(jnp.float32)
    center = lax.optimization_barrier(jnp.mean(values, axis=0))
    spread = values - center[None]
    posterior = center[None] + jnp.einsum('ktf,tkm->mtf', spread, transform_matrix, precision=lax.Precision.HIGHEST)
    posterior = posterior.astype(jnp.bfloat16)
    analysed = jnp.dot(posterior.reshape(-1, attention_span), decoder_linear_map, preferred_element_type=jnp.float32)
    return analysed.astype(jnp.bfloat16).reshape(members, regions, feats)

def reference(starting_ensemble, patch_lifting, query_keyvalue_lift, output_combiner, decoder_linear_map, cosine_logit_scale, sensor_variable_loadings, sensor_gridpoint, sensor_domain_index, sensor_channel_list, sensor_reading, sensor_noise_deviation):
    embedded_patches = lax.map(lambda single_pane: hidden_ensemble_draw(single_pane, patch_lifting, query_keyvalue_lift, output_combiner, cosine_logit_scale), starting_ensemble)
    pieces = embedded_patches.reshape(ENS, LAT, N_TILE, LON_DEV, D).transpose(2, 0, 1, 3, 4)
    pieces = pieces.reshape(N_TILE, ENS, N_MEM, TOKP, D).transpose(2, 0, 1, 3, 4)
    pieces = pieces.reshape(N_MEM * N_TILE, ENS, TOKP, D)
    flat = N_MEM * N_TILE

    def one_piece(items):
        return local_analysis(items[0], decoder_linear_map, items[1], items[2], items[3], items[4], items[5], sensor_variable_loadings)
    analysed = lax.map(one_piece, (pieces, sensor_gridpoint.reshape(flat, OBS_DEV), sensor_domain_index.reshape(flat, OBS_DEV), sensor_channel_list.reshape(flat, OBS_DEV), sensor_reading.reshape(flat, OBS_DEV), sensor_noise_deviation.reshape(flat, OBS_DEV)))
    analysed = analysed.reshape(N_MEM, N_TILE, ENS, TOKP, FEAT).transpose(2, 1, 0, 3, 4)
    analysed = analysed.reshape(ENS, N_TILE, LAT, LON_DEV, FEAT).transpose(0, 2, 1, 3, 4)
    return analysed.reshape(ENS, LAT, LON, FEAT)
```

```python
import functools

import jax
import jax.numpy as jnp
from jax import lax
from jax.experimental import pallas as pl
from jax.experimental.pallas import tpu as pltpu
from jax.sharding import PartitionSpec as P

PANE_SIDE = 8
NS_ITERS = 5
KINDS = 15
MESH = pl.DeviceIdType.MESH
HIGHEST = lax.Precision.HIGHEST


eps_norm = 1e-05
normalizing_guard = 1e-06


def passed_along(value, axis, by):
    devices = lax.axis_size(axis)
    return lax.ppermute(value, axis, [(i, (i + by) % devices) for i in range(devices)])


def layer_norm(values):
    values = values.astype(jnp.float32)
    center = values - jnp.mean(values, axis=-1, keepdims=True)
    spread = jnp.mean(center * center, axis=-1, keepdims=True)
    return center * lax.rsqrt(spread + eps_norm)


def unit_rows(values):
    values = values.astype(jnp.float32)
    return (
        values * lax.rsqrt(jnp.sum(values * values, axis=-1, keepdims=True) + normalizing_guard)
    ).astype(jnp.bfloat16)


def pane_cosine_mixer(padded_part, query_keyvalue_lift, cosine_logit_scale):
    members, rows, cols, attention_span = padded_part.shape
    focus_groups = cosine_logit_scale.shape[0]
    head_dim = attention_span // focus_groups
    qkv = jnp.dot(
        padded_part.reshape(-1, attention_span),
        query_keyvalue_lift,
        preferred_element_type=jnp.float32,
    ).astype(jnp.bfloat16)
    qkv = qkv.reshape(
        members, rows // PANE_SIDE, PANE_SIDE, cols // PANE_SIDE, PANE_SIDE, 3 * attention_span
    )
    qkv = qkv.transpose(0, 1, 3, 2, 4, 5).reshape(
        -1, PANE_SIDE * PANE_SIDE, 3, focus_groups, head_dim
    )
    query = unit_rows(qkv[:, :, 0])
    key_rows = unit_rows(qkv[:, :, 1])
    value_rows = qkv[:, :, 2]
    affinity_logits = jnp.einsum(
        "bihd,bjhd->bhij", query, key_rows, preferred_element_type=jnp.float32
    )
    affinity_logits = affinity_logits * cosine_logit_scale[None, :, None, None]
    weights = jnp.exp(affinity_logits)
    probs = (weights / jnp.sum(weights, axis=-1, keepdims=True)).astype(jnp.bfloat16)
    mixed_outcome = jnp.einsum(
        "bhij,bjhd->bihd", probs, value_rows, preferred_element_type=jnp.float32
    )
    mixed_outcome = mixed_outcome.astype(jnp.bfloat16).reshape(
        members, rows // PANE_SIDE, cols // PANE_SIDE, PANE_SIDE, PANE_SIDE, attention_span
    )
    return mixed_outcome.transpose(0, 1, 3, 2, 4, 5).reshape(members, rows, cols, attention_span)


def batched(left, right):
    return jnp.einsum("rij,rjk->rik", left, right, precision=lax.Precision.HIGHEST)


def local_analysis(
    embedded_patches,
    decoder_linear_map,
    sensor_gridpoint,
    sensor_domain_index,
    sensor_channel_list,
    sensor_reading,
    sensor_noise_deviation,
    sensor_variable_loadings,
):
    members, regions, attention_span = embedded_patches.shape
    feats = decoder_linear_map.shape[1]
    channels, variables = sensor_variable_loadings.shape
    points = feats // variables
    count = sensor_gridpoint.shape[0]
    prior_member_grids = jnp.dot(
        embedded_patches.reshape(-1, attention_span),
        decoder_linear_map,
        preferred_element_type=jnp.float32,
    ).astype(jnp.bfloat16)
    token = sensor_gridpoint // points
    point = sensor_gridpoint - token * points
    pick_point = (point[:, None] == jnp.arange(points, dtype=jnp.int32)[None, :]).astype(
        jnp.float32
    )
    pick_chan = (
        sensor_channel_list[:, None] == jnp.arange(channels, dtype=jnp.int32)[None, :]
    ).astype(jnp.float32)
    rows_h = jnp.dot(
        pick_chan, sensor_variable_loadings.astype(jnp.float32), precision=lax.Precision.HIGHEST
    )
    measurement_mapping = (
        (pick_point[:, :, None] * rows_h[:, None, :]).reshape(count, feats).astype(jnp.bfloat16)
    )
    mapped_samples = lax.dot_general(
        prior_member_grids,
        measurement_mapping,
        (((1,), (1,)), ((), ())),
        preferred_element_type=jnp.float32,
    )
    mapped_samples = mapped_samples.reshape(members, regions, count)
    pick_token = (token[None, :] == jnp.arange(regions, dtype=jnp.int32)[:, None]).astype(
        jnp.float32
    )
    ens_obs = jnp.sum(mapped_samples * pick_token[None], axis=1)
    mean_obs = jnp.mean(ens_obs, axis=0)
    pert_obs = ens_obs - mean_obs[None, :]
    innovation = sensor_reading - mean_obs
    distance = (token - sensor_domain_index).astype(jnp.float32)
    obs_weight = jnp.exp(-0.5 * distance * distance) / (
        sensor_noise_deviation * sensor_noise_deviation
    )
    pick_region = (
        sensor_domain_index[:, None] == jnp.arange(regions, dtype=jnp.int32)[None, :]
    ).astype(jnp.float32)
    weighted = pert_obs * obs_weight[None, :]
    gram = jnp.einsum(
        "kj,jr,lj->rkl", weighted, pick_region, pert_obs, precision=lax.Precision.HIGHEST
    )
    drive = jnp.einsum(
        "kj,jr,j->rk", weighted, pick_region, innovation, precision=lax.Precision.HIGHEST
    )
    eye = jnp.eye(members, dtype=jnp.float32)
    system = eye[None] + gram / (members - 1.0)
    bound = jnp.max(jnp.sum(jnp.abs(system), axis=2), axis=1)
    iterate = system / bound[:, None, None]
    inverse_root = jnp.broadcast_to(eye, system.shape)
    for step in range(NS_ITERS):
        factor = 1.5 * eye[None] - 0.5 * batched(inverse_root, iterate)
        iterate = batched(iterate, factor)
        inverse_root = batched(factor, inverse_root)
    root = inverse_root * lax.rsqrt(bound)[:, None, None]
    inner = jnp.einsum("rkl,rl->rk", root, drive, precision=lax.Precision.HIGHEST)
    mean_weight = jnp.einsum("rkl,rl->rk", root, inner, precision=lax.Precision.HIGHEST) / (
        members - 1.0
    )
    transform_matrix = root + mean_weight[:, :, None]
    values = embedded_patches.astype(jnp.float32)
    center = jnp.mean(values, axis=0)
    spread = values - center[None]
    posterior = center[None] + jnp.einsum(
        "ktf,tkm->mtf", spread, transform_matrix, precision=lax.Precision.HIGHEST
    )
    return posterior.astype(jnp.bfloat16)


def per_device(
    starting_ensemble,
    patch_lifting,
    query_keyvalue_lift,
    output_combiner,
    decoder_linear_map,
    cosine_logit_scale,
    sensor_variable_loadings,
    sensor_gridpoint,
    sensor_domain_index,
    sensor_channel_list,
    sensor_reading,
    sensor_noise_deviation,
):
    members, rows, cols, feats = starting_ensemble.shape
    full_embed, entire_triplet_product, full_out, full_head = (
        lax.all_gather(patch_lifting, "mem", axis=0, tiled=True),
        lax.all_gather(query_keyvalue_lift, "mem", axis=1, tiled=True),
        lax.all_gather(output_combiner, "mem", axis=1, tiled=True),
        lax.all_gather(decoder_linear_map, "mem", axis=1, tiled=True),
    )
    attention_span = full_embed.shape[1]
    hidden = jnp.dot(
        starting_ensemble.reshape(-1, feats), full_embed, preferred_element_type=jnp.float32
    )
    hidden = hidden.astype(jnp.bfloat16).reshape(members, rows, cols, attention_span)
    normed = layer_norm(hidden).astype(jnp.bfloat16)
    half = PANE_SIDE // 2
    incoming_rows = passed_along(normed[:, :, :half], "tile", -1)
    padded_sequence = jnp.concatenate([normed[:, :, half:], incoming_rows], axis=2)
    mixed_outcome_padded = pane_cosine_mixer(
        padded_sequence, entire_triplet_product, cosine_logit_scale
    )
    returned = passed_along(mixed_outcome_padded[:, :, cols - half :], "tile", 1)
    mixed_outcome = jnp.concatenate([returned, mixed_outcome_padded[:, :, : cols - half]], axis=2)
    mixed = hidden.astype(jnp.float32) + jnp.dot(
        mixed_outcome.reshape(-1, attention_span), full_out, preferred_element_type=jnp.float32
    ).reshape(members, rows, cols, attention_span)
    embedded_patches = layer_norm(mixed).astype(jnp.bfloat16)
    tile_tokens = rows * cols
    moved = lax.all_to_all(
        embedded_patches.reshape(members, tile_tokens, attention_span),
        "mem",
        split_axis=1,
        concat_axis=0,
        tiled=True,
    )
    ensemble, regions = (moved.shape[0], moved.shape[1])
    posterior = local_analysis(
        moved,
        full_head,
        sensor_gridpoint.reshape(-1),
        sensor_domain_index.reshape(-1),
        sensor_channel_list.reshape(-1),
        sensor_reading.reshape(-1),
        sensor_noise_deviation.reshape(-1),
        sensor_variable_loadings,
    )
    produced = jnp.dot(
        posterior.reshape(-1, attention_span), full_head, preferred_element_type=jnp.float32
    )
    produced = produced.astype(jnp.bfloat16).reshape(ensemble, regions, feats)
    analysed = lax.all_to_all(produced, "mem", split_axis=0, concat_axis=1, tiled=True)
    return analysed.reshape(members, rows, cols, feats)


def iota(shape, dim):
    return lax.broadcasted_iota(jnp.int32, shape, dim)


def dot(left, right):
    return jnp.dot(left, right, preferred_element_type=jnp.float32)


def dot_nt(left, right):
    return lax.dot_general(
        left, right, (((1,), (1,)), ((), ())), preferred_element_type=jnp.float32
    )


def exact(left, right):
    return jnp.dot(left, right, precision=HIGHEST, preferred_element_type=jnp.float32)


def one_hot(mask):
    return jnp.where(mask, 1.0, 0.0).astype(jnp.bfloat16)


def picked(rows, source):
    return one_hot(source == iota((rows, rows), 1))


def forecast_and_analyse(
    heads,
    x_ref,
    embed_ref,
    qkv_ref,
    comb_ref,
    dec_ref,
    scale_ref,
    load_ref,
    grid_ref,
    dom_ref,
    chan_ref,
    read_ref,
    noise_ref,
    out_ref,
    g_embed,
    g_qkv,
    g_comb,
    g_dec,
    x_pad,
    to_west,
    window,
    qkv_buf,
    ctx,
    from_west,
    lat_send,
    lat_recv,
    pos_send,
    pos_recv,
    w_send,
    w_recv,
    t_send,
    t_recv,
    a_send,
    a_recv,
):
    bf16, f32 = jnp.bfloat16, jnp.float32
    me = lax.axis_index("mem")
    tile = lax.axis_index("tile")
    tiles = lax.axis_size("tile")
    n = lax.axis_size("mem")
    core = me % 2
    along_x = (me // 2) % 2
    along_y = me // 4
    to_sib = 1 - 2 * core
    sib = me + to_sib
    x_nb = me + 2 - 4 * along_x
    y_nb = me + 4 - 8 * along_y
    diag = x_nb + 4 - 8 * along_y
    odd = tile % 2
    partner = tile + 1 - 2 * odd
    west = (tile + tiles - 1) % tiles
    east = (tile + 1) % tiles

    tokens, span = window.shape
    half = tokens // 2
    feats = x_ref.shape[1]
    piece = feats // n
    padded = g_embed.shape[0] // n
    width = padded * n
    count = grid_ref.shape[2]
    variables = load_ref.shape[1]

    barrier = pltpu.get_barrier_semaphore()
    for step in range(1, n):
        pl.semaphore_signal(
            barrier, inc=1, device_id=((me + step) % n, tile), device_id_type=MESH
        )
    for other in (west, east):
        pl.semaphore_signal(barrier, inc=1, device_id=(me, other), device_id_type=MESH)

    gathered = (g_embed, g_qkv, g_comb, g_dec)
    sends = []

    def copy(w, kind, owner, first, rows, target):
        held = gathered[w]
        block = held.shape[0] // n
        part = held.at[pl.ds(pl.multiple_of(owner * block + first, 16), rows)]
        return pltpu.make_async_remote_copy(
            src_ref=part,
            dst_ref=part,
            send_sem=w_send.at[w * KINDS + kind],
            recv_sem=w_recv.at[w * KINDS + kind],
            device_id=target,
            device_id_type=MESH,
        )

    here = {
        "sib": (sib, tile),
        "x": (x_nb, tile),
        "y": (y_nb, tile),
        "z": (me, partner),
    }

    def send(w, kind, owner, first, rows, way):
        sent = copy(w, kind, owner, first, rows, here[way])
        sent.start()
        sends.append(sent)

    def arrived(w, kind, owner, first, rows):
        copy(w, kind, owner, first, rows, here["sib"]).wait_recv()

    def third(w):
        return gathered[w].shape[0] // n // 3

    def own(w):
        t = third(w)
        send(w, 1, me, odd * t, 2 * t, "x")
        send(w, 2, me, odd * t, 2 * t, "y")
        send(w, 0, me, 0, 3 * t, "sib")

    def pass_neighbours(w):
        t = third(w)
        arrived(w, 1, x_nb, odd * t, 2 * t)
        send(w, 5, x_nb, 2 * odd * t, t, "y")
        send(w, 9, x_nb, 2 * odd * t, t, "z")
        send(w, 3, x_nb, odd * t, 2 * t, "sib")
        arrived(w, 2, y_nb, odd * t, 2 * t)
        send(w, 6, y_nb, t, t, "x")
        send(w, 10, y_nb, 2 * odd * t, t, "z")
        send(w, 4, y_nb, odd * t, 2 * t, "sib")

    def pass_diagonal(w):
        t = third(w)
        arrived(w, 5, diag, 2 * odd * t, t)
        send(w, 11, diag, 2 * odd * t, t, "z")
        send(w, 7, diag, 2 * odd * t, t, "sib")
        arrived(w, 6, diag, t, t)
        send(w, 8, diag, t, t, "sib")

    def pass_partner(w):
        t = third(w)
        for kind, owner in ((9, x_nb), (10, y_nb), (11, diag)):
            arrived(w, kind, owner, 2 * (1 - odd) * t, t)
            send(w, kind + 3, owner, 2 * (1 - odd) * t, t, "sib")

    def complete(w):
        t = third(w)
        arrived(w, 0, sib, 0, 3 * t)
        arrived(w, 3, x_nb + to_sib, odd * t, 2 * t)
        arrived(w, 4, y_nb + to_sib, odd * t, 2 * t)
        arrived(w, 7, diag + to_sib, 2 * odd * t, t)
        arrived(w, 8, diag + to_sib, t, t)
        for kind, owner in ((12, x_nb), (13, y_nb), (14, diag)):
            arrived(w, kind, owner + to_sib, 2 * (1 - odd) * t, t)

    def keep_own(w, value):
        block = gathered[w].shape[0] // n
        gathered[w][pl.ds(pl.multiple_of(me * block, 16), block), :] = value.astype(bf16)

    def eye(rows, cols):
        return one_hot(iota((rows, cols), 0) == iota((rows, cols), 1))

    EMBED, QKV, COMB, DEC = 0, 1, 2, 3

    keep_own(EMBED, dot(eye(padded, piece), embed_ref[...]))
    pl.semaphore_wait(barrier, n + 1)
    own(EMBED)
    keep_own(QKV, dot_nt(eye(qkv_ref.shape[1], qkv_ref.shape[1]), qkv_ref[...]))
    own(QKV)
    keep_own(COMB, dot_nt(eye(comb_ref.shape[1], comb_ref.shape[1]), comb_ref[...]))
    keep_own(DEC, dot_nt(eye(padded, piece), dec_ref[...]))

    row = iota((tokens, tokens), 0)
    by_half = picked(
        tokens,
        ((row >> 5) & 1) * 64 + ((row >> 2) & 7) * 8 + (row >> 6) * 4 + (row & 3),
    )
    x_rows = dot(by_half, x_ref[...]).astype(bf16)
    x_pad[...] = jnp.zeros(x_pad.shape, bf16)
    for d in range(n):
        x_pad[:, padded * d : padded * d + piece] = x_rows[:, piece * d : piece * (d + 1)]

    pass_neighbours(EMBED)
    own(COMB)

    within = iota((n, padded, variables), 1)
    within = within - jnp.where(within >= variables, variables, 0)
    pick_variable = one_hot(within == iota((n, padded, variables), 2)).reshape(width, variables)
    channels = load_ref.shape[0]
    loads = dot_nt(pick_variable, load_ref[...]).astype(bf16)
    chan_hot = one_hot(jnp.broadcast_to(chan_ref[0], (channels, count)) == iota((channels, count), 0))
    mapping = dot(loads, chan_hot)
    grid_point = grid_ref[0]
    points = feats // variables
    token_row = grid_point >> 4
    point_row = grid_point & (points - 1)
    dom_row = dom_ref[0]
    slot = iota((n, padded, count), 0) * 2 + jnp.where(
        iota((n, padded, count), 1) >= variables, 1, 0
    )
    mapping = jnp.where(
        slot.reshape(width, count) == jnp.broadcast_to(point_row, (width, count)), mapping, 0.0
    ).astype(bf16)

    pass_diagonal(EMBED)
    pass_partner(EMBED)
    complete(EMBED)

    hidden = dot(x_pad[...], g_embed[...]).astype(bf16)
    normed = layer_norm(hidden).astype(bf16)
    to_west[...] = normed[:half]
    window[half:, :] = normed[half:]

    def along_tile(index, source, target, way):
        return pltpu.make_async_remote_copy(
            src_ref=source,
            dst_ref=target,
            send_sem=t_send.at[index],
            recv_sem=t_recv.at[index],
            device_id=(me, way),
            device_id_type=MESH,
        )

    westward = along_tile(0, to_west, window.at[pl.ds(0, half)], west)
    westward.start()
    sends.append(westward)

    pass_neighbours(QKV)
    own(DEC)
    pass_diagonal(QKV)
    pass_neighbours(COMB)
    pass_partner(QKV)
    westward.wait_recv()
    complete(QKV)

    qkv_buf[...] = dot_nt(window[...], g_qkv[...]).astype(bf16)
    pass_diagonal(COMB)
    pass_neighbours(DEC)

    side = span // heads
    same_member = ((row >> 5) & 1) == ((iota((tokens, tokens), 1) >> 5) & 1)
    for h in range(heads):
        query = unit_rows(qkv_buf[:, side * h : side * (h + 1)])
        key = unit_rows(qkv_buf[:, span + side * h : span + side * (h + 1)])
        value = qkv_buf[:, 2 * span + side * h : 2 * span + side * (h + 1)]
        weights = jnp.where(same_member, jnp.exp(dot_nt(query, key) * scale_ref[h]), 0.0)
        probs = (weights / jnp.sum(weights, axis=-1, keepdims=True)).astype(bf16)
        ctx[:, side * h : side * (h + 1)] = dot(probs, value).astype(bf16)
        if h == heads // 2:
            pass_partner(COMB)
            pass_diagonal(DEC)

    eastward = along_tile(1, ctx.at[pl.ds(0, half)], from_west, east)
    eastward.start()
    sends.append(eastward)
    complete(COMB)
    pass_partner(DEC)
    own_half = dot_nt(ctx[half:, :], g_comb[...])
    eastward.wait_recv()
    mixed = hidden.astype(f32) + jnp.concatenate(
        [dot_nt(from_west[...], g_comb[...]), own_half], axis=0
    )
    latent = layer_norm(mixed).astype(bf16)
    by_region = picked(
        tokens,
        ((row >> 2) & 1) * 64 + ((row >> 3) & 1) * 32 + (row >> 4) * 4 + (row & 3),
    )
    lat_send[...] = dot(by_region, latent).astype(bf16)

    block = tokens // n

    def exchange(index, source, target):
        mine = pl.ds(pl.multiple_of(me * block, 16), block)
        for step in range(1, n):
            to = (me + step) % n
            sent = pltpu.make_async_remote_copy(
                src_ref=source.at[pl.ds(pl.multiple_of(to * block, 16), block)],
                dst_ref=target.at[mine],
                send_sem=a_send.at[index * n + step],
                recv_sem=a_recv.at[index * n + step],
                device_id=(to, tile),
                device_id_type=MESH,
            )
            sent.start()
            sends.append(sent)
        target[mine, :] = source[mine, :]

    def exchanged(index, source, target):
        for step in range(1, n):
            origin = (me + n - step) % n
            part = pl.ds(pl.multiple_of(origin * block, 16), block)
            pltpu.make_async_remote_copy(
                src_ref=source.at[part],
                dst_ref=target.at[part],
                send_sem=a_send.at[index * n + step],
                recv_sem=a_recv.at[index * n + step],
                device_id=(origin, tile),
                device_id_type=MESH,
            ).wait_recv()

    exchange(0, lat_send, lat_recv)
    complete(DEC)
    exchanged(0, lat_send, lat_recv)

    members, regions = tokens // n, n
    members = tokens // regions
    values = lat_recv[...]
    prior = dot_nt(values, g_dec[...]).astype(bf16)
    samples = dot(prior, mapping).reshape(members, regions, count)
    region3 = iota((members, regions, count), 1)
    samples = jnp.where(region3 == token_row[None], samples, 0.0)
    ens_obs = jnp.sum(samples, axis=1, keepdims=True)
    mean_obs = jnp.mean(ens_obs, axis=0, keepdims=True)
    in_region = region3 == dom_row[None]
    pert = jnp.where(in_region, ens_obs - mean_obs, 0.0).reshape(tokens, count)
    innovation = read_ref[0] - mean_obs[0]
    distance = (token_row - dom_row).astype(f32)
    noise = noise_ref[0]
    obs_weight = jnp.exp(-0.5 * distance * distance) / (noise * noise)
    weighted = pert * obs_weight
    gram = lax.dot_general(
        weighted, pert, (((1,), (1,)), ((), ())), precision=HIGHEST, preferred_element_type=f32
    )
    drive = jnp.sum(weighted * innovation, axis=1, keepdims=True)
    unit = jnp.where(row == iota((tokens, tokens), 1), 1.0, 0.0)
    system = unit + gram * (1.0 / (members - 1.0))
    sums = jnp.sum(jnp.abs(system), axis=1, keepdims=True).reshape(members, regions, 1)
    bound = jnp.broadcast_to(
        jnp.max(sums, axis=0, keepdims=True), (members, regions, 1)
    ).reshape(tokens, 1)
    iterate = system / bound
    inverse_root = None
    for step in range(NS_ITERS):
        if step == 0:
            factor = 1.5 * unit - 0.5 * iterate
            inverse_root = factor
        else:
            factor = 1.5 * unit - 0.5 * exact(inverse_root, iterate)
            inverse_root = exact(factor, inverse_root)
        if step < NS_ITERS - 1:
            iterate = exact(iterate, factor)
    root = inverse_root * lax.rsqrt(bound)
    inner = exact(root, jnp.broadcast_to(drive, (tokens, tokens)))
    mean_weight = exact(root, inner) * (1.0 / (members - 1.0))
    same_region = (row & (regions - 1)) == (iota((tokens, tokens), 1) & (regions - 1))
    transform = jnp.where(same_region, root + mean_weight, 0.0)
    latents = values.astype(f32).reshape(members, regions, span)
    center = jnp.mean(latents, axis=0, keepdims=True)
    spread = (latents - center).reshape(tokens, span)
    posterior = jnp.broadcast_to(center, latents.shape).reshape(tokens, span) + exact(
        transform.T, spread
    )
    pos_send[...] = posterior.astype(bf16)
    exchange(1, pos_send, pos_recv)
    exchanged(1, pos_send, pos_recv)
    by_member = picked(tokens, ((row >> 3) & 7) * 16 + (row >> 6) * 8 + (row & 7))
    analysed = dot_nt(dot(by_member, pos_recv[...]).astype(bf16), g_dec[...])
    for d in range(n):
        out_ref[:, piece * d : piece * (d + 1)] = analysed[
            :, padded * d : padded * d + piece
        ].astype(bf16)
    for sent in sends:
        sent.wait_send()


def per_device_fused(
    starting_ensemble,
    patch_lifting,
    query_keyvalue_lift,
    output_combiner,
    decoder_linear_map,
    cosine_logit_scale,
    sensor_variable_loadings,
    *sensors,
):
    n = lax.axis_size("mem")
    members, rows, cols, feats = starting_ensemble.shape
    tokens = members * rows * cols
    span = patch_lifting.shape[1]
    padded = -(-patch_lifting.shape[0] // 48) * 48
    vmem = pl.BlockSpec(memory_space=pltpu.VMEM)
    smem = pl.BlockSpec(memory_space=pltpu.SMEM)

    def held(*shape):
        return pltpu.VMEM(shape, jnp.bfloat16)

    out = pl.pallas_call(
        functools.partial(forecast_and_analyse, cosine_logit_scale.shape[0]),
        out_shape=jax.ShapeDtypeStruct((tokens, feats), jnp.bfloat16),
        in_specs=[vmem] * 5 + [smem] + [vmem] * 6,
        out_specs=vmem,
        scratch_shapes=[
            held(padded * n, span),
            held(query_keyvalue_lift.shape[1] * n, span),
            held(output_combiner.shape[1] * n, span),
            held(padded * n, span),
            held(tokens, padded * n),
            held(tokens // 2, span),
            held(tokens, span),
            held(tokens, 3 * span),
            held(tokens, span),
            held(tokens // 2, span),
            held(tokens, span),
            held(tokens, span),
            held(tokens, span),
            held(tokens, span),
            pltpu.SemaphoreType.DMA((4 * KINDS,)),
            pltpu.SemaphoreType.DMA((4 * KINDS,)),
            pltpu.SemaphoreType.DMA((2,)),
            pltpu.SemaphoreType.DMA((2,)),
            pltpu.SemaphoreType.DMA((2 * n,)),
            pltpu.SemaphoreType.DMA((2 * n,)),
        ],
        compiler_params=pltpu.CompilerParams(
            collective_id=0, has_side_effects=True, vmem_limit_bytes=48 * 1024 * 1024
        ),
        cost_estimate=pl.CostEstimate(
            flops=2 * tokens * span * (3 * feats + 4 * span),
            bytes_accessed=16 * 1024 * 1024,
            transcendentals=0,
        ),
    )(
        starting_ensemble.reshape(tokens, feats),
        patch_lifting,
        query_keyvalue_lift,
        output_combiner,
        decoder_linear_map,
        cosine_logit_scale,
        sensor_variable_loadings,
        *sensors,
    )
    return out.reshape(members, rows, cols, feats)


def fits_fused(mesh, starting_ensemble, patch_lifting, query_keyvalue_lift, output_combiner, loads):
    n, tiles = mesh.shape["mem"], mesh.shape["tile"]
    members, rows, cols, feats = starting_ensemble.shape
    return (
        n == 8
        and tiles % 2 == 0
        and tiles > 2
        and (members // n, rows, cols // tiles) == (2, 8, 8)
        and feats == 16 * loads.shape[1]
        and query_keyvalue_lift.shape[1] % (48 * n) == 0
        and output_combiner.shape[1] % (48 * n) == 0
    )


def solution(mesh):
    def whole(*args):
        fused = fits_fused(mesh, args[0], args[1], args[2], args[3], args[6])
        return jax.shard_map(
            per_device_fused if fused else per_device,
            mesh=mesh,
            in_specs=(
                P("mem", None, "tile", None),
                P("mem", None),
                P(None, "mem"),
                P(None, "mem"),
                P(None, "mem"),
                P(),
                P(),
                P("mem", "tile", None),
                P("mem", "tile", None),
                P("mem", "tile", None),
                P("mem", "tile", None),
                P("mem", "tile", None),
            ),
            out_specs=P("mem", None, "tile", None),
            check_vma=False,
        )(*args)

    return whole
```

```python
import functools

import jax
import jax.numpy as jnp
from jax import lax
from jax.experimental import pallas as pl
from jax.experimental.pallas import tpu as pltpu
from jax.sharding import PartitionSpec as P

PANE_SIDE = 8
NS_ITERS = 5
KINDS = 17
MESH = pl.DeviceIdType.MESH


eps_norm = 1e-05
normalizing_guard = 1e-06


def passed_along(value, axis, by):
    devices = lax.axis_size(axis)
    return lax.ppermute(value, axis, [(i, (i + by) % devices) for i in range(devices)])


def layer_norm(values):
    values = values.astype(jnp.float32)
    center = values - jnp.mean(values, axis=-1, keepdims=True)
    spread = jnp.mean(center * center, axis=-1, keepdims=True)
    return center * lax.rsqrt(spread + eps_norm)


def unit_rows(values):
    values = values.astype(jnp.float32)
    return (
        values * lax.rsqrt(jnp.sum(values * values, axis=-1, keepdims=True) + normalizing_guard)
    ).astype(jnp.bfloat16)


def pane_cosine_mixer(padded_part, query_keyvalue_lift, cosine_logit_scale):
    members, rows, cols, attention_span = padded_part.shape
    focus_groups = cosine_logit_scale.shape[0]
    head_dim = attention_span // focus_groups
    qkv = jnp.dot(
        padded_part.reshape(-1, attention_span),
        query_keyvalue_lift,
        preferred_element_type=jnp.float32,
    ).astype(jnp.bfloat16)
    qkv = qkv.reshape(
        members, rows // PANE_SIDE, PANE_SIDE, cols // PANE_SIDE, PANE_SIDE, 3 * attention_span
    )
    qkv = qkv.transpose(0, 1, 3, 2, 4, 5).reshape(
        -1, PANE_SIDE * PANE_SIDE, 3, focus_groups, head_dim
    )
    query = unit_rows(qkv[:, :, 0])
    key_rows = unit_rows(qkv[:, :, 1])
    value_rows = qkv[:, :, 2]
    affinity_logits = jnp.einsum(
        "bihd,bjhd->bhij", query, key_rows, preferred_element_type=jnp.float32
    )
    affinity_logits = affinity_logits * cosine_logit_scale[None, :, None, None]
    weights = jnp.exp(affinity_logits)
    probs = (weights / jnp.sum(weights, axis=-1, keepdims=True)).astype(jnp.bfloat16)
    mixed_outcome = jnp.einsum(
        "bhij,bjhd->bihd", probs, value_rows, preferred_element_type=jnp.float32
    )
    mixed_outcome = mixed_outcome.astype(jnp.bfloat16).reshape(
        members, rows // PANE_SIDE, cols // PANE_SIDE, PANE_SIDE, PANE_SIDE, attention_span
    )
    return mixed_outcome.transpose(0, 1, 3, 2, 4, 5).reshape(members, rows, cols, attention_span)


def batched(left, right):
    return jnp.einsum("rij,rjk->rik", left, right, precision=lax.Precision.HIGHEST)


def local_analysis(
    embedded_patches,
    decoder_linear_map,
    sensor_gridpoint,
    sensor_domain_index,
    sensor_channel_list,
    sensor_reading,
    sensor_noise_deviation,
    sensor_variable_loadings,
):
    members, regions, attention_span = embedded_patches.shape
    feats = decoder_linear_map.shape[1]
    channels, variables = sensor_variable_loadings.shape
    points = feats // variables
    count = sensor_gridpoint.shape[0]
    prior_member_grids = jnp.dot(
        embedded_patches.reshape(-1, attention_span),
        decoder_linear_map,
        preferred_element_type=jnp.float32,
    ).astype(jnp.bfloat16)
    token = sensor_gridpoint // points
    point = sensor_gridpoint - token * points
    pick_point = (point[:, None] == jnp.arange(points, dtype=jnp.int32)[None, :]).astype(
        jnp.float32
    )
    pick_chan = (
        sensor_channel_list[:, None] == jnp.arange(channels, dtype=jnp.int32)[None, :]
    ).astype(jnp.float32)
    rows_h = jnp.dot(
        pick_chan, sensor_variable_loadings.astype(jnp.float32), precision=lax.Precision.HIGHEST
    )
    measurement_mapping = (
        (pick_point[:, :, None] * rows_h[:, None, :]).reshape(count, feats).astype(jnp.bfloat16)
    )
    mapped_samples = lax.dot_general(
        prior_member_grids,
        measurement_mapping,
        (((1,), (1,)), ((), ())),
        preferred_element_type=jnp.float32,
    )
    mapped_samples = mapped_samples.reshape(members, regions, count)
    pick_token = (token[None, :] == jnp.arange(regions, dtype=jnp.int32)[:, None]).astype(
        jnp.float32
    )
    ens_obs = jnp.sum(mapped_samples * pick_token[None], axis=1)
    mean_obs = jnp.mean(ens_obs, axis=0)
    pert_obs = ens_obs - mean_obs[None, :]
    innovation = sensor_reading - mean_obs
    distance = (token - sensor_domain_index).astype(jnp.float32)
    obs_weight = jnp.exp(-0.5 * distance * distance) / (
        sensor_noise_deviation * sensor_noise_deviation
    )
    pick_region = (
        sensor_domain_index[:, None] == jnp.arange(regions, dtype=jnp.int32)[None, :]
    ).astype(jnp.float32)
    weighted = pert_obs * obs_weight[None, :]
    gram = jnp.einsum(
        "kj,jr,lj->rkl", weighted, pick_region, pert_obs, precision=lax.Precision.HIGHEST
    )
    drive = jnp.einsum(
        "kj,jr,j->rk", weighted, pick_region, innovation, precision=lax.Precision.HIGHEST
    )
    eye = jnp.eye(members, dtype=jnp.float32)
    system = eye[None] + gram / (members - 1.0)
    bound = jnp.max(jnp.sum(jnp.abs(system), axis=2), axis=1)
    iterate = system / bound[:, None, None]
    inverse_root = jnp.broadcast_to(eye, system.shape)
    for step in range(NS_ITERS):
        factor = 1.5 * eye[None] - 0.5 * batched(inverse_root, iterate)
        iterate = batched(iterate, factor)
        inverse_root = batched(factor, inverse_root)
    root = inverse_root * lax.rsqrt(bound)[:, None, None]
    inner = jnp.einsum("rkl,rl->rk", root, drive, precision=lax.Precision.HIGHEST)
    mean_weight = jnp.einsum("rkl,rl->rk", root, inner, precision=lax.Precision.HIGHEST) / (
        members - 1.0
    )
    transform_matrix = root + mean_weight[:, :, None]
    values = embedded_patches.astype(jnp.float32)
    center = jnp.mean(values, axis=0)
    spread = values - center[None]
    posterior = center[None] + jnp.einsum(
        "ktf,tkm->mtf", spread, transform_matrix, precision=lax.Precision.HIGHEST
    )
    return posterior.astype(jnp.bfloat16)


def per_device(
    starting_ensemble,
    patch_lifting,
    query_keyvalue_lift,
    output_combiner,
    decoder_linear_map,
    cosine_logit_scale,
    sensor_variable_loadings,
    sensor_gridpoint,
    sensor_domain_index,
    sensor_channel_list,
    sensor_reading,
    sensor_noise_deviation,
):
    members, rows, cols, feats = starting_ensemble.shape
    full_embed, entire_triplet_product, full_out, full_head = (
        lax.all_gather(patch_lifting, "mem", axis=0, tiled=True),
        lax.all_gather(query_keyvalue_lift, "mem", axis=1, tiled=True),
        lax.all_gather(output_combiner, "mem", axis=1, tiled=True),
        lax.all_gather(decoder_linear_map, "mem", axis=1, tiled=True),
    )
    attention_span = full_embed.shape[1]
    hidden = jnp.dot(
        starting_ensemble.reshape(-1, feats), full_embed, preferred_element_type=jnp.float32
    )
    hidden = hidden.astype(jnp.bfloat16).reshape(members, rows, cols, attention_span)
    normed = layer_norm(hidden).astype(jnp.bfloat16)
    half = PANE_SIDE // 2
    incoming_rows = passed_along(normed[:, :, :half], "tile", -1)
    padded_sequence = jnp.concatenate([normed[:, :, half:], incoming_rows], axis=2)
    mixed_outcome_padded = pane_cosine_mixer(
        padded_sequence, entire_triplet_product, cosine_logit_scale
    )
    returned = passed_along(mixed_outcome_padded[:, :, cols - half :], "tile", 1)
    mixed_outcome = jnp.concatenate([returned, mixed_outcome_padded[:, :, : cols - half]], axis=2)
    mixed = hidden.astype(jnp.float32) + jnp.dot(
        mixed_outcome.reshape(-1, attention_span), full_out, preferred_element_type=jnp.float32
    ).reshape(members, rows, cols, attention_span)
    embedded_patches = layer_norm(mixed).astype(jnp.bfloat16)
    tile_tokens = rows * cols
    moved = lax.all_to_all(
        embedded_patches.reshape(members, tile_tokens, attention_span),
        "mem",
        split_axis=1,
        concat_axis=0,
        tiled=True,
    )
    ensemble, regions = (moved.shape[0], moved.shape[1])
    posterior = local_analysis(
        moved,
        full_head,
        sensor_gridpoint.reshape(-1),
        sensor_domain_index.reshape(-1),
        sensor_channel_list.reshape(-1),
        sensor_reading.reshape(-1),
        sensor_noise_deviation.reshape(-1),
        sensor_variable_loadings,
    )
    produced = jnp.dot(
        posterior.reshape(-1, attention_span), full_head, preferred_element_type=jnp.float32
    )
    produced = produced.astype(jnp.bfloat16).reshape(ensemble, regions, feats)
    analysed = lax.all_to_all(produced, "mem", split_axis=0, concat_axis=1, tiled=True)
    return analysed.reshape(members, rows, cols, feats)


def iota(shape, dim):
    return lax.broadcasted_iota(jnp.int32, shape, dim)


def dot(left, right):
    return jnp.dot(left, right, preferred_element_type=jnp.float32)


def dot_nt(left, right):
    return lax.dot_general(
        left, right, (((1,), (1,)), ((), ())), preferred_element_type=jnp.float32
    )


def two_terms(values):
    high = values.astype(jnp.bfloat16)
    return high, (values - high.astype(jnp.float32)).astype(jnp.bfloat16)


def fine(left, right):
    left_high, left_low = two_terms(left)
    right_high, right_low = two_terms(right)
    return dot(
        jnp.concatenate([left_high, left_low], axis=1),
        jnp.concatenate([right_high, right_high], axis=0),
    ) + dot(left_high, right_low)


def fine_nt(left, right):
    left_high, left_low = two_terms(left)
    right_high, right_low = two_terms(right)
    return (
        dot_nt(left_high, right_high) + dot_nt(left_low, right_high) + dot_nt(left_high, right_low)
    )


def one_hot(mask):
    return jnp.where(mask, 1.0, 0.0).astype(jnp.bfloat16)


def picked(rows, source):
    return one_hot(source == iota((rows, rows), 1))


def forecast_and_analyse(
    heads,
    x_ref,
    embed_ref,
    qkv_ref,
    comb_ref,
    dec_ref,
    scale_ref,
    load_ref,
    grid_ref,
    dom_ref,
    chan_ref,
    read_ref,
    noise_ref,
    out_ref,
    g_embed,
    g_qkv,
    g_comb,
    g_dec,
    x_pad,
    to_west,
    window,
    qkv_buf,
    ctx,
    from_west,
    lat_send,
    lat_recv,
    pos_send,
    pos_recv,
    w_send,
    w_recv,
    t_send,
    t_recv,
    a_send,
    a_recv,
):
    bf16, f32 = jnp.bfloat16, jnp.float32
    me = lax.axis_index("mem")
    tile = lax.axis_index("tile")
    tiles = lax.axis_size("tile")
    n = lax.axis_size("mem")
    core = me % 2
    along_x = (me // 2) % 2
    along_y = me // 4
    to_sib = 1 - 2 * core
    sib = me + to_sib
    x_nb = me + 2 - 4 * along_x
    y_nb = me + 4 - 8 * along_y
    diag = x_nb + 4 - 8 * along_y
    odd = tile % 2
    partner = tile + 1 - 2 * odd
    west = (tile + tiles - 1) % tiles
    east = (tile + 1) % tiles

    tokens, span = window.shape
    half = tokens // 2
    feats = x_ref.shape[1]
    piece = feats // n
    padded = g_embed.shape[0] // n
    width = padded * n
    count = grid_ref.shape[2]
    variables = load_ref.shape[1]

    barrier = pltpu.get_barrier_semaphore()
    for step in range(1, n):
        pl.semaphore_signal(
            barrier, inc=1, device_id=((me + step) % n, tile), device_id_type=MESH
        )
    for other in (west, east):
        pl.semaphore_signal(barrier, inc=1, device_id=(me, other), device_id_type=MESH)

    gathered = (g_embed, g_qkv, g_comb, g_dec)
    sends = []

    def copy(w, kind, owner, first, rows, target):
        held = gathered[w]
        block = held.shape[0] // n
        part = held.at[pl.ds(pl.multiple_of(owner * block + first, 16), rows)]
        return pltpu.make_async_remote_copy(
            src_ref=part,
            dst_ref=part,
            send_sem=w_send.at[w * KINDS + kind],
            recv_sem=w_recv.at[w * KINDS + kind],
            device_id=target,
            device_id_type=MESH,
        )

    here = {
        "sib": (sib, tile),
        "x": (x_nb, tile),
        "y": (y_nb, tile),
        "z": (me, partner),
    }

    def send(w, kind, owner, first, rows, way):
        sent = copy(w, kind, owner, first, rows, here[way])
        sent.start()
        sends.append(sent)

    def arrived(w, kind, owner, first, rows):
        copy(w, kind, owner, first, rows, here["sib"]).wait_recv()

    def third(w):
        return gathered[w].shape[0] // n // 3

    def own_first(w):
        t = third(w)
        send(w, 1, me, 2 * odd * t, t, "x")
        send(w, 2, me, 2 * odd * t, t, "y")

    def own_second(w):
        t = third(w)
        send(w, 15, me, t, t, "x")
        send(w, 16, me, t, t, "y")
        send(w, 0, me, 0, 3 * t, "sib")

    def pass_first(w):
        t = third(w)
        arrived(w, 1, x_nb, 2 * odd * t, t)
        send(w, 5, x_nb, 2 * odd * t, t, "y")
        send(w, 9, x_nb, 2 * odd * t, t, "z")
        arrived(w, 2, y_nb, 2 * odd * t, t)
        send(w, 10, y_nb, 2 * odd * t, t, "z")

    def pass_second(w):
        t = third(w)
        arrived(w, 16, y_nb, t, t)
        send(w, 6, y_nb, t, t, "x")
        send(w, 4, y_nb, odd * t, 2 * t, "sib")
        arrived(w, 15, x_nb, t, t)
        send(w, 3, x_nb, odd * t, 2 * t, "sib")

    def pass_diagonal(w):
        t = third(w)
        arrived(w, 5, diag, 2 * odd * t, t)
        send(w, 11, diag, 2 * odd * t, t, "z")
        send(w, 7, diag, 2 * odd * t, t, "sib")
        arrived(w, 6, diag, t, t)
        send(w, 8, diag, t, t, "sib")

    def pass_partner(w):
        t = third(w)
        for kind, owner in ((9, x_nb), (10, y_nb), (11, diag)):
            arrived(w, kind, owner, 2 * (1 - odd) * t, t)
            send(w, kind + 3, owner, 2 * (1 - odd) * t, t, "sib")

    def complete(w):
        t = third(w)
        arrived(w, 0, sib, 0, 3 * t)
        arrived(w, 3, x_nb + to_sib, odd * t, 2 * t)
        arrived(w, 4, y_nb + to_sib, odd * t, 2 * t)
        arrived(w, 7, diag + to_sib, 2 * odd * t, t)
        arrived(w, 8, diag + to_sib, t, t)
        for kind, owner in ((12, x_nb), (13, y_nb), (14, diag)):
            arrived(w, kind, owner + to_sib, 2 * (1 - odd) * t, t)

    def keep_own(w, ref):
        block = gathered[w].shape[0] // n
        rows = ref.shape[0] // 16 * 16
        gathered[w][pl.ds(pl.multiple_of(me * block, 16), rows), :] = ref[:rows, :]
        if rows < block:
            left = ref.shape[0] - rows
            mask = one_hot(iota((block - rows, left), 0) == iota((block - rows, left), 1))
            gathered[w][pl.ds(pl.multiple_of(me * block + rows, 16), block - rows), :] = dot(
                mask, ref[rows:, :]
            ).astype(bf16)

    EMBED, QKV, COMB, DEC = 0, 1, 2, 3

    keep_own(EMBED, embed_ref)
    keep_own(QKV, qkv_ref)
    pl.semaphore_wait(barrier, n + 1)
    own_first(EMBED)
    own_second(EMBED)
    own_first(QKV)
    keep_own(COMB, comb_ref)
    keep_own(DEC, dec_ref)

    row = iota((tokens, tokens), 0)
    by_half = picked(
        tokens,
        ((row >> 5) & 1) * 64 + ((row >> 2) & 7) * 8 + (row >> 6) * 4 + (row & 3),
    )
    x_rows = dot(by_half, x_ref[...]).astype(bf16)
    x_pad[...] = jnp.zeros(x_pad.shape, bf16)
    for d in range(n):
        x_pad[:, padded * d : padded * d + piece] = x_rows[:, piece * d : piece * (d + 1)]

    pass_first(EMBED)
    pass_second(EMBED)
    own_second(QKV)

    within = iota((n, padded, variables), 1)
    within = within - jnp.where(within >= variables, variables, 0)
    pick_variable = one_hot(within == iota((n, padded, variables), 2)).reshape(width, variables)
    channels = load_ref.shape[0]
    loads = dot_nt(pick_variable, load_ref[...]).astype(bf16)
    chan_hot = one_hot(jnp.broadcast_to(chan_ref[0], (channels, count)) == iota((channels, count), 0))
    mapping = dot(loads, chan_hot)
    grid_point = grid_ref[0]
    points = feats // variables
    token_row = grid_point >> 4
    point_row = grid_point & (points - 1)
    dom_row = dom_ref[0]
    slot = iota((n, padded, count), 0) * 2 + jnp.where(
        iota((n, padded, count), 1) >= variables, 1, 0
    )
    mapping = jnp.where(
        slot.reshape(width, count) == jnp.broadcast_to(point_row, (width, count)), mapping, 0.0
    ).astype(bf16)

    pass_diagonal(EMBED)
    own_first(COMB)
    pass_first(QKV)
    pass_partner(EMBED)
    own_second(COMB)
    complete(EMBED)

    hidden = dot(x_pad[...], g_embed[...]).astype(bf16)
    normed = layer_norm(hidden).astype(bf16)
    to_west[...] = normed[:half]
    window[half:, :] = normed[half:]

    def along_tile(index, source, target, way):
        return pltpu.make_async_remote_copy(
            src_ref=source,
            dst_ref=target,
            send_sem=t_send.at[index],
            recv_sem=t_recv.at[index],
            device_id=(me, way),
            device_id_type=MESH,
        )

    westward = along_tile(0, to_west, window.at[pl.ds(0, half)], west)
    westward.start()
    sends.append(westward)

    pass_second(QKV)
    own_first(DEC)
    pass_first(COMB)
    pass_diagonal(QKV)
    own_second(DEC)
    pass_second(COMB)
    pass_partner(QKV)
    complete(QKV)
    qkv_buf[half:, :] = dot_nt(window[half:, :], g_qkv[...]).astype(bf16)
    pass_first(DEC)
    pass_diagonal(COMB)
    westward.wait_recv()
    qkv_buf[:half, :] = dot_nt(window[:half, :], g_qkv[...]).astype(bf16)
    pass_second(DEC)

    side = span // heads
    pair = 2 * side
    one_head = iota((pair, pair), 0) // side == iota((pair, pair), 1) // side
    head_sum = one_hot(one_head)
    head_sums = jnp.concatenate([head_sum, head_sum], axis=0)
    lane = iota((tokens, pair), 1)
    first = jnp.where(lane < side, 1.0, 0.0).astype(bf16)
    second = jnp.where(lane < side, 0.0, 1.0).astype(bf16)
    share = jnp.concatenate([first, second], axis=0)
    key_of = iota((half, 2 * tokens), 1)
    same_member = ((iota((half, 2 * tokens), 0) >> 5) & 1) == ((key_of >> 5) & 1)

    def unit_pair(rows, start):
        values = qkv_buf[rows, start : start + pair].astype(f32)
        squares = jnp.concatenate(two_terms(values * values), axis=1)
        return (values * lax.rsqrt(dot(squares, head_sums) + normalizing_guard)).astype(bf16)

    def attend(rows, pairs):
        for p in pairs:
            start = pair * p
            query = unit_pair(rows, start)
            key = keys[p]
            scales = jnp.where(key_of < tokens, scale_ref[2 * p], scale_ref[2 * p + 1])
            weights = jnp.where(same_member, jnp.exp(dot_nt(query, key) * scales), 0.0).astype(bf16)
            value = qkv_buf[:, 2 * span + start : 2 * span + start + pair]
            value = jnp.concatenate([value * first, value * second], axis=0)
            total = dot(weights, jnp.concatenate([value, share], axis=1))
            ctx[rows, start : start + pair] = (total[:, :pair] / total[:, pair:]).astype(bf16)

    keys = []
    for p in range(heads // 2):
        key = unit_pair(slice(None), span + pair * p)
        keys.append(jnp.concatenate([key * first, key * second], axis=0))
    attend(slice(0, half), range(heads // 2))
    eastward = along_tile(1, ctx.at[pl.ds(0, half)], from_west, east)
    eastward.start()
    sends.append(eastward)
    pass_partner(COMB)
    pass_diagonal(DEC)
    attend(slice(half, tokens), range(heads // 2))
    complete(COMB)
    pass_partner(DEC)
    own_half = dot_nt(ctx[half:, :], g_comb[...])
    eastward.wait_recv()
    mixed = hidden.astype(f32) + jnp.concatenate(
        [dot_nt(from_west[...], g_comb[...]), own_half], axis=0
    )
    latent = layer_norm(mixed).astype(bf16)
    by_region = picked(
        tokens,
        ((row >> 2) & 1) * 64 + ((row >> 3) & 1) * 32 + (row >> 4) * 4 + (row & 3),
    )
    lat_send[...] = dot(by_region, latent).astype(bf16)

    block = tokens // n

    def exchange(index, source, target):
        mine = pl.ds(pl.multiple_of(me * block, 16), block)
        for step in range(1, n):
            to = (me + step) % n
            sent = pltpu.make_async_remote_copy(
                src_ref=source.at[pl.ds(pl.multiple_of(to * block, 16), block)],
                dst_ref=target.at[mine],
                send_sem=a_send.at[index * n + step],
                recv_sem=a_recv.at[index * n + step],
                device_id=(to, tile),
                device_id_type=MESH,
            )
            sent.start()
            sends.append(sent)
        target[mine, :] = source[mine, :]

    def exchanged(index, source, target):
        for step in range(1, n):
            origin = (me + n - step) % n
            part = pl.ds(pl.multiple_of(origin * block, 16), block)
            pltpu.make_async_remote_copy(
                src_ref=source.at[part],
                dst_ref=target.at[part],
                send_sem=a_send.at[index * n + step],
                recv_sem=a_recv.at[index * n + step],
                device_id=(origin, tile),
                device_id_type=MESH,
            ).wait_recv()

    exchange(0, lat_send, lat_recv)
    complete(DEC)
    exchanged(0, lat_send, lat_recv)

    regions = n
    members = tokens // regions
    values = lat_recv[...]
    prior = dot_nt(values, g_dec[...]).astype(bf16)
    samples = dot(prior, mapping).reshape(members, regions, count)
    region3 = iota((members, regions, count), 1)
    samples = jnp.where(region3 == token_row[None], samples, 0.0)
    ens_obs = jnp.sum(samples, axis=1, keepdims=True)
    mean_obs = jnp.mean(ens_obs, axis=0, keepdims=True)
    in_region = region3 == dom_row[None]
    pert = jnp.where(in_region, ens_obs - mean_obs, 0.0).reshape(tokens, count)
    innovation = read_ref[0] - mean_obs[0]
    distance = (token_row - dom_row).astype(f32)
    noise = noise_ref[0]
    obs_weight = jnp.exp(-0.5 * distance * distance) / (noise * noise)
    weighted = pert * obs_weight
    gram = fine_nt(weighted, pert)
    drive = fine_nt(jnp.broadcast_to(innovation, (tokens, count)), weighted)
    unit = jnp.where(row == iota((tokens, tokens), 1), 1.0, 0.0)
    system = unit + gram * (1.0 / (members - 1.0))
    sums = jnp.sum(jnp.abs(system), axis=1, keepdims=True).reshape(members, regions, 1)
    bound = jnp.broadcast_to(
        jnp.max(sums, axis=0, keepdims=True), (members, regions, 1)
    ).reshape(tokens, 1)
    iterate = system / bound
    inverse_root = None
    for step in range(NS_ITERS):
        if step == 0:
            factor = 1.5 * unit - 0.5 * iterate
            inverse_root = factor
        else:
            factor = 1.5 * unit - 0.5 * fine(inverse_root, iterate)
            inverse_root = fine(factor, inverse_root)
        if step < NS_ITERS - 1:
            iterate = fine(iterate, factor)
    root = inverse_root * lax.rsqrt(bound)
    inner = fine(drive, root)
    mean_weight = fine(inner, root) * (1.0 / (members - 1.0))
    same_region = (row & (regions - 1)) == (iota((tokens, tokens), 1) & (regions - 1))
    transform_back = jnp.where(same_region, root + mean_weight, 0.0)
    latents = values.astype(f32).reshape(members, regions, span)
    center = jnp.mean(latents, axis=0, keepdims=True)
    spread = (latents - center).reshape(tokens, span)
    posterior = jnp.broadcast_to(center, latents.shape).reshape(tokens, span) + fine(
        transform_back, spread
    )
    pos_send[...] = posterior.astype(bf16)
    exchange(1, pos_send, pos_recv)
    exchanged(1, pos_send, pos_recv)
    by_member = picked(tokens, ((row >> 3) & 7) * 16 + (row >> 6) * 8 + (row & 7))
    analysed = dot_nt(dot(by_member, pos_recv[...]).astype(bf16), g_dec[...])
    for d in range(n):
        out_ref[:, piece * d : piece * (d + 1)] = analysed[
            :, padded * d : padded * d + piece
        ].astype(bf16)
    for sent in sends:
        sent.wait_send()


def per_device_fused(
    starting_ensemble,
    patch_lifting,
    query_keyvalue_lift,
    output_combiner,
    decoder_linear_map,
    cosine_logit_scale,
    sensor_variable_loadings,
    *sensors,
):
    n = lax.axis_size("mem")
    members, rows, cols, feats = starting_ensemble.shape
    tokens = members * rows * cols
    span = patch_lifting.shape[1]
    padded = -(-patch_lifting.shape[0] // 48) * 48
    vmem = pl.BlockSpec(memory_space=pltpu.VMEM)
    smem = pl.BlockSpec(memory_space=pltpu.SMEM)

    def held(*shape):
        return pltpu.VMEM(shape, jnp.bfloat16)

    out = pl.pallas_call(
        functools.partial(forecast_and_analyse, cosine_logit_scale.shape[0]),
        out_shape=jax.ShapeDtypeStruct((tokens, feats), jnp.bfloat16),
        in_specs=[vmem] * 5 + [smem] + [vmem] * 6,
        out_specs=vmem,
        scratch_shapes=[
            held(padded * n, span),
            held(query_keyvalue_lift.shape[1] * n, span),
            held(output_combiner.shape[1] * n, span),
            held(padded * n, span),
            held(tokens, padded * n),
            held(tokens // 2, span),
            held(tokens, span),
            held(tokens, 3 * span),
            held(tokens, span),
            held(tokens // 2, span),
            held(tokens, span),
            held(tokens, span),
            held(tokens, span),
            held(tokens, span),
            pltpu.SemaphoreType.DMA((4 * KINDS,)),
            pltpu.SemaphoreType.DMA((4 * KINDS,)),
            pltpu.SemaphoreType.DMA((2,)),
            pltpu.SemaphoreType.DMA((2,)),
            pltpu.SemaphoreType.DMA((2 * n,)),
            pltpu.SemaphoreType.DMA((2 * n,)),
        ],
        compiler_params=pltpu.CompilerParams(
            collective_id=0, has_side_effects=True, vmem_limit_bytes=48 * 1024 * 1024
        ),
        cost_estimate=pl.CostEstimate(
            flops=2 * tokens * span * (3 * feats + 4 * span),
            bytes_accessed=16 * 1024 * 1024,
            transcendentals=0,
        ),
    )(
        starting_ensemble.reshape(tokens, feats),
        patch_lifting,
        query_keyvalue_lift.T,
        output_combiner.T,
        decoder_linear_map.T,
        cosine_logit_scale,
        sensor_variable_loadings,
        *sensors,
    )
    return out.reshape(members, rows, cols, feats)


def fits_fused(mesh, starting_ensemble, patch_lifting, query_keyvalue_lift, output_combiner, loads):
    n, tiles = mesh.shape["mem"], mesh.shape["tile"]
    members, rows, cols, feats = starting_ensemble.shape
    return (
        n == 8
        and tiles % 2 == 0
        and tiles > 2
        and (members // n, rows, cols // tiles) == (2, 8, 8)
        and feats == 16 * loads.shape[1]
        and query_keyvalue_lift.shape[1] % (48 * n) == 0
        and output_combiner.shape[1] % (48 * n) == 0
    )


def solution(mesh):
    def whole(*args):
        fused = fits_fused(mesh, args[0], args[1], args[2], args[3], args[6])
        return jax.shard_map(
            per_device_fused if fused else per_device,
            mesh=mesh,
            in_specs=(
                P("mem", None, "tile", None),
                P("mem", None),
                P(None, "mem"),
                P(None, "mem"),
                P(None, "mem"),
                P(),
                P(),
                P("mem", "tile", None),
                P("mem", "tile", None),
                P("mem", "tile", None),
                P("mem", "tile", None),
                P("mem", "tile", None),
            ),
            out_specs=P("mem", None, "tile", None),
            check_vma=False,
        )(*args)

    return whole
```

```python
import functools

import jax
import jax.numpy as jnp
from jax import lax
from jax.experimental import pallas as pl
from jax.experimental.pallas import tpu as pltpu
from jax.sharding import PartitionSpec as P

PANE_SIDE = 8
NS_ITERS = 5
KINDS = 17
MESH = pl.DeviceIdType.MESH


eps_norm = 1e-05
normalizing_guard = 1e-06


def passed_along(value, axis, by):
    devices = lax.axis_size(axis)
    return lax.ppermute(value, axis, [(i, (i + by) % devices) for i in range(devices)])


def layer_norm(values):
    values = values.astype(jnp.float32)
    center = values - jnp.mean(values, axis=-1, keepdims=True)
    spread = jnp.mean(center * center, axis=-1, keepdims=True)
    return center * lax.rsqrt(spread + eps_norm)


def unit_rows(values):
    values = values.astype(jnp.float32)
    return (
        values * lax.rsqrt(jnp.sum(values * values, axis=-1, keepdims=True) + normalizing_guard)
    ).astype(jnp.bfloat16)


def pane_cosine_mixer(padded_part, query_keyvalue_lift, cosine_logit_scale):
    members, rows, cols, attention_span = padded_part.shape
    focus_groups = cosine_logit_scale.shape[0]
    head_dim = attention_span // focus_groups
    qkv = jnp.dot(
        padded_part.reshape(-1, attention_span),
        query_keyvalue_lift,
        preferred_element_type=jnp.float32,
    ).astype(jnp.bfloat16)
    qkv = qkv.reshape(
        members, rows // PANE_SIDE, PANE_SIDE, cols // PANE_SIDE, PANE_SIDE, 3 * attention_span
    )
    qkv = qkv.transpose(0, 1, 3, 2, 4, 5).reshape(
        -1, PANE_SIDE * PANE_SIDE, 3, focus_groups, head_dim
    )
    query = unit_rows(qkv[:, :, 0])
    key_rows = unit_rows(qkv[:, :, 1])
    value_rows = qkv[:, :, 2]
    affinity_logits = jnp.einsum(
        "bihd,bjhd->bhij", query, key_rows, preferred_element_type=jnp.float32
    )
    affinity_logits = affinity_logits * cosine_logit_scale[None, :, None, None]
    weights = jnp.exp(affinity_logits)
    probs = (weights / jnp.sum(weights, axis=-1, keepdims=True)).astype(jnp.bfloat16)
    mixed_outcome = jnp.einsum(
        "bhij,bjhd->bihd", probs, value_rows, preferred_element_type=jnp.float32
    )
    mixed_outcome = mixed_outcome.astype(jnp.bfloat16).reshape(
        members, rows // PANE_SIDE, cols // PANE_SIDE, PANE_SIDE, PANE_SIDE, attention_span
    )
    return mixed_outcome.transpose(0, 1, 3, 2, 4, 5).reshape(members, rows, cols, attention_span)


def batched(left, right):
    return jnp.einsum("rij,rjk->rik", left, right, precision=lax.Precision.HIGHEST)


def local_analysis(
    embedded_patches,
    decoder_linear_map,
    sensor_gridpoint,
    sensor_domain_index,
    sensor_channel_list,
    sensor_reading,
    sensor_noise_deviation,
    sensor_variable_loadings,
):
    members, regions, attention_span = embedded_patches.shape
    feats = decoder_linear_map.shape[1]
    channels, variables = sensor_variable_loadings.shape
    points = feats // variables
    count = sensor_gridpoint.shape[0]
    prior_member_grids = jnp.dot(
        embedded_patches.reshape(-1, attention_span),
        decoder_linear_map,
        preferred_element_type=jnp.float32,
    ).astype(jnp.bfloat16)
    token = sensor_gridpoint // points
    point = sensor_gridpoint - token * points
    pick_point = (point[:, None] == jnp.arange(points, dtype=jnp.int32)[None, :]).astype(
        jnp.float32
    )
    pick_chan = (
        sensor_channel_list[:, None] == jnp.arange(channels, dtype=jnp.int32)[None, :]
    ).astype(jnp.float32)
    rows_h = jnp.dot(
        pick_chan, sensor_variable_loadings.astype(jnp.float32), precision=lax.Precision.HIGHEST
    )
    measurement_mapping = (
        (pick_point[:, :, None] * rows_h[:, None, :]).reshape(count, feats).astype(jnp.bfloat16)
    )
    mapped_samples = lax.dot_general(
        prior_member_grids,
        measurement_mapping,
        (((1,), (1,)), ((), ())),
        preferred_element_type=jnp.float32,
    )
    mapped_samples = mapped_samples.reshape(members, regions, count)
    pick_token = (token[None, :] == jnp.arange(regions, dtype=jnp.int32)[:, None]).astype(
        jnp.float32
    )
    ens_obs = jnp.sum(mapped_samples * pick_token[None], axis=1)
    mean_obs = jnp.mean(ens_obs, axis=0)
    pert_obs = ens_obs - mean_obs[None, :]
    innovation = sensor_reading - mean_obs
    distance = (token - sensor_domain_index).astype(jnp.float32)
    obs_weight = jnp.exp(-0.5 * distance * distance) / (
        sensor_noise_deviation * sensor_noise_deviation
    )
    pick_region = (
        sensor_domain_index[:, None] == jnp.arange(regions, dtype=jnp.int32)[None, :]
    ).astype(jnp.float32)
    weighted = pert_obs * obs_weight[None, :]
    gram = jnp.einsum(
        "kj,jr,lj->rkl", weighted, pick_region, pert_obs, precision=lax.Precision.HIGHEST
    )
    drive = jnp.einsum(
        "kj,jr,j->rk", weighted, pick_region, innovation, precision=lax.Precision.HIGHEST
    )
    eye = jnp.eye(members, dtype=jnp.float32)
    system = eye[None] + gram / (members - 1.0)
    bound = jnp.max(jnp.sum(jnp.abs(system), axis=2), axis=1)
    iterate = system / bound[:, None, None]
    inverse_root = jnp.broadcast_to(eye, system.shape)
    for step in range(NS_ITERS):
        factor = 1.5 * eye[None] - 0.5 * batched(inverse_root, iterate)
        iterate = batched(iterate, factor)
        inverse_root = batched(factor, inverse_root)
    root = inverse_root * lax.rsqrt(bound)[:, None, None]
    inner = jnp.einsum("rkl,rl->rk", root, drive, precision=lax.Precision.HIGHEST)
    mean_weight = jnp.einsum("rkl,rl->rk", root, inner, precision=lax.Precision.HIGHEST) / (
        members - 1.0
    )
    transform_matrix = root + mean_weight[:, :, None]
    values = embedded_patches.astype(jnp.float32)
    center = jnp.mean(values, axis=0)
    spread = values - center[None]
    posterior = center[None] + jnp.einsum(
        "ktf,tkm->mtf", spread, transform_matrix, precision=lax.Precision.HIGHEST
    )
    return posterior.astype(jnp.bfloat16)


def per_device(
    starting_ensemble,
    patch_lifting,
    query_keyvalue_lift,
    output_combiner,
    decoder_linear_map,
    cosine_logit_scale,
    sensor_variable_loadings,
    sensor_gridpoint,
    sensor_domain_index,
    sensor_channel_list,
    sensor_reading,
    sensor_noise_deviation,
):
    members, rows, cols, feats = starting_ensemble.shape
    full_embed, entire_triplet_product, full_out, full_head = (
        lax.all_gather(patch_lifting, "mem", axis=0, tiled=True),
        lax.all_gather(query_keyvalue_lift, "mem", axis=1, tiled=True),
        lax.all_gather(output_combiner, "mem", axis=1, tiled=True),
        lax.all_gather(decoder_linear_map, "mem", axis=1, tiled=True),
    )
    attention_span = full_embed.shape[1]
    hidden = jnp.dot(
        starting_ensemble.reshape(-1, feats), full_embed, preferred_element_type=jnp.float32
    )
    hidden = hidden.astype(jnp.bfloat16).reshape(members, rows, cols, attention_span)
    normed = layer_norm(hidden).astype(jnp.bfloat16)
    half = PANE_SIDE // 2
    incoming_rows = passed_along(normed[:, :, :half], "tile", -1)
    padded_sequence = jnp.concatenate([normed[:, :, half:], incoming_rows], axis=2)
    mixed_outcome_padded = pane_cosine_mixer(
        padded_sequence, entire_triplet_product, cosine_logit_scale
    )
    returned = passed_along(mixed_outcome_padded[:, :, cols - half :], "tile", 1)
    mixed_outcome = jnp.concatenate([returned, mixed_outcome_padded[:, :, : cols - half]], axis=2)
    mixed = hidden.astype(jnp.float32) + jnp.dot(
        mixed_outcome.reshape(-1, attention_span), full_out, preferred_element_type=jnp.float32
    ).reshape(members, rows, cols, attention_span)
    embedded_patches = layer_norm(mixed).astype(jnp.bfloat16)
    tile_tokens = rows * cols
    moved = lax.all_to_all(
        embedded_patches.reshape(members, tile_tokens, attention_span),
        "mem",
        split_axis=1,
        concat_axis=0,
        tiled=True,
    )
    ensemble, regions = (moved.shape[0], moved.shape[1])
    posterior = local_analysis(
        moved,
        full_head,
        sensor_gridpoint.reshape(-1),
        sensor_domain_index.reshape(-1),
        sensor_channel_list.reshape(-1),
        sensor_reading.reshape(-1),
        sensor_noise_deviation.reshape(-1),
        sensor_variable_loadings,
    )
    produced = jnp.dot(
        posterior.reshape(-1, attention_span), full_head, preferred_element_type=jnp.float32
    )
    produced = produced.astype(jnp.bfloat16).reshape(ensemble, regions, feats)
    analysed = lax.all_to_all(produced, "mem", split_axis=0, concat_axis=1, tiled=True)
    return analysed.reshape(members, rows, cols, feats)


def iota(shape, dim):
    return lax.broadcasted_iota(jnp.int32, shape, dim)


def dot(left, right):
    return jnp.dot(left, right, preferred_element_type=jnp.float32)


def dot_nt(left, right):
    return lax.dot_general(
        left, right, (((1,), (1,)), ((), ())), preferred_element_type=jnp.float32
    )


def two_terms(values):
    high = values.astype(jnp.bfloat16)
    return high, (values - high.astype(jnp.float32)).astype(jnp.bfloat16)


def fine(left, right):
    left_high, left_low = two_terms(left)
    right_high, right_low = two_terms(right)
    return dot(
        jnp.concatenate([left_high, left_low], axis=1),
        jnp.concatenate([right_high, right_high], axis=0),
    ) + dot(left_high, right_low)


def fine_nt(left, right):
    left_high, left_low = two_terms(left)
    right_high, right_low = two_terms(right)
    return (
        dot_nt(left_high, right_high) + dot_nt(left_low, right_high) + dot_nt(left_high, right_low)
    )


def one_hot(mask):
    return jnp.where(mask, 1.0, 0.0).astype(jnp.bfloat16)


def picked(rows, source):
    return one_hot(source == iota((rows, rows), 1))


def forecast_and_analyse(
    heads,
    x_hbm,
    embed_hbm,
    qkv_hbm,
    comb_hbm,
    dec_hbm,
    scale_hbm,
    load_hbm,
    grid_hbm,
    dom_hbm,
    chan_hbm,
    read_hbm,
    noise_hbm,
    out_ref,
    x_ref,
    embed_ref,
    dec_ref,
    scale_ref,
    load_ref,
    grid_ref,
    dom_ref,
    chan_ref,
    read_ref,
    noise_ref,
    g_embed,
    g_qkv,
    g_comb,
    g_dec,
    x_pad,
    to_west,
    window,
    qkv_buf,
    ctx,
    from_west,
    lat_send,
    lat_recv,
    pos_send,
    pos_recv,
    w_send,
    w_recv,
    t_send,
    t_recv,
    a_send,
    a_recv,
    l_sem,
):
    bf16, f32 = jnp.bfloat16, jnp.float32
    me = lax.axis_index("mem")
    tile = lax.axis_index("tile")
    tiles = lax.axis_size("tile")
    n = lax.axis_size("mem")
    core = me % 2
    along_x = (me // 2) % 2
    along_y = me // 4
    to_sib = 1 - 2 * core
    sib = me + to_sib
    x_nb = me + 2 - 4 * along_x
    y_nb = me + 4 - 8 * along_y
    diag = x_nb + 4 - 8 * along_y
    odd = tile % 2
    partner = tile + 1 - 2 * odd
    west = (tile + tiles - 1) % tiles
    east = (tile + 1) % tiles

    tokens, span = window.shape
    half = tokens // 2
    feats = x_ref.shape[1]
    piece = feats // n
    padded = g_embed.shape[0] // n
    width = padded * n
    count = grid_ref.shape[2]
    variables = load_ref.shape[1]

    def own_rows(held):
        rows = held.shape[0] // n
        return held.at[pl.ds(pl.multiple_of(me * rows, 16), rows)]

    local = [
        pltpu.make_async_copy(source, target, l_sem.at[i])
        for i, (source, target) in enumerate(
            (
                (embed_hbm, embed_ref),
                (qkv_hbm, own_rows(g_qkv)),
                (x_hbm, x_ref),
                (comb_hbm, own_rows(g_comb)),
                (dec_hbm, dec_ref),
                (load_hbm, load_ref),
                (grid_hbm, grid_ref),
                (chan_hbm, chan_ref),
                (dom_hbm, dom_ref),
                (read_hbm, read_ref),
                (noise_hbm, noise_ref),
                (scale_hbm, scale_ref),
            )
        )
    ]
    for fetched in local:
        fetched.start()

    barrier = pltpu.get_barrier_semaphore()
    for step in range(1, n):
        pl.semaphore_signal(
            barrier, inc=1, device_id=((me + step) % n, tile), device_id_type=MESH
        )
    for other in (west, east):
        pl.semaphore_signal(barrier, inc=1, device_id=(me, other), device_id_type=MESH)

    gathered = (g_embed, g_qkv, g_comb, g_dec)
    sends = []

    def copy(w, kind, owner, first, rows, target):
        held = gathered[w]
        block = held.shape[0] // n
        part = held.at[pl.ds(pl.multiple_of(owner * block + first, 16), rows)]
        return pltpu.make_async_remote_copy(
            src_ref=part,
            dst_ref=part,
            send_sem=w_send.at[w * KINDS + kind],
            recv_sem=w_recv.at[w * KINDS + kind],
            device_id=target,
            device_id_type=MESH,
        )

    here = {
        "sib": (sib, tile),
        "x": (x_nb, tile),
        "y": (y_nb, tile),
        "z": (me, partner),
    }

    def send(w, kind, owner, first, rows, way):
        sent = copy(w, kind, owner, first, rows, here[way])
        sent.start()
        sends.append(sent)

    def arrived(w, kind, owner, first, rows):
        copy(w, kind, owner, first, rows, here["sib"]).wait_recv()

    def third(w):
        return gathered[w].shape[0] // n // 3

    def own_first(w):
        t = third(w)
        send(w, 1, me, 2 * odd * t, t, "x")
        send(w, 2, me, 2 * odd * t, t, "y")

    def own_second(w):
        t = third(w)
        send(w, 15, me, t, t, "x")
        send(w, 16, me, t, t, "y")
        send(w, 0, me, 0, 3 * t, "sib")

    def pass_first(w):
        t = third(w)
        arrived(w, 1, x_nb, 2 * odd * t, t)
        send(w, 5, x_nb, 2 * odd * t, t, "y")
        send(w, 9, x_nb, 2 * odd * t, t, "z")
        arrived(w, 2, y_nb, 2 * odd * t, t)
        send(w, 10, y_nb, 2 * odd * t, t, "z")

    def pass_second(w):
        t = third(w)
        arrived(w, 16, y_nb, t, t)
        send(w, 6, y_nb, t, t, "x")
        send(w, 4, y_nb, odd * t, 2 * t, "sib")
        arrived(w, 15, x_nb, t, t)
        send(w, 3, x_nb, odd * t, 2 * t, "sib")

    def pass_diagonal(w):
        t = third(w)
        arrived(w, 5, diag, 2 * odd * t, t)
        send(w, 11, diag, 2 * odd * t, t, "z")
        send(w, 7, diag, 2 * odd * t, t, "sib")
        arrived(w, 6, diag, t, t)
        send(w, 8, diag, t, t, "sib")

    def pass_partner(w):
        t = third(w)
        for kind, owner in ((9, x_nb), (10, y_nb), (11, diag)):
            arrived(w, kind, owner, 2 * (1 - odd) * t, t)
            send(w, kind + 3, owner, 2 * (1 - odd) * t, t, "sib")

    def complete(w):
        t = third(w)
        arrived(w, 0, sib, 0, 3 * t)
        arrived(w, 3, x_nb + to_sib, odd * t, 2 * t)
        arrived(w, 4, y_nb + to_sib, odd * t, 2 * t)
        arrived(w, 7, diag + to_sib, 2 * odd * t, t)
        arrived(w, 8, diag + to_sib, t, t)
        for kind, owner in ((12, x_nb), (13, y_nb), (14, diag)):
            arrived(w, kind, owner + to_sib, 2 * (1 - odd) * t, t)

    def own_whole(w):
        rows = gathered[w].shape[0] // n
        send(w, 1, me, 0, rows, "x")
        send(w, 2, me, 0, rows, "y")
        send(w, 0, me, 0, rows, "sib")

    def pass_whole(w):
        rows = gathered[w].shape[0] // n
        upper = rows // 32 * 16
        arrived(w, 1, x_nb, 0, rows)
        send(w, 5, x_nb, 0, upper, "y")
        send(w, 3, x_nb, 0, rows, "sib")
        arrived(w, 2, y_nb, 0, rows)
        send(w, 6, y_nb, upper, rows - upper, "x")
        send(w, 4, y_nb, 0, rows, "sib")

    def pass_corner(w):
        rows = gathered[w].shape[0] // n
        upper = rows // 32 * 16
        arrived(w, 5, diag, 0, upper)
        arrived(w, 6, diag, upper, rows - upper)
        send(w, 7, diag, 0, rows, "sib")

    def complete_whole(w):
        rows = gathered[w].shape[0] // n
        for kind, owner in ((0, me), (3, x_nb), (4, y_nb), (7, diag)):
            arrived(w, kind, owner + to_sib, 0, rows)

    def keep_own(w, ref):
        block = gathered[w].shape[0] // n
        rows = ref.shape[0] // 16 * 16
        gathered[w][pl.ds(pl.multiple_of(me * block, 16), rows), :] = ref[:rows, :]
        if rows < block:
            left = ref.shape[0] - rows
            mask = one_hot(iota((block - rows, left), 0) == iota((block - rows, left), 1))
            gathered[w][pl.ds(pl.multiple_of(me * block + rows, 16), block - rows), :] = dot(
                mask, ref[rows:, :]
            ).astype(bf16)

    EMBED, QKV, COMB, DEC = 0, 1, 2, 3

    local[0].wait()
    keep_own(EMBED, embed_ref)
    pl.semaphore_wait(barrier, n + 1)
    own_first(EMBED)
    own_second(EMBED)
    local[1].wait()
    own_first(QKV)
    for fetched in local[2:]:
        fetched.wait()
    keep_own(DEC, dec_ref)

    row = iota((tokens, tokens), 0)
    by_half = picked(
        tokens,
        ((row >> 5) & 1) * 64 + ((row >> 2) & 7) * 8 + (row >> 6) * 4 + (row & 3),
    )
    x_rows = dot(by_half, x_ref[...]).astype(bf16)
    x_pad[...] = jnp.zeros(x_pad.shape, bf16)
    for d in range(n):
        x_pad[:, padded * d : padded * d + piece] = x_rows[:, piece * d : piece * (d + 1)]

    pass_first(EMBED)
    pass_second(EMBED)
    own_second(QKV)

    within = iota((n, padded, variables), 1)
    within = within - jnp.where(within >= variables, variables, 0)
    pick_variable = one_hot(within == iota((n, padded, variables), 2)).reshape(width, variables)
    channels = load_ref.shape[0]
    loads = dot_nt(pick_variable, load_ref[...]).astype(bf16)
    chan_hot = one_hot(jnp.broadcast_to(chan_ref[0], (channels, count)) == iota((channels, count), 0))
    mapping = dot(loads, chan_hot)
    grid_point = grid_ref[0]
    points = feats // variables
    token_row = grid_point >> 4
    point_row = grid_point & (points - 1)
    dom_row = dom_ref[0]
    slot = iota((n, padded, count), 0) * 2 + jnp.where(
        iota((n, padded, count), 1) >= variables, 1, 0
    )
    mapping = jnp.where(
        slot.reshape(width, count) == jnp.broadcast_to(point_row, (width, count)), mapping, 0.0
    ).astype(bf16)

    pass_diagonal(EMBED)
    pass_first(QKV)
    pass_partner(EMBED)
    own_whole(COMB)
    complete(EMBED)

    hidden = dot(x_pad[...], g_embed[...]).astype(bf16)
    normed = layer_norm(hidden).astype(bf16)
    to_west[...] = normed[:half]
    window[half:, :] = normed[half:]

    def along_tile(index, source, target, way):
        return pltpu.make_async_remote_copy(
            src_ref=source,
            dst_ref=target,
            send_sem=t_send.at[index],
            recv_sem=t_recv.at[index],
            device_id=(me, way),
            device_id_type=MESH,
        )

    westward = along_tile(0, to_west, window.at[pl.ds(0, half)], west)
    westward.start()
    sends.append(westward)

    pass_second(QKV)
    pass_diagonal(QKV)
    own_whole(DEC)
    pass_partner(QKV)
    complete(QKV)
    westward.wait_recv()
    qkv_buf[...] = dot_nt(window[...], g_qkv[...]).astype(bf16)
    pass_whole(COMB)

    side = span // heads
    pair = 2 * side
    one_head = iota((pair, pair), 0) // side == iota((pair, pair), 1) // side
    head_sum = one_hot(one_head)
    head_sums = jnp.concatenate([head_sum, head_sum], axis=0)
    lane = iota((tokens, pair), 1)
    first = jnp.where(lane < side, 1.0, 0.0).astype(bf16)
    second = jnp.where(lane < side, 0.0, 1.0).astype(bf16)
    share = jnp.concatenate([first, second], axis=0)
    key_of = iota((half, 2 * tokens), 1)
    same_member = ((iota((half, 2 * tokens), 0) >> 5) & 1) == ((key_of >> 5) & 1)

    def unit_pair(rows, start):
        values = qkv_buf[rows, start : start + pair].astype(f32)
        squares = jnp.concatenate(two_terms(values * values), axis=1)
        return (values * lax.rsqrt(dot(squares, head_sums) + normalizing_guard)).astype(bf16)

    def attend(rows, pairs):
        for p in pairs:
            start = pair * p
            query = unit_pair(rows, start)
            key = keys[p]
            scales = jnp.where(
                key_of < tokens,
                scale_ref[:, 2 * p : 2 * p + 1],
                scale_ref[:, 2 * p + 1 : 2 * p + 2],
            )
            weights = jnp.where(same_member, jnp.exp(dot_nt(query, key) * scales), 0.0).astype(bf16)
            value = qkv_buf[:, 2 * span + start : 2 * span + start + pair]
            value = jnp.concatenate([value * first, value * second], axis=0)
            total = dot(weights, jnp.concatenate([value, share], axis=1))
            ctx[rows, start : start + pair] = (total[:, :pair] / total[:, pair:]).astype(bf16)

    keys = []
    for p in range(heads // 2):
        key = unit_pair(slice(None), span + pair * p)
        keys.append(jnp.concatenate([key * first, key * second], axis=0))
    attend(slice(0, half), range(heads // 2))
    eastward = along_tile(1, ctx.at[pl.ds(0, half)], from_west, east)
    eastward.start()
    sends.append(eastward)
    pass_corner(COMB)
    pass_whole(DEC)
    attend(slice(half, tokens), range(heads // 2))
    complete_whole(COMB)
    pass_corner(DEC)
    eastward.wait_recv()
    context = jnp.concatenate([from_west[...], ctx[half:, :]], axis=0)
    mixed = hidden.astype(f32) + dot_nt(context, g_comb[...])
    latent = layer_norm(mixed).astype(bf16)
    by_region = picked(
        tokens,
        ((row >> 2) & 1) * 64 + ((row >> 3) & 1) * 32 + (row >> 4) * 4 + (row & 3),
    )
    lat_send[...] = dot(by_region, latent).astype(bf16)

    block = tokens // n

    def exchange(index, source, target):
        mine = pl.ds(pl.multiple_of(me * block, 16), block)
        for step in range(1, n):
            to = (me + step) % n
            sent = pltpu.make_async_remote_copy(
                src_ref=source.at[pl.ds(pl.multiple_of(to * block, 16), block)],
                dst_ref=target.at[mine],
                send_sem=a_send.at[index * n + step],
                recv_sem=a_recv.at[index * n + step],
                device_id=(to, tile),
                device_id_type=MESH,
            )
            sent.start()
            sends.append(sent)
        target[mine, :] = source[mine, :]

    def exchanged(index, source, target):
        for step in range(1, n):
            origin = (me + n - step) % n
            part = pl.ds(pl.multiple_of(origin * block, 16), block)
            pltpu.make_async_remote_copy(
                src_ref=source.at[part],
                dst_ref=target.at[part],
                send_sem=a_send.at[index * n + step],
                recv_sem=a_recv.at[index * n + step],
                device_id=(origin, tile),
                device_id_type=MESH,
            ).wait_recv()

    exchange(0, lat_send, lat_recv)
    complete_whole(DEC)
    exchanged(0, lat_send, lat_recv)

    regions = n
    members = tokens // regions
    values = lat_recv[...]
    prior = dot_nt(values, g_dec[...]).astype(bf16)
    samples = dot(prior, mapping).reshape(members, regions, count)
    region3 = iota((members, regions, count), 1)
    samples = jnp.where(region3 == token_row[None], samples, 0.0)
    ens_obs = jnp.sum(samples, axis=1, keepdims=True)
    mean_obs = jnp.mean(ens_obs, axis=0, keepdims=True)
    in_region = region3 == dom_row[None]
    pert = jnp.where(in_region, ens_obs - mean_obs, 0.0).reshape(tokens, count)
    innovation = read_ref[0] - mean_obs[0]
    distance = (token_row - dom_row).astype(f32)
    noise = noise_ref[0]
    obs_weight = jnp.exp(-0.5 * distance * distance) / (noise * noise)
    weighted = pert * obs_weight
    gram = fine_nt(weighted, pert)
    drive = fine_nt(jnp.broadcast_to(innovation, (tokens, count)), weighted)
    unit = jnp.where(row == iota((tokens, tokens), 1), 1.0, 0.0)
    system = unit + gram * (1.0 / (members - 1.0))
    sums = jnp.sum(jnp.abs(system), axis=1, keepdims=True).reshape(members, regions, 1)
    bound = jnp.broadcast_to(
        jnp.max(sums, axis=0, keepdims=True), (members, regions, 1)
    ).reshape(tokens, 1)
    iterate = system / bound
    inverse_root = None
    for step in range(NS_ITERS):
        if step == 0:
            factor = 1.5 * unit - 0.5 * iterate
            inverse_root = factor
        else:
            factor = 1.5 * unit - 0.5 * fine(inverse_root, iterate)
            inverse_root = fine(factor, inverse_root)
        if step < NS_ITERS - 1:
            iterate = fine(iterate, factor)
    root = inverse_root * lax.rsqrt(bound)
    inner = fine(drive, root)
    mean_weight = fine(inner, root) * (1.0 / (members - 1.0))
    same_region = (row & (regions - 1)) == (iota((tokens, tokens), 1) & (regions - 1))
    transform_back = jnp.where(same_region, root + mean_weight, 0.0)
    latents = values.astype(f32).reshape(members, regions, span)
    center = jnp.mean(latents, axis=0, keepdims=True)
    spread = (latents - center).reshape(tokens, span)
    posterior = jnp.broadcast_to(center, latents.shape).reshape(tokens, span) + fine(
        transform_back, spread
    )
    pos_send[...] = posterior.astype(bf16)
    exchange(1, pos_send, pos_recv)
    exchanged(1, pos_send, pos_recv)
    by_member = picked(tokens, ((row >> 3) & 7) * 16 + (row >> 6) * 8 + (row & 7))
    analysed = dot_nt(dot(by_member, pos_recv[...]).astype(bf16), g_dec[...])
    for d in range(n):
        out_ref[:, piece * d : piece * (d + 1)] = analysed[
            :, padded * d : padded * d + piece
        ].astype(bf16)
    for sent in sends:
        sent.wait_send()


def per_device_fused(
    starting_ensemble,
    patch_lifting,
    query_keyvalue_lift,
    output_combiner,
    decoder_linear_map,
    cosine_logit_scale,
    sensor_variable_loadings,
    *sensors,
):
    n = lax.axis_size("mem")
    members, rows, cols, feats = starting_ensemble.shape
    tokens = members * rows * cols
    span = patch_lifting.shape[1]
    padded = -(-patch_lifting.shape[0] // 48) * 48
    vmem = pl.BlockSpec(memory_space=pltpu.VMEM)
    hbm = pl.BlockSpec(memory_space=pltpu.HBM)

    def held(*shape):
        return pltpu.VMEM(shape, jnp.bfloat16)

    out = pl.pallas_call(
        functools.partial(forecast_and_analyse, cosine_logit_scale.shape[0]),
        out_shape=jax.ShapeDtypeStruct((tokens, feats), jnp.bfloat16),
        in_specs=[hbm] * 12,
        out_specs=vmem,
        scratch_shapes=[
            held(tokens, feats),
            held(*patch_lifting.shape),
            held(decoder_linear_map.shape[1], span),
            pltpu.VMEM((1, cosine_logit_scale.shape[0]), jnp.float32),
            held(*sensor_variable_loadings.shape),
            *[pltpu.VMEM(sensor.shape, sensor.dtype) for sensor in sensors],
            held(padded * n, span),
            held(query_keyvalue_lift.shape[1] * n, span),
            held(output_combiner.shape[1] * n, span),
            held(padded * n, span),
            held(tokens, padded * n),
            held(tokens // 2, span),
            held(tokens, span),
            held(tokens, 3 * span),
            held(tokens, span),
            held(tokens // 2, span),
            held(tokens, span),
            held(tokens, span),
            held(tokens, span),
            held(tokens, span),
            pltpu.SemaphoreType.DMA((4 * KINDS,)),
            pltpu.SemaphoreType.DMA((4 * KINDS,)),
            pltpu.SemaphoreType.DMA((2,)),
            pltpu.SemaphoreType.DMA((2,)),
            pltpu.SemaphoreType.DMA((2 * n,)),
            pltpu.SemaphoreType.DMA((2 * n,)),
            pltpu.SemaphoreType.DMA((12,)),
        ],
        compiler_params=pltpu.CompilerParams(
            collective_id=0, has_side_effects=True, vmem_limit_bytes=63 * 1024 * 1024
        ),
        cost_estimate=pl.CostEstimate(
            flops=2 * tokens * span * (3 * feats + 4 * span),
            bytes_accessed=16 * 1024 * 1024,
            transcendentals=0,
        ),
    )(
        starting_ensemble.reshape(tokens, feats),
        patch_lifting,
        query_keyvalue_lift.T,
        output_combiner.T,
        decoder_linear_map.T,
        cosine_logit_scale.reshape(1, -1),
        sensor_variable_loadings,
        *sensors,
    )
    return out.reshape(members, rows, cols, feats)


def fits_fused(mesh, starting_ensemble, patch_lifting, query_keyvalue_lift, output_combiner, loads):
    n, tiles = mesh.shape["mem"], mesh.shape["tile"]
    members, rows, cols, feats = starting_ensemble.shape
    return (
        n == 8
        and tiles % 2 == 0
        and tiles > 2
        and (members // n, rows, cols // tiles) == (2, 8, 8)
        and feats == 16 * loads.shape[1]
        and query_keyvalue_lift.shape[1] % (48 * n) == 0
        and output_combiner.shape[1] % (48 * n) == 0
    )


def solution(mesh):
    def whole(*args):
        fused = fits_fused(mesh, args[0], args[1], args[2], args[3], args[6])
        return jax.shard_map(
            per_device_fused if fused else per_device,
            mesh=mesh,
            in_specs=(
                P("mem", None, "tile", None),
                P("mem", None),
                P(None, "mem"),
                P(None, "mem"),
                P(None, "mem"),
                P(),
                P(),
                P("mem", "tile", None),
                P("mem", "tile", None),
                P("mem", "tile", None),
                P("mem", "tile", None),
                P("mem", "tile", None),
            ),
            out_specs=P("mem", None, "tile", None),
            check_vma=False,
        )(*args)

    return whole
```

```python
import functools

import jax
import jax.numpy as jnp
from jax import lax
from jax.experimental import pallas as pl
from jax.experimental.pallas import tpu as pltpu
from jax.sharding import PartitionSpec as P

PANE_SIDE = 8
NS_ITERS = 5
KINDS = 17
MESH = pl.DeviceIdType.MESH


eps_norm = 1e-05
normalizing_guard = 1e-06


def passed_along(value, axis, by):
    devices = lax.axis_size(axis)
    return lax.ppermute(value, axis, [(i, (i + by) % devices) for i in range(devices)])


def layer_norm(values):
    values = values.astype(jnp.float32)
    center = values - jnp.mean(values, axis=-1, keepdims=True)
    spread = jnp.mean(center * center, axis=-1, keepdims=True)
    return center * lax.rsqrt(spread + eps_norm)


def unit_rows(values):
    values = values.astype(jnp.float32)
    return (
        values * lax.rsqrt(jnp.sum(values * values, axis=-1, keepdims=True) + normalizing_guard)
    ).astype(jnp.bfloat16)


def pane_cosine_mixer(padded_part, query_keyvalue_lift, cosine_logit_scale):
    members, rows, cols, attention_span = padded_part.shape
    focus_groups = cosine_logit_scale.shape[0]
    head_dim = attention_span // focus_groups
    qkv = jnp.dot(
        padded_part.reshape(-1, attention_span),
        query_keyvalue_lift,
        preferred_element_type=jnp.float32,
    ).astype(jnp.bfloat16)
    qkv = qkv.reshape(
        members, rows // PANE_SIDE, PANE_SIDE, cols // PANE_SIDE, PANE_SIDE, 3 * attention_span
    )
    qkv = qkv.transpose(0, 1, 3, 2, 4, 5).reshape(
        -1, PANE_SIDE * PANE_SIDE, 3, focus_groups, head_dim
    )
    query = unit_rows(qkv[:, :, 0])
    key_rows = unit_rows(qkv[:, :, 1])
    value_rows = qkv[:, :, 2]
    affinity_logits = jnp.einsum(
        "bihd,bjhd->bhij", query, key_rows, preferred_element_type=jnp.float32
    )
    affinity_logits = affinity_logits * cosine_logit_scale[None, :, None, None]
    weights = jnp.exp(affinity_logits)
    probs = (weights / jnp.sum(weights, axis=-1, keepdims=True)).astype(jnp.bfloat16)
    mixed_outcome = jnp.einsum(
        "bhij,bjhd->bihd", probs, value_rows, preferred_element_type=jnp.float32
    )
    mixed_outcome = mixed_outcome.astype(jnp.bfloat16).reshape(
        members, rows // PANE_SIDE, cols // PANE_SIDE, PANE_SIDE, PANE_SIDE, attention_span
    )
    return mixed_outcome.transpose(0, 1, 3, 2, 4, 5).reshape(members, rows, cols, attention_span)


def batched(left, right):
    return jnp.einsum("rij,rjk->rik", left, right, precision=lax.Precision.HIGHEST)


def local_analysis(
    embedded_patches,
    decoder_linear_map,
    sensor_gridpoint,
    sensor_domain_index,
    sensor_channel_list,
    sensor_reading,
    sensor_noise_deviation,
    sensor_variable_loadings,
):
    members, regions, attention_span = embedded_patches.shape
    feats = decoder_linear_map.shape[1]
    channels, variables = sensor_variable_loadings.shape
    points = feats // variables
    count = sensor_gridpoint.shape[0]
    prior_member_grids = jnp.dot(
        embedded_patches.reshape(-1, attention_span),
        decoder_linear_map,
        preferred_element_type=jnp.float32,
    ).astype(jnp.bfloat16)
    token = sensor_gridpoint // points
    point = sensor_gridpoint - token * points
    pick_point = (point[:, None] == jnp.arange(points, dtype=jnp.int32)[None, :]).astype(
        jnp.float32
    )
    pick_chan = (
        sensor_channel_list[:, None] == jnp.arange(channels, dtype=jnp.int32)[None, :]
    ).astype(jnp.float32)
    rows_h = jnp.dot(
        pick_chan, sensor_variable_loadings.astype(jnp.float32), precision=lax.Precision.HIGHEST
    )
    measurement_mapping = (
        (pick_point[:, :, None] * rows_h[:, None, :]).reshape(count, feats).astype(jnp.bfloat16)
    )
    mapped_samples = lax.dot_general(
        prior_member_grids,
        measurement_mapping,
        (((1,), (1,)), ((), ())),
        preferred_element_type=jnp.float32,
    )
    mapped_samples = mapped_samples.reshape(members, regions, count)
    pick_token = (token[None, :] == jnp.arange(regions, dtype=jnp.int32)[:, None]).astype(
        jnp.float32
    )
    ens_obs = jnp.sum(mapped_samples * pick_token[None], axis=1)
    mean_obs = jnp.mean(ens_obs, axis=0)
    pert_obs = ens_obs - mean_obs[None, :]
    innovation = sensor_reading - mean_obs
    distance = (token - sensor_domain_index).astype(jnp.float32)
    obs_weight = jnp.exp(-0.5 * distance * distance) / (
        sensor_noise_deviation * sensor_noise_deviation
    )
    pick_region = (
        sensor_domain_index[:, None] == jnp.arange(regions, dtype=jnp.int32)[None, :]
    ).astype(jnp.float32)
    weighted = pert_obs * obs_weight[None, :]
    gram = jnp.einsum(
        "kj,jr,lj->rkl", weighted, pick_region, pert_obs, precision=lax.Precision.HIGHEST
    )
    drive = jnp.einsum(
        "kj,jr,j->rk", weighted, pick_region, innovation, precision=lax.Precision.HIGHEST
    )
    eye = jnp.eye(members, dtype=jnp.float32)
    system = eye[None] + gram / (members - 1.0)
    bound = jnp.max(jnp.sum(jnp.abs(system), axis=2), axis=1)
    iterate = system / bound[:, None, None]
    inverse_root = jnp.broadcast_to(eye, system.shape)
    for step in range(NS_ITERS):
        factor = 1.5 * eye[None] - 0.5 * batched(inverse_root, iterate)
        iterate = batched(iterate, factor)
        inverse_root = batched(factor, inverse_root)
    root = inverse_root * lax.rsqrt(bound)[:, None, None]
    inner = jnp.einsum("rkl,rl->rk", root, drive, precision=lax.Precision.HIGHEST)
    mean_weight = jnp.einsum("rkl,rl->rk", root, inner, precision=lax.Precision.HIGHEST) / (
        members - 1.0
    )
    transform_matrix = root + mean_weight[:, :, None]
    values = embedded_patches.astype(jnp.float32)
    center = jnp.mean(values, axis=0)
    spread = values - center[None]
    posterior = center[None] + jnp.einsum(
        "ktf,tkm->mtf", spread, transform_matrix, precision=lax.Precision.HIGHEST
    )
    return posterior.astype(jnp.bfloat16)


def per_device(
    starting_ensemble,
    patch_lifting,
    query_keyvalue_lift,
    output_combiner,
    decoder_linear_map,
    cosine_logit_scale,
    sensor_variable_loadings,
    sensor_gridpoint,
    sensor_domain_index,
    sensor_channel_list,
    sensor_reading,
    sensor_noise_deviation,
):
    members, rows, cols, feats = starting_ensemble.shape
    full_embed, entire_triplet_product, full_out, full_head = (
        lax.all_gather(patch_lifting, "mem", axis=0, tiled=True),
        lax.all_gather(query_keyvalue_lift, "mem", axis=1, tiled=True),
        lax.all_gather(output_combiner, "mem", axis=1, tiled=True),
        lax.all_gather(decoder_linear_map, "mem", axis=1, tiled=True),
    )
    attention_span = full_embed.shape[1]
    hidden = jnp.dot(
        starting_ensemble.reshape(-1, feats), full_embed, preferred_element_type=jnp.float32
    )
    hidden = hidden.astype(jnp.bfloat16).reshape(members, rows, cols, attention_span)
    normed = layer_norm(hidden).astype(jnp.bfloat16)
    half = PANE_SIDE // 2
    incoming_rows = passed_along(normed[:, :, :half], "tile", -1)
    padded_sequence = jnp.concatenate([normed[:, :, half:], incoming_rows], axis=2)
    mixed_outcome_padded = pane_cosine_mixer(
        padded_sequence, entire_triplet_product, cosine_logit_scale
    )
    returned = passed_along(mixed_outcome_padded[:, :, cols - half :], "tile", 1)
    mixed_outcome = jnp.concatenate([returned, mixed_outcome_padded[:, :, : cols - half]], axis=2)
    mixed = hidden.astype(jnp.float32) + jnp.dot(
        mixed_outcome.reshape(-1, attention_span), full_out, preferred_element_type=jnp.float32
    ).reshape(members, rows, cols, attention_span)
    embedded_patches = layer_norm(mixed).astype(jnp.bfloat16)
    tile_tokens = rows * cols
    moved = lax.all_to_all(
        embedded_patches.reshape(members, tile_tokens, attention_span),
        "mem",
        split_axis=1,
        concat_axis=0,
        tiled=True,
    )
    ensemble, regions = (moved.shape[0], moved.shape[1])
    posterior = local_analysis(
        moved,
        full_head,
        sensor_gridpoint.reshape(-1),
        sensor_domain_index.reshape(-1),
        sensor_channel_list.reshape(-1),
        sensor_reading.reshape(-1),
        sensor_noise_deviation.reshape(-1),
        sensor_variable_loadings,
    )
    produced = jnp.dot(
        posterior.reshape(-1, attention_span), full_head, preferred_element_type=jnp.float32
    )
    produced = produced.astype(jnp.bfloat16).reshape(ensemble, regions, feats)
    analysed = lax.all_to_all(produced, "mem", split_axis=0, concat_axis=1, tiled=True)
    return analysed.reshape(members, rows, cols, feats)


def iota(shape, dim):
    return lax.broadcasted_iota(jnp.int32, shape, dim)


def dot(left, right):
    return jnp.dot(left, right, preferred_element_type=jnp.float32)


def dot_nt(left, right):
    return lax.dot_general(
        left, right, (((1,), (1,)), ((), ())), preferred_element_type=jnp.float32
    )


def two_terms(values):
    high = values.astype(jnp.bfloat16)
    return high, (values - high.astype(jnp.float32)).astype(jnp.bfloat16)


def fine(left, right):
    left_high, left_low = two_terms(left)
    right_high, right_low = two_terms(right)
    return dot(
        jnp.concatenate([left_high, left_low], axis=1),
        jnp.concatenate([right_high, right_high], axis=0),
    ) + dot(left_high, right_low)


def fine_nt(left, right):
    left_high, left_low = two_terms(left)
    right_high, right_low = two_terms(right)
    return (
        dot_nt(left_high, right_high) + dot_nt(left_low, right_high) + dot_nt(left_high, right_low)
    )


def one_hot(mask):
    return jnp.where(mask, 1.0, 0.0).astype(jnp.bfloat16)


def picked(rows, source):
    return one_hot(source == iota((rows, rows), 1))


def forecast_and_analyse(
    heads,
    x_hbm,
    embed_hbm,
    qkv_hbm,
    comb_hbm,
    dec_hbm,
    scale_hbm,
    load_hbm,
    grid_hbm,
    dom_hbm,
    chan_hbm,
    read_hbm,
    noise_hbm,
    out_ref,
    x_ref,
    embed_ref,
    dec_ref,
    scale_ref,
    load_ref,
    grid_ref,
    dom_ref,
    chan_ref,
    read_ref,
    noise_ref,
    g_embed,
    g_qkv,
    g_comb,
    g_dec,
    x_pad,
    to_west,
    window,
    qkv_buf,
    ctx,
    from_west,
    lat_send,
    lat_recv,
    pos_send,
    pos_recv,
    w_send,
    w_recv,
    t_send,
    t_recv,
    a_send,
    a_recv,
    l_sem,
):
    bf16, f32 = jnp.bfloat16, jnp.float32
    me = lax.axis_index("mem")
    tile = lax.axis_index("tile")
    tiles = lax.axis_size("tile")
    n = lax.axis_size("mem")
    core = me % 2
    along_x = (me // 2) % 2
    along_y = me // 4
    to_sib = 1 - 2 * core
    sib = me + to_sib
    x_nb = me + 2 - 4 * along_x
    y_nb = me + 4 - 8 * along_y
    diag = x_nb + 4 - 8 * along_y
    odd = tile % 2
    partner = tile + 1 - 2 * odd
    west = (tile + tiles - 1) % tiles
    east = (tile + 1) % tiles

    tokens, span = window.shape
    half = tokens // 2
    feats = x_ref.shape[1]
    piece = feats // n
    padded = g_embed.shape[0] // n
    width = padded * n
    count = grid_ref.shape[2]
    variables = load_ref.shape[1]

    def own_rows(held):
        rows = held.shape[0] // n
        return held.at[pl.ds(pl.multiple_of(me * rows, 16), rows)]

    local = [
        pltpu.make_async_copy(source, target, l_sem.at[i])
        for i, (source, target) in enumerate(
            (
                (embed_hbm, embed_ref),
                (qkv_hbm, own_rows(g_qkv)),
                (x_hbm, x_ref),
                (comb_hbm, own_rows(g_comb)),
                (dec_hbm, dec_ref),
                (load_hbm, load_ref),
                (grid_hbm, grid_ref),
                (chan_hbm, chan_ref),
                (dom_hbm, dom_ref),
                (read_hbm, read_ref),
                (noise_hbm, noise_ref),
                (scale_hbm, scale_ref),
            )
        )
    ]
    for fetched in local:
        fetched.start()

    barrier = pltpu.get_barrier_semaphore()
    for step in range(1, n):
        pl.semaphore_signal(
            barrier, inc=1, device_id=((me + step) % n, tile), device_id_type=MESH
        )
    for other in (west, east):
        pl.semaphore_signal(barrier, inc=1, device_id=(me, other), device_id_type=MESH)

    gathered = (g_embed, g_qkv, g_comb, g_dec)
    sends = []

    def copy(w, kind, owner, first, rows, target):
        held = gathered[w]
        block = held.shape[0] // n
        part = held.at[pl.ds(pl.multiple_of(owner * block + first, 16), rows)]
        return pltpu.make_async_remote_copy(
            src_ref=part,
            dst_ref=part,
            send_sem=w_send.at[w * KINDS + kind],
            recv_sem=w_recv.at[w * KINDS + kind],
            device_id=target,
            device_id_type=MESH,
        )

    here = {
        "sib": (sib, tile),
        "x": (x_nb, tile),
        "y": (y_nb, tile),
        "z": (me, partner),
    }

    def send(w, kind, owner, first, rows, way):
        sent = copy(w, kind, owner, first, rows, here[way])
        sent.start()
        sends.append(sent)

    def arrived(w, kind, owner, first, rows):
        copy(w, kind, owner, first, rows, here["sib"]).wait_recv()

    def third(w):
        return gathered[w].shape[0] // n // 3

    def own_first(w):
        t = third(w)
        send(w, 1, me, 2 * odd * t, t, "x")
        send(w, 2, me, 2 * odd * t, t, "y")

    def own_second(w):
        t = third(w)
        send(w, 15, me, t, t, "x")
        send(w, 16, me, t, t, "y")
        send(w, 0, me, 0, 3 * t, "sib")

    def pass_first(w):
        t = third(w)
        arrived(w, 1, x_nb, 2 * odd * t, t)
        send(w, 5, x_nb, 2 * odd * t, t, "y")
        send(w, 9, x_nb, 2 * odd * t, t, "z")
        arrived(w, 2, y_nb, 2 * odd * t, t)
        send(w, 10, y_nb, 2 * odd * t, t, "z")

    def pass_second(w):
        t = third(w)
        arrived(w, 16, y_nb, t, t)
        send(w, 6, y_nb, t, t, "x")
        send(w, 4, y_nb, odd * t, 2 * t, "sib")
        arrived(w, 15, x_nb, t, t)
        send(w, 3, x_nb, odd * t, 2 * t, "sib")

    def pass_diagonal(w):
        t = third(w)
        arrived(w, 5, diag, 2 * odd * t, t)
        send(w, 11, diag, 2 * odd * t, t, "z")
        send(w, 7, diag, 2 * odd * t, t, "sib")
        arrived(w, 6, diag, t, t)
        send(w, 8, diag, t, t, "sib")

    def pass_partner(w):
        t = third(w)
        for kind, owner in ((9, x_nb), (10, y_nb), (11, diag)):
            arrived(w, kind, owner, 2 * (1 - odd) * t, t)
            send(w, kind + 3, owner, 2 * (1 - odd) * t, t, "sib")

    def complete(w):
        t = third(w)
        arrived(w, 0, sib, 0, 3 * t)
        arrived(w, 3, x_nb + to_sib, odd * t, 2 * t)
        arrived(w, 4, y_nb + to_sib, odd * t, 2 * t)
        arrived(w, 7, diag + to_sib, 2 * odd * t, t)
        arrived(w, 8, diag + to_sib, t, t)
        for kind, owner in ((12, x_nb), (13, y_nb), (14, diag)):
            arrived(w, kind, owner + to_sib, 2 * (1 - odd) * t, t)

    def own_whole(w):
        rows = gathered[w].shape[0] // n
        send(w, 1, me, 0, rows, "x")
        send(w, 2, me, 0, rows, "y")
        send(w, 0, me, 0, rows, "sib")

    def pass_whole(w):
        rows = gathered[w].shape[0] // n
        upper = rows // 32 * 16
        arrived(w, 1, x_nb, 0, rows)
        send(w, 5, x_nb, 0, upper, "y")
        send(w, 3, x_nb, 0, rows, "sib")
        arrived(w, 2, y_nb, 0, rows)
        send(w, 6, y_nb, upper, rows - upper, "x")
        send(w, 4, y_nb, 0, rows, "sib")

    def pass_corner(w):
        rows = gathered[w].shape[0] // n
        upper = rows // 32 * 16
        arrived(w, 5, diag, 0, upper)
        arrived(w, 6, diag, upper, rows - upper)
        send(w, 7, diag, 0, rows, "sib")

    def complete_whole(w):
        rows = gathered[w].shape[0] // n
        for kind, owner in ((0, me), (3, x_nb), (4, y_nb), (7, diag)):
            arrived(w, kind, owner + to_sib, 0, rows)

    def keep_own(w, ref):
        block = gathered[w].shape[0] // n
        rows = ref.shape[0] // 16 * 16
        gathered[w][pl.ds(pl.multiple_of(me * block, 16), rows), :] = ref[:rows, :]
        if rows < block:
            left = ref.shape[0] - rows
            mask = one_hot(iota((block - rows, left), 0) == iota((block - rows, left), 1))
            gathered[w][pl.ds(pl.multiple_of(me * block + rows, 16), block - rows), :] = dot(
                mask, ref[rows:, :]
            ).astype(bf16)

    EMBED, QKV, COMB, DEC = 0, 1, 2, 3

    local[0].wait()
    keep_own(EMBED, embed_ref)
    pl.semaphore_wait(barrier, n + 1)
    own_first(EMBED)
    own_second(EMBED)
    for fetched in local[1:]:
        fetched.wait()

    row = iota((tokens, tokens), 0)
    by_half = picked(
        tokens,
        ((row >> 5) & 1) * 64 + ((row >> 2) & 7) * 8 + (row >> 6) * 4 + (row & 3),
    )
    x_rows = dot(by_half, x_ref[...]).astype(bf16)
    x_pad[...] = jnp.zeros(x_pad.shape, bf16)
    for d in range(n):
        x_pad[:, padded * d : padded * d + piece] = x_rows[:, piece * d : piece * (d + 1)]

    pass_first(EMBED)
    pass_second(EMBED)
    own_first(QKV)
    own_second(QKV)
    pass_diagonal(EMBED)
    pass_partner(EMBED)
    complete(EMBED)
    pass_first(QKV)

    hidden = dot(x_pad[...], g_embed[...]).astype(bf16)
    normed = layer_norm(hidden).astype(bf16)
    to_west[...] = normed[:half]
    window[half:, :] = normed[half:]

    def along_tile(index, source, target, way):
        return pltpu.make_async_remote_copy(
            src_ref=source,
            dst_ref=target,
            send_sem=t_send.at[index],
            recv_sem=t_recv.at[index],
            device_id=(me, way),
            device_id_type=MESH,
        )

    westward = along_tile(0, to_west, window.at[pl.ds(0, half)], west)
    westward.start()
    sends.append(westward)

    pass_second(QKV)
    own_whole(COMB)

    keep_own(DEC, dec_ref)
    within = iota((n, padded, variables), 1)
    within = within - jnp.where(within >= variables, variables, 0)
    pick_variable = one_hot(within == iota((n, padded, variables), 2)).reshape(width, variables)
    channels = load_ref.shape[0]
    loads = dot_nt(pick_variable, load_ref[...]).astype(bf16)
    chan_hot = one_hot(jnp.broadcast_to(chan_ref[0], (channels, count)) == iota((channels, count), 0))
    mapping = dot(loads, chan_hot)
    grid_point = grid_ref[0]
    points = feats // variables
    token_row = grid_point >> 4
    point_row = grid_point & (points - 1)
    dom_row = dom_ref[0]
    slot = iota((n, padded, count), 0) * 2 + jnp.where(
        iota((n, padded, count), 1) >= variables, 1, 0
    )
    mapping = jnp.where(
        slot.reshape(width, count) == jnp.broadcast_to(point_row, (width, count)), mapping, 0.0
    ).astype(bf16)

    pass_diagonal(QKV)
    pass_whole(COMB)
    own_whole(DEC)
    pass_partner(QKV)
    complete(QKV)
    westward.wait_recv()
    qkv_buf[...] = dot_nt(window[...], g_qkv[...]).astype(bf16)
    pass_corner(COMB)

    side = span // heads
    pair = 2 * side
    one_head = iota((pair, pair), 0) // side == iota((pair, pair), 1) // side
    head_sum = one_hot(one_head)
    head_sums = jnp.concatenate([head_sum, head_sum], axis=0)
    lane = iota((tokens, pair), 1)
    first = jnp.where(lane < side, 1.0, 0.0).astype(bf16)
    second = jnp.where(lane < side, 0.0, 1.0).astype(bf16)
    share = jnp.concatenate([first, second], axis=0)
    key_of = iota((half, 2 * tokens), 1)
    same_member = ((iota((half, 2 * tokens), 0) >> 5) & 1) == ((key_of >> 5) & 1)

    def unit_pair(rows, start):
        values = qkv_buf[rows, start : start + pair].astype(f32)
        squares = jnp.concatenate(two_terms(values * values), axis=1)
        return (values * lax.rsqrt(dot(squares, head_sums) + normalizing_guard)).astype(bf16)

    def attend(rows, pairs):
        for p in pairs:
            start = pair * p
            query = unit_pair(rows, start)
            key = keys[p]
            scales = jnp.where(
                key_of < tokens,
                scale_ref[:, 2 * p : 2 * p + 1],
                scale_ref[:, 2 * p + 1 : 2 * p + 2],
            )
            weights = jnp.where(same_member, jnp.exp(dot_nt(query, key) * scales), 0.0).astype(bf16)
            value = qkv_buf[:, 2 * span + start : 2 * span + start + pair]
            value = jnp.concatenate([value * first, value * second], axis=0)
            total = dot(weights, jnp.concatenate([value, share], axis=1))
            ctx[rows, start : start + pair] = (total[:, :pair] / total[:, pair:]).astype(bf16)

    keys = []
    for p in range(heads // 2):
        key = unit_pair(slice(None), span + pair * p)
        keys.append(jnp.concatenate([key * first, key * second], axis=0))
    attend(slice(0, half), range(heads // 2))
    eastward = along_tile(1, ctx.at[pl.ds(0, half)], from_west, east)
    eastward.start()
    sends.append(eastward)
    pass_whole(DEC)
    attend(slice(half, tokens), range(heads // 2))
    complete_whole(COMB)
    pass_corner(DEC)
    eastward.wait_recv()
    context = jnp.concatenate([from_west[...], ctx[half:, :]], axis=0)
    mixed = hidden.astype(f32) + dot_nt(context, g_comb[...])
    latent = layer_norm(mixed).astype(bf16)
    by_region = picked(
        tokens,
        ((row >> 2) & 1) * 64 + ((row >> 3) & 1) * 32 + (row >> 4) * 4 + (row & 3),
    )
    lat_send[...] = dot(by_region, latent).astype(bf16)

    block = tokens // n

    def exchange(index, source, target):
        mine = pl.ds(pl.multiple_of(me * block, 16), block)
        for step in range(1, n):
            to = (me + step) % n
            sent = pltpu.make_async_remote_copy(
                src_ref=source.at[pl.ds(pl.multiple_of(to * block, 16), block)],
                dst_ref=target.at[mine],
                send_sem=a_send.at[index * n + step],
                recv_sem=a_recv.at[index * n + step],
                device_id=(to, tile),
                device_id_type=MESH,
            )
            sent.start()
            sends.append(sent)
        target[mine, :] = source[mine, :]

    def exchanged(index, source, target):
        for step in range(1, n):
            origin = (me + n - step) % n
            part = pl.ds(pl.multiple_of(origin * block, 16), block)
            pltpu.make_async_remote_copy(
                src_ref=source.at[part],
                dst_ref=target.at[part],
                send_sem=a_send.at[index * n + step],
                recv_sem=a_recv.at[index * n + step],
                device_id=(origin, tile),
                device_id_type=MESH,
            ).wait_recv()

    exchange(0, lat_send, lat_recv)
    complete_whole(DEC)
    exchanged(0, lat_send, lat_recv)

    regions = n
    members = tokens // regions
    values = lat_recv[...]
    prior = dot_nt(values, g_dec[...]).astype(bf16)
    samples = dot(prior, mapping).reshape(members, regions, count)
    region3 = iota((members, regions, count), 1)
    samples = jnp.where(region3 == token_row[None], samples, 0.0)
    ens_obs = jnp.sum(samples, axis=1, keepdims=True)
    mean_obs = jnp.mean(ens_obs, axis=0, keepdims=True)
    in_region = region3 == dom_row[None]
    pert = jnp.where(in_region, ens_obs - mean_obs, 0.0).reshape(tokens, count)
    innovation = read_ref[0] - mean_obs[0]
    distance = (token_row - dom_row).astype(f32)
    noise = noise_ref[0]
    obs_weight = jnp.exp(-0.5 * distance * distance) / (noise * noise)
    weighted = pert * obs_weight
    gram = fine_nt(weighted, pert)
    drive = fine_nt(jnp.broadcast_to(innovation, (tokens, count)), weighted)
    unit = jnp.where(row == iota((tokens, tokens), 1), 1.0, 0.0)
    system = unit + gram * (1.0 / (members - 1.0))
    sums = jnp.sum(jnp.abs(system), axis=1, keepdims=True).reshape(members, regions, 1)
    bound = jnp.broadcast_to(
        jnp.max(sums, axis=0, keepdims=True), (members, regions, 1)
    ).reshape(tokens, 1)
    iterate = system / bound
    inverse_root = None
    for step in range(NS_ITERS):
        if step == 0:
            factor = 1.5 * unit - 0.5 * iterate
            inverse_root = factor
        else:
            factor = 1.5 * unit - 0.5 * fine(inverse_root, iterate)
            inverse_root = fine(factor, inverse_root)
        if step < NS_ITERS - 1:
            iterate = fine(iterate, factor)
    root = inverse_root * lax.rsqrt(bound)
    inner = fine(drive, root)
    mean_weight = fine(inner, root) * (1.0 / (members - 1.0))
    same_region = (row & (regions - 1)) == (iota((tokens, tokens), 1) & (regions - 1))
    transform_back = jnp.where(same_region, root + mean_weight, 0.0)
    latents = values.astype(f32).reshape(members, regions, span)
    center = jnp.mean(latents, axis=0, keepdims=True)
    spread = (latents - center).reshape(tokens, span)
    posterior = jnp.broadcast_to(center, latents.shape).reshape(tokens, span) + fine(
        transform_back, spread
    )
    pos_send[...] = posterior.astype(bf16)
    exchange(1, pos_send, pos_recv)
    for sent in sends[: 1 - n]:
        sent.wait_send()
    exchanged(1, pos_send, pos_recv)
    by_member = picked(tokens, ((row >> 3) & 7) * 16 + (row >> 6) * 8 + (row & 7))
    analysed = dot_nt(dot(by_member, pos_recv[...]).astype(bf16), g_dec[...])
    for d in range(n):
        out_ref[:, piece * d : piece * (d + 1)] = analysed[
            :, padded * d : padded * d + piece
        ].astype(bf16)
    for sent in sends[1 - n :]:
        sent.wait_send()


def per_device_fused(
    starting_ensemble,
    patch_lifting,
    query_keyvalue_lift,
    output_combiner,
    decoder_linear_map,
    cosine_logit_scale,
    sensor_variable_loadings,
    *sensors,
):
    n = lax.axis_size("mem")
    members, rows, cols, feats = starting_ensemble.shape
    tokens = members * rows * cols
    span = patch_lifting.shape[1]
    padded = -(-patch_lifting.shape[0] // 48) * 48
    vmem = pl.BlockSpec(memory_space=pltpu.VMEM)
    hbm = pl.BlockSpec(memory_space=pltpu.HBM)

    def held(*shape):
        return pltpu.VMEM(shape, jnp.bfloat16)

    out = pl.pallas_call(
        functools.partial(forecast_and_analyse, cosine_logit_scale.shape[0]),
        out_shape=jax.ShapeDtypeStruct((tokens, feats), jnp.bfloat16),
        in_specs=[hbm] * 12,
        out_specs=vmem,
        scratch_shapes=[
            held(tokens, feats),
            held(*patch_lifting.shape),
            held(decoder_linear_map.shape[1], span),
            pltpu.VMEM((1, cosine_logit_scale.shape[0]), jnp.float32),
            held(*sensor_variable_loadings.shape),
            *[pltpu.VMEM(sensor.shape, sensor.dtype) for sensor in sensors],
            held(padded * n, span),
            held(query_keyvalue_lift.shape[1] * n, span),
            held(output_combiner.shape[1] * n, span),
            held(padded * n, span),
            held(tokens, padded * n),
            held(tokens // 2, span),
            held(tokens, span),
            held(tokens, 3 * span),
            held(tokens, span),
            held(tokens // 2, span),
            held(tokens, span),
            held(tokens, span),
            held(tokens, span),
            held(tokens, span),
            pltpu.SemaphoreType.DMA((4 * KINDS,)),
            pltpu.SemaphoreType.DMA((4 * KINDS,)),
            pltpu.SemaphoreType.DMA((2,)),
            pltpu.SemaphoreType.DMA((2,)),
            pltpu.SemaphoreType.DMA((2 * n,)),
            pltpu.SemaphoreType.DMA((2 * n,)),
            pltpu.SemaphoreType.DMA((12,)),
        ],
        compiler_params=pltpu.CompilerParams(
            collective_id=0, has_side_effects=True, vmem_limit_bytes=63 * 1024 * 1024
        ),
        cost_estimate=pl.CostEstimate(
            flops=2 * tokens * span * (3 * feats + 4 * span),
            bytes_accessed=16 * 1024 * 1024,
            transcendentals=0,
        ),
    )(
        starting_ensemble.reshape(tokens, feats),
        patch_lifting,
        query_keyvalue_lift.T,
        output_combiner.T,
        decoder_linear_map.T,
        cosine_logit_scale.reshape(1, -1),
        sensor_variable_loadings,
        *sensors,
    )
    return out.reshape(members, rows, cols, feats)


def fits_fused(mesh, starting_ensemble, patch_lifting, query_keyvalue_lift, output_combiner, loads):
    n, tiles = mesh.shape["mem"], mesh.shape["tile"]
    members, rows, cols, feats = starting_ensemble.shape
    return (
        n == 8
        and tiles % 2 == 0
        and tiles > 2
        and (members // n, rows, cols // tiles) == (2, 8, 8)
        and feats == 16 * loads.shape[1]
        and query_keyvalue_lift.shape[1] % (48 * n) == 0
        and output_combiner.shape[1] % (48 * n) == 0
    )


def solution(mesh):
    def whole(*args):
        fused = fits_fused(mesh, args[0], args[1], args[2], args[3], args[6])
        return jax.shard_map(
            per_device_fused if fused else per_device,
            mesh=mesh,
            in_specs=(
                P("mem", None, "tile", None),
                P("mem", None),
                P(None, "mem"),
                P(None, "mem"),
                P(None, "mem"),
                P(),
                P(),
                P("mem", "tile", None),
                P("mem", "tile", None),
                P("mem", "tile", None),
                P("mem", "tile", None),
                P("mem", "tile", None),
            ),
            out_specs=P("mem", None, "tile", None),
            check_vma=False,
        )(*args)

    return whole
```

```python
import functools

import jax
import jax.numpy as jnp
from jax import lax
from jax.experimental import pallas as pl
from jax.experimental.pallas import tpu as pltpu
from jax.sharding import PartitionSpec as P

PANE_SIDE = 8
NS_ITERS = 5
KINDS = 17
MESH = pl.DeviceIdType.MESH


eps_norm = 1e-05
normalizing_guard = 1e-06


def passed_along(value, axis, by):
    devices = lax.axis_size(axis)
    return lax.ppermute(value, axis, [(i, (i + by) % devices) for i in range(devices)])


def layer_norm(values):
    values = values.astype(jnp.float32)
    center = values - jnp.mean(values, axis=-1, keepdims=True)
    spread = jnp.mean(center * center, axis=-1, keepdims=True)
    return center * lax.rsqrt(spread + eps_norm)


def unit_rows(values):
    values = values.astype(jnp.float32)
    return (
        values * lax.rsqrt(jnp.sum(values * values, axis=-1, keepdims=True) + normalizing_guard)
    ).astype(jnp.bfloat16)


def pane_cosine_mixer(padded_part, query_keyvalue_lift, cosine_logit_scale):
    members, rows, cols, attention_span = padded_part.shape
    focus_groups = cosine_logit_scale.shape[0]
    head_dim = attention_span // focus_groups
    qkv = jnp.dot(
        padded_part.reshape(-1, attention_span),
        query_keyvalue_lift,
        preferred_element_type=jnp.float32,
    ).astype(jnp.bfloat16)
    qkv = qkv.reshape(
        members, rows // PANE_SIDE, PANE_SIDE, cols // PANE_SIDE, PANE_SIDE, 3 * attention_span
    )
    qkv = qkv.transpose(0, 1, 3, 2, 4, 5).reshape(
        -1, PANE_SIDE * PANE_SIDE, 3, focus_groups, head_dim
    )
    query = unit_rows(qkv[:, :, 0])
    key_rows = unit_rows(qkv[:, :, 1])
    value_rows = qkv[:, :, 2]
    affinity_logits = jnp.einsum(
        "bihd,bjhd->bhij", query, key_rows, preferred_element_type=jnp.float32
    )
    affinity_logits = affinity_logits * cosine_logit_scale[None, :, None, None]
    weights = jnp.exp(affinity_logits)
    probs = (weights / jnp.sum(weights, axis=-1, keepdims=True)).astype(jnp.bfloat16)
    mixed_outcome = jnp.einsum(
        "bhij,bjhd->bihd", probs, value_rows, preferred_element_type=jnp.float32
    )
    mixed_outcome = mixed_outcome.astype(jnp.bfloat16).reshape(
        members, rows // PANE_SIDE, cols // PANE_SIDE, PANE_SIDE, PANE_SIDE, attention_span
    )
    return mixed_outcome.transpose(0, 1, 3, 2, 4, 5).reshape(members, rows, cols, attention_span)


def batched(left, right):
    return jnp.einsum("rij,rjk->rik", left, right, precision=lax.Precision.HIGHEST)


def local_analysis(
    embedded_patches,
    decoder_linear_map,
    sensor_gridpoint,
    sensor_domain_index,
    sensor_channel_list,
    sensor_reading,
    sensor_noise_deviation,
    sensor_variable_loadings,
):
    members, regions, attention_span = embedded_patches.shape
    feats = decoder_linear_map.shape[1]
    channels, variables = sensor_variable_loadings.shape
    points = feats // variables
    count = sensor_gridpoint.shape[0]
    prior_member_grids = jnp.dot(
        embedded_patches.reshape(-1, attention_span),
        decoder_linear_map,
        preferred_element_type=jnp.float32,
    ).astype(jnp.bfloat16)
    token = sensor_gridpoint // points
    point = sensor_gridpoint - token * points
    pick_point = (point[:, None] == jnp.arange(points, dtype=jnp.int32)[None, :]).astype(
        jnp.float32
    )
    pick_chan = (
        sensor_channel_list[:, None] == jnp.arange(channels, dtype=jnp.int32)[None, :]
    ).astype(jnp.float32)
    rows_h = jnp.dot(
        pick_chan, sensor_variable_loadings.astype(jnp.float32), precision=lax.Precision.HIGHEST
    )
    measurement_mapping = (
        (pick_point[:, :, None] * rows_h[:, None, :]).reshape(count, feats).astype(jnp.bfloat16)
    )
    mapped_samples = lax.dot_general(
        prior_member_grids,
        measurement_mapping,
        (((1,), (1,)), ((), ())),
        preferred_element_type=jnp.float32,
    )
    mapped_samples = mapped_samples.reshape(members, regions, count)
    pick_token = (token[None, :] == jnp.arange(regions, dtype=jnp.int32)[:, None]).astype(
        jnp.float32
    )
    ens_obs = jnp.sum(mapped_samples * pick_token[None], axis=1)
    mean_obs = jnp.mean(ens_obs, axis=0)
    pert_obs = ens_obs - mean_obs[None, :]
    innovation = sensor_reading - mean_obs
    distance = (token - sensor_domain_index).astype(jnp.float32)
    obs_weight = jnp.exp(-0.5 * distance * distance) / (
        sensor_noise_deviation * sensor_noise_deviation
    )
    pick_region = (
        sensor_domain_index[:, None] == jnp.arange(regions, dtype=jnp.int32)[None, :]
    ).astype(jnp.float32)
    weighted = pert_obs * obs_weight[None, :]
    gram = jnp.einsum(
        "kj,jr,lj->rkl", weighted, pick_region, pert_obs, precision=lax.Precision.HIGHEST
    )
    drive = jnp.einsum(
        "kj,jr,j->rk", weighted, pick_region, innovation, precision=lax.Precision.HIGHEST
    )
    eye = jnp.eye(members, dtype=jnp.float32)
    system = eye[None] + gram / (members - 1.0)
    bound = jnp.max(jnp.sum(jnp.abs(system), axis=2), axis=1)
    iterate = system / bound[:, None, None]
    inverse_root = jnp.broadcast_to(eye, system.shape)
    for step in range(NS_ITERS):
        factor = 1.5 * eye[None] - 0.5 * batched(inverse_root, iterate)
        iterate = batched(iterate, factor)
        inverse_root = batched(factor, inverse_root)
    root = inverse_root * lax.rsqrt(bound)[:, None, None]
    inner = jnp.einsum("rkl,rl->rk", root, drive, precision=lax.Precision.HIGHEST)
    mean_weight = jnp.einsum("rkl,rl->rk", root, inner, precision=lax.Precision.HIGHEST) / (
        members - 1.0
    )
    transform_matrix = root + mean_weight[:, :, None]
    values = embedded_patches.astype(jnp.float32)
    center = jnp.mean(values, axis=0)
    spread = values - center[None]
    posterior = center[None] + jnp.einsum(
        "ktf,tkm->mtf", spread, transform_matrix, precision=lax.Precision.HIGHEST
    )
    return posterior.astype(jnp.bfloat16)


def per_device(
    starting_ensemble,
    patch_lifting,
    query_keyvalue_lift,
    output_combiner,
    decoder_linear_map,
    cosine_logit_scale,
    sensor_variable_loadings,
    sensor_gridpoint,
    sensor_domain_index,
    sensor_channel_list,
    sensor_reading,
    sensor_noise_deviation,
):
    members, rows, cols, feats = starting_ensemble.shape
    full_embed, entire_triplet_product, full_out, full_head = (
        lax.all_gather(patch_lifting, "mem", axis=0, tiled=True),
        lax.all_gather(query_keyvalue_lift, "mem", axis=1, tiled=True),
        lax.all_gather(output_combiner, "mem", axis=1, tiled=True),
        lax.all_gather(decoder_linear_map, "mem", axis=1, tiled=True),
    )
    attention_span = full_embed.shape[1]
    hidden = jnp.dot(
        starting_ensemble.reshape(-1, feats), full_embed, preferred_element_type=jnp.float32
    )
    hidden = hidden.astype(jnp.bfloat16).reshape(members, rows, cols, attention_span)
    normed = layer_norm(hidden).astype(jnp.bfloat16)
    half = PANE_SIDE // 2
    incoming_rows = passed_along(normed[:, :, :half], "tile", -1)
    padded_sequence = jnp.concatenate([normed[:, :, half:], incoming_rows], axis=2)
    mixed_outcome_padded = pane_cosine_mixer(
        padded_sequence, entire_triplet_product, cosine_logit_scale
    )
    returned = passed_along(mixed_outcome_padded[:, :, cols - half :], "tile", 1)
    mixed_outcome = jnp.concatenate([returned, mixed_outcome_padded[:, :, : cols - half]], axis=2)
    mixed = hidden.astype(jnp.float32) + jnp.dot(
        mixed_outcome.reshape(-1, attention_span), full_out, preferred_element_type=jnp.float32
    ).reshape(members, rows, cols, attention_span)
    embedded_patches = layer_norm(mixed).astype(jnp.bfloat16)
    tile_tokens = rows * cols
    moved = lax.all_to_all(
        embedded_patches.reshape(members, tile_tokens, attention_span),
        "mem",
        split_axis=1,
        concat_axis=0,
        tiled=True,
    )
    ensemble, regions = (moved.shape[0], moved.shape[1])
    posterior = local_analysis(
        moved,
        full_head,
        sensor_gridpoint.reshape(-1),
        sensor_domain_index.reshape(-1),
        sensor_channel_list.reshape(-1),
        sensor_reading.reshape(-1),
        sensor_noise_deviation.reshape(-1),
        sensor_variable_loadings,
    )
    produced = jnp.dot(
        posterior.reshape(-1, attention_span), full_head, preferred_element_type=jnp.float32
    )
    produced = produced.astype(jnp.bfloat16).reshape(ensemble, regions, feats)
    analysed = lax.all_to_all(produced, "mem", split_axis=0, concat_axis=1, tiled=True)
    return analysed.reshape(members, rows, cols, feats)


def iota(shape, dim):
    return lax.broadcasted_iota(jnp.int32, shape, dim)


def dot(left, right):
    return jnp.dot(left, right, preferred_element_type=jnp.float32)


def dot_nt(left, right):
    return lax.dot_general(
        left, right, (((1,), (1,)), ((), ())), preferred_element_type=jnp.float32
    )


def two_terms(values):
    high = values.astype(jnp.bfloat16)
    return high, (values - high.astype(jnp.float32)).astype(jnp.bfloat16)


def fine(left, right):
    left_high, left_low = two_terms(left)
    right_high, right_low = two_terms(right)
    left_terms = jnp.concatenate([left_high, left_low], axis=1)
    if right.shape[1] > 128:
        return dot(left_terms, jnp.concatenate([right_high, right_high], axis=0)) + dot(
            left_high, right_low
        )
    both = dot(
        left_terms,
        jnp.concatenate(
            [
                jnp.concatenate([right_high, right_low], axis=1),
                jnp.concatenate([right_high, jnp.zeros_like(right_low)], axis=1),
            ],
            axis=0,
        ),
    )
    return both[:, : right.shape[1]] + both[:, right.shape[1] :]


def fine_nt(left, right):
    left_high, left_low = two_terms(left)
    right_high, right_low = two_terms(right)
    return (
        dot_nt(left_high, right_high) + dot_nt(left_low, right_high) + dot_nt(left_high, right_low)
    )


def one_hot(mask):
    return jnp.where(mask, 1.0, 0.0).astype(jnp.bfloat16)


def picked(rows, source):
    return one_hot(source == iota((rows, rows), 1))


def forecast_and_analyse(
    heads,
    x_hbm,
    embed_hbm,
    qkv_hbm,
    comb_hbm,
    dec_hbm,
    scale_hbm,
    load_hbm,
    grid_hbm,
    dom_hbm,
    chan_hbm,
    read_hbm,
    noise_hbm,
    out_ref,
    x_ref,
    embed_ref,
    dec_ref,
    scale_ref,
    load_ref,
    grid_ref,
    dom_ref,
    chan_ref,
    read_ref,
    noise_ref,
    g_embed,
    g_qkv,
    g_comb,
    g_dec,
    x_pad,
    to_west,
    window,
    qkv_buf,
    ctx,
    from_west,
    lat_send,
    lat_recv,
    pos_send,
    pos_recv,
    w_send,
    w_recv,
    t_send,
    t_recv,
    a_send,
    a_recv,
    l_sem,
):
    bf16, f32 = jnp.bfloat16, jnp.float32
    me = lax.axis_index("mem")
    tile = lax.axis_index("tile")
    tiles = lax.axis_size("tile")
    n = lax.axis_size("mem")
    core = me % 2
    along_x = (me // 2) % 2
    along_y = me // 4
    to_sib = 1 - 2 * core
    sib = me + to_sib
    x_nb = me + 2 - 4 * along_x
    y_nb = me + 4 - 8 * along_y
    diag = x_nb + 4 - 8 * along_y
    odd = tile % 2
    partner = tile + 1 - 2 * odd
    west = (tile + tiles - 1) % tiles
    east = (tile + 1) % tiles

    tokens, span = window.shape
    half = tokens // 2
    feats = x_ref.shape[1]
    piece = feats // n
    padded = g_embed.shape[0] // n
    width = padded * n
    count = grid_ref.shape[2]
    variables = load_ref.shape[1]

    def own_rows(held):
        rows = held.shape[0] // n
        return held.at[pl.ds(pl.multiple_of(me * rows, 16), rows)]

    local = [
        pltpu.make_async_copy(source, target, l_sem.at[i])
        for i, (source, target) in enumerate(
            (
                (embed_hbm, embed_ref),
                (qkv_hbm, own_rows(g_qkv)),
                (x_hbm, x_ref),
                (comb_hbm, own_rows(g_comb)),
                (dec_hbm, dec_ref),
                (load_hbm, load_ref),
                (grid_hbm, grid_ref),
                (chan_hbm, chan_ref),
                (dom_hbm, dom_ref),
                (read_hbm, read_ref),
                (noise_hbm, noise_ref),
                (scale_hbm, scale_ref),
            )
        )
    ]
    for fetched in local:
        fetched.start()

    barrier = pltpu.get_barrier_semaphore()
    for step in range(1, n):
        pl.semaphore_signal(
            barrier, inc=1, device_id=((me + step) % n, tile), device_id_type=MESH
        )
    for other in (west, east):
        pl.semaphore_signal(barrier, inc=1, device_id=(me, other), device_id_type=MESH)

    gathered = (g_embed, g_qkv, g_comb, g_dec)
    sends = []

    def copy(w, kind, owner, first, rows, target):
        held = gathered[w]
        block = held.shape[0] // n
        part = held.at[pl.ds(pl.multiple_of(owner * block + first, 16), rows)]
        return pltpu.make_async_remote_copy(
            src_ref=part,
            dst_ref=part,
            send_sem=w_send.at[w * KINDS + kind],
            recv_sem=w_recv.at[w * KINDS + kind],
            device_id=target,
            device_id_type=MESH,
        )

    here = {
        "sib": (sib, tile),
        "x": (x_nb, tile),
        "y": (y_nb, tile),
        "z": (me, partner),
    }

    def send(w, kind, owner, first, rows, way):
        sent = copy(w, kind, owner, first, rows, here[way])
        sent.start()
        sends.append(sent)

    def arrived(w, kind, owner, first, rows):
        copy(w, kind, owner, first, rows, here["sib"]).wait_recv()

    def third(w):
        return gathered[w].shape[0] // n // 3

    def own_first(w):
        t = third(w)
        send(w, 1, me, 2 * odd * t, t, "x")
        send(w, 2, me, 2 * odd * t, t, "y")

    def own_second(w):
        t = third(w)
        send(w, 15, me, t, t, "x")
        send(w, 16, me, t, t, "y")
        send(w, 0, me, 0, 3 * t, "sib")

    def pass_first(w):
        t = third(w)
        arrived(w, 1, x_nb, 2 * odd * t, t)
        send(w, 5, x_nb, 2 * odd * t, t, "y")
        send(w, 9, x_nb, 2 * odd * t, t, "z")
        arrived(w, 2, y_nb, 2 * odd * t, t)
        send(w, 10, y_nb, 2 * odd * t, t, "z")

    def pass_second(w):
        t = third(w)
        arrived(w, 16, y_nb, t, t)
        send(w, 6, y_nb, t, t, "x")
        send(w, 4, y_nb, odd * t, 2 * t, "sib")
        arrived(w, 15, x_nb, t, t)
        send(w, 3, x_nb, odd * t, 2 * t, "sib")

    def pass_diagonal(w):
        t = third(w)
        arrived(w, 5, diag, 2 * odd * t, t)
        send(w, 11, diag, 2 * odd * t, t, "z")
        send(w, 7, diag, 2 * odd * t, t, "sib")
        arrived(w, 6, diag, t, t)
        send(w, 8, diag, t, t, "sib")

    def pass_partner(w):
        t = third(w)
        for kind, owner in ((9, x_nb), (10, y_nb), (11, diag)):
            arrived(w, kind, owner, 2 * (1 - odd) * t, t)
            send(w, kind + 3, owner, 2 * (1 - odd) * t, t, "sib")

    def complete(w):
        t = third(w)
        arrived(w, 0, sib, 0, 3 * t)
        arrived(w, 3, x_nb + to_sib, odd * t, 2 * t)
        arrived(w, 4, y_nb + to_sib, odd * t, 2 * t)
        arrived(w, 7, diag + to_sib, 2 * odd * t, t)
        arrived(w, 8, diag + to_sib, t, t)
        for kind, owner in ((12, x_nb), (13, y_nb), (14, diag)):
            arrived(w, kind, owner + to_sib, 2 * (1 - odd) * t, t)

    def own_whole(w):
        rows = gathered[w].shape[0] // n
        send(w, 1, me, 0, rows, "x")
        send(w, 2, me, 0, rows, "y")
        send(w, 0, me, 0, rows, "sib")

    def pass_whole(w):
        rows = gathered[w].shape[0] // n
        upper = rows // 32 * 16
        arrived(w, 1, x_nb, 0, rows)
        send(w, 5, x_nb, 0, upper, "y")
        send(w, 3, x_nb, 0, rows, "sib")
        arrived(w, 2, y_nb, 0, rows)
        send(w, 6, y_nb, upper, rows - upper, "x")
        send(w, 4, y_nb, 0, rows, "sib")

    def pass_corner(w):
        rows = gathered[w].shape[0] // n
        upper = rows // 32 * 16
        arrived(w, 5, diag, 0, upper)
        arrived(w, 6, diag, upper, rows - upper)
        send(w, 7, diag, 0, rows, "sib")

    def complete_whole(w):
        rows = gathered[w].shape[0] // n
        for kind, owner in ((0, me), (3, x_nb), (4, y_nb), (7, diag)):
            arrived(w, kind, owner + to_sib, 0, rows)

    def keep_own(w, ref):
        block = gathered[w].shape[0] // n
        rows = ref.shape[0] // 16 * 16
        gathered[w][pl.ds(pl.multiple_of(me * block, 16), rows), :] = ref[:rows, :]
        if rows < block:
            left = ref.shape[0] - rows
            mask = one_hot(iota((block - rows, left), 0) == iota((block - rows, left), 1))
            gathered[w][pl.ds(pl.multiple_of(me * block + rows, 16), block - rows), :] = dot(
                mask, ref[rows:, :]
            ).astype(bf16)

    EMBED, QKV, COMB, DEC = 0, 1, 2, 3

    local[0].wait()
    keep_own(EMBED, embed_ref)
    pl.semaphore_wait(barrier, n + 1)
    own_first(EMBED)
    own_second(EMBED)
    for fetched in local[1:]:
        fetched.wait()

    row = iota((tokens, tokens), 0)
    by_half = picked(
        tokens,
        ((row >> 5) & 1) * 64 + ((row >> 2) & 7) * 8 + (row >> 6) * 4 + (row & 3),
    )
    x_rows = dot(by_half, x_ref[...]).astype(bf16)
    x_pad[...] = jnp.zeros(x_pad.shape, bf16)
    for d in range(n):
        x_pad[:, padded * d : padded * d + piece] = x_rows[:, piece * d : piece * (d + 1)]

    pass_first(EMBED)
    pass_second(EMBED)
    own_first(QKV)
    own_second(QKV)
    keep_own(DEC, dec_ref)
    within = iota((n, padded, variables), 1)
    within = within - jnp.where(within >= variables, variables, 0)
    pick_variable = one_hot(within == iota((n, padded, variables), 2)).reshape(width, variables)
    channels = load_ref.shape[0]
    loads = dot_nt(pick_variable, load_ref[...]).astype(bf16)
    chan_hot = one_hot(jnp.broadcast_to(chan_ref[0], (channels, count)) == iota((channels, count), 0))
    mapping = dot(loads, chan_hot)
    grid_point = grid_ref[0]
    points = feats // variables
    token_row = grid_point >> 4
    point_row = grid_point & (points - 1)
    dom_row = dom_ref[0]
    slot = iota((n, padded, count), 0) * 2 + jnp.where(
        iota((n, padded, count), 1) >= variables, 1, 0
    )
    mapping = jnp.where(
        slot.reshape(width, count) == jnp.broadcast_to(point_row, (width, count)), mapping, 0.0
    ).astype(bf16)

    pass_diagonal(EMBED)
    pass_partner(EMBED)
    complete(EMBED)
    pass_first(QKV)

    hidden = dot(x_pad[...], g_embed[...]).astype(bf16)
    normed = layer_norm(hidden).astype(bf16)
    to_west[...] = normed[:half]
    window[half:, :] = normed[half:]

    def along_tile(index, source, target, way):
        return pltpu.make_async_remote_copy(
            src_ref=source,
            dst_ref=target,
            send_sem=t_send.at[index],
            recv_sem=t_recv.at[index],
            device_id=(me, way),
            device_id_type=MESH,
        )

    westward = along_tile(0, to_west, window.at[pl.ds(0, half)], west)
    westward.start()
    sends.append(westward)

    pass_second(QKV)
    own_whole(COMB)

    pass_diagonal(QKV)
    pass_whole(COMB)
    own_whole(DEC)
    pass_partner(QKV)
    complete(QKV)
    westward.wait_recv()
    qkv_buf[...] = dot_nt(window[...], g_qkv[...]).astype(bf16)
    pass_corner(COMB)

    side = span // heads
    pair = 2 * side
    one_head = iota((pair, pair), 0) // side == iota((pair, pair), 1) // side
    head_sum = one_hot(one_head)
    head_sums = jnp.concatenate([head_sum, head_sum], axis=0)
    lane = iota((tokens, pair), 1)
    first = jnp.where(lane < side, 1.0, 0.0).astype(bf16)
    second = jnp.where(lane < side, 0.0, 1.0).astype(bf16)
    share = jnp.concatenate([first, second], axis=0)
    key_of = iota((half, 2 * tokens), 1)
    same_member = ((iota((half, 2 * tokens), 0) >> 5) & 1) == ((key_of >> 5) & 1)

    def unit_pair(rows, start):
        values = qkv_buf[rows, start : start + pair].astype(f32)
        squares = jnp.concatenate(two_terms(values * values), axis=1)
        return (values * lax.rsqrt(dot(squares, head_sums) + normalizing_guard)).astype(bf16)

    def attend(rows, pairs):
        for p in pairs:
            start = pair * p
            query = unit_pair(rows, start)
            key = keys[p]
            scales = jnp.where(
                key_of < tokens,
                scale_ref[:, 2 * p : 2 * p + 1],
                scale_ref[:, 2 * p + 1 : 2 * p + 2],
            )
            weights = jnp.where(same_member, jnp.exp(dot_nt(query, key) * scales), 0.0).astype(bf16)
            value = qkv_buf[:, 2 * span + start : 2 * span + start + pair]
            value = jnp.concatenate([value * first, value * second], axis=0)
            total = dot(weights, jnp.concatenate([value, share], axis=1))
            ctx[rows, start : start + pair] = (total[:, :pair] / total[:, pair:]).astype(bf16)

    keys = []
    for p in range(heads // 2):
        key = unit_pair(slice(None), span + pair * p)
        keys.append(jnp.concatenate([key * first, key * second], axis=0))
    attend(slice(0, half), range(heads // 2))
    eastward = along_tile(1, ctx.at[pl.ds(0, half)], from_west, east)
    eastward.start()
    sends.append(eastward)
    pass_whole(DEC)
    attend(slice(half, tokens), range(heads // 2))
    complete_whole(COMB)
    pass_corner(DEC)
    by_region = picked(
        tokens,
        ((row >> 2) & 1) * 64 + ((row >> 3) & 1) * 32 + (row >> 4) * 4 + (row & 3),
    )
    eastward.wait_recv()
    context = jnp.concatenate([from_west[...], ctx[half:, :]], axis=0)
    mixed = hidden.astype(f32) + dot_nt(context, g_comb[...])
    latent = layer_norm(mixed).astype(bf16)
    lat_send[...] = dot(by_region, latent).astype(bf16)

    block = tokens // n

    def exchange(index, source, target):
        mine = pl.ds(pl.multiple_of(me * block, 16), block)
        for step in range(1, n):
            to = (me + step) % n
            sent = pltpu.make_async_remote_copy(
                src_ref=source.at[pl.ds(pl.multiple_of(to * block, 16), block)],
                dst_ref=target.at[mine],
                send_sem=a_send.at[index * n + step],
                recv_sem=a_recv.at[index * n + step],
                device_id=(to, tile),
                device_id_type=MESH,
            )
            sent.start()
            sends.append(sent)
        target[mine, :] = source[mine, :]

    def exchanged(index, source, target):
        for step in range(1, n):
            origin = (me + n - step) % n
            part = pl.ds(pl.multiple_of(origin * block, 16), block)
            pltpu.make_async_remote_copy(
                src_ref=source.at[part],
                dst_ref=target.at[part],
                send_sem=a_send.at[index * n + step],
                recv_sem=a_recv.at[index * n + step],
                device_id=(origin, tile),
                device_id_type=MESH,
            ).wait_recv()

    exchange(0, lat_send, lat_recv)
    complete_whole(DEC)
    regions = n
    members = tokens // regions
    region3 = iota((members, regions, count), 1)
    on_token = jnp.where(region3 == token_row[None], 1.0, 0.0)
    in_region = jnp.where(region3 == dom_row[None], 1.0, 0.0).reshape(tokens, count)
    distance = (token_row - dom_row).astype(f32)
    noise = noise_ref[0]
    obs_weight = jnp.exp(-0.5 * distance * distance) / (noise * noise)
    in_region_weight = in_region * obs_weight
    reading = read_ref[0]
    unit = jnp.where(row == iota((tokens, tokens), 1), 1.0, 0.0)
    same_region = (row & (regions - 1)) == (iota((tokens, tokens), 1) & (regions - 1))
    by_member = picked(tokens, ((row >> 3) & 7) * 16 + (row >> 6) * 8 + (row & 7))
    exchanged(0, lat_send, lat_recv)

    values = lat_recv[...]
    prior = dot_nt(values, g_dec[...]).astype(bf16)
    samples = dot(prior, mapping).reshape(members, regions, count)
    ens_obs = jnp.sum(samples * on_token, axis=1, keepdims=True)
    mean_obs = jnp.mean(ens_obs, axis=0, keepdims=True)
    pert = jnp.broadcast_to(ens_obs - mean_obs, samples.shape).reshape(tokens, count)
    innovation = reading - mean_obs[0]
    weighted = pert * in_region_weight
    pert = pert * in_region
    gram = fine_nt(weighted, pert)
    drive = fine_nt(jnp.broadcast_to(innovation, (tokens, count)), weighted)
    system = unit + gram * (1.0 / (members - 1.0))
    sums = jnp.sum(jnp.abs(system), axis=1, keepdims=True).reshape(members, regions, 1)
    bound = jnp.broadcast_to(
        jnp.max(sums, axis=0, keepdims=True), (members, regions, 1)
    ).reshape(tokens, 1)
    iterate = system / bound
    inverse_root = None
    for step in range(NS_ITERS):
        if step == 0:
            factor = 1.5 * unit - 0.5 * iterate
            inverse_root = factor
        else:
            factor = 1.5 * unit - 0.5 * fine(inverse_root, iterate)
            inverse_root = fine(factor, inverse_root)
        if step < NS_ITERS - 1:
            iterate = fine(iterate, factor)
    root = inverse_root * lax.rsqrt(bound)
    inner = fine(drive, root)
    mean_weight = fine(inner, root) * (1.0 / (members - 1.0))
    transform_back = jnp.where(same_region, root + mean_weight, 0.0)
    latents = values.astype(f32).reshape(members, regions, span)
    center = jnp.mean(latents, axis=0, keepdims=True)
    spread = (latents - center).reshape(tokens, span)
    posterior = jnp.broadcast_to(center, latents.shape).reshape(tokens, span) + fine(
        transform_back, spread
    )
    pos_send[...] = posterior.astype(bf16)
    exchange(1, pos_send, pos_recv)
    for sent in sends[: 1 - n]:
        sent.wait_send()
    exchanged(1, pos_send, pos_recv)
    analysed = dot_nt(dot(by_member, pos_recv[...]).astype(bf16), g_dec[...])
    for d in range(n):
        out_ref[:, piece * d : piece * (d + 1)] = analysed[
            :, padded * d : padded * d + piece
        ].astype(bf16)
    for sent in sends[1 - n :]:
        sent.wait_send()


def per_device_fused(
    starting_ensemble,
    patch_lifting,
    query_keyvalue_lift,
    output_combiner,
    decoder_linear_map,
    cosine_logit_scale,
    sensor_variable_loadings,
    *sensors,
):
    n = lax.axis_size("mem")
    members, rows, cols, feats = starting_ensemble.shape
    tokens = members * rows * cols
    span = patch_lifting.shape[1]
    padded = -(-patch_lifting.shape[0] // 48) * 48
    vmem = pl.BlockSpec(memory_space=pltpu.VMEM)
    hbm = pl.BlockSpec(memory_space=pltpu.HBM)

    def held(*shape):
        return pltpu.VMEM(shape, jnp.bfloat16)

    out = pl.pallas_call(
        functools.partial(forecast_and_analyse, cosine_logit_scale.shape[0]),
        out_shape=jax.ShapeDtypeStruct((tokens, feats), jnp.bfloat16),
        in_specs=[hbm] * 12,
        out_specs=vmem,
        scratch_shapes=[
            held(tokens, feats),
            held(*patch_lifting.shape),
            held(decoder_linear_map.shape[1], span),
            pltpu.VMEM((1, cosine_logit_scale.shape[0]), jnp.float32),
            held(*sensor_variable_loadings.shape),
            *[pltpu.VMEM(sensor.shape, sensor.dtype) for sensor in sensors],
            held(padded * n, span),
            held(query_keyvalue_lift.shape[1] * n, span),
            held(output_combiner.shape[1] * n, span),
            held(padded * n, span),
            held(tokens, padded * n),
            held(tokens // 2, span),
            held(tokens, span),
            held(tokens, 3 * span),
            held(tokens, span),
            held(tokens // 2, span),
            held(tokens, span),
            held(tokens, span),
            held(tokens, span),
            held(tokens, span),
            pltpu.SemaphoreType.DMA((4 * KINDS,)),
            pltpu.SemaphoreType.DMA((4 * KINDS,)),
            pltpu.SemaphoreType.DMA((2,)),
            pltpu.SemaphoreType.DMA((2,)),
            pltpu.SemaphoreType.DMA((2 * n,)),
            pltpu.SemaphoreType.DMA((2 * n,)),
            pltpu.SemaphoreType.DMA((12,)),
        ],
        compiler_params=pltpu.CompilerParams(
            collective_id=0, has_side_effects=True, vmem_limit_bytes=63 * 1024 * 1024
        ),
        cost_estimate=pl.CostEstimate(
            flops=2 * tokens * span * (3 * feats + 4 * span),
            bytes_accessed=16 * 1024 * 1024,
            transcendentals=0,
        ),
    )(
        starting_ensemble.reshape(tokens, feats),
        patch_lifting,
        query_keyvalue_lift.T,
        output_combiner.T,
        decoder_linear_map.T,
        cosine_logit_scale.reshape(1, -1),
        sensor_variable_loadings,
        *sensors,
    )
    return out.reshape(members, rows, cols, feats)


def fits_fused(mesh, starting_ensemble, patch_lifting, query_keyvalue_lift, output_combiner, loads):
    n, tiles = mesh.shape["mem"], mesh.shape["tile"]
    members, rows, cols, feats = starting_ensemble.shape
    return (
        n == 8
        and tiles % 2 == 0
        and tiles > 2
        and (members // n, rows, cols // tiles) == (2, 8, 8)
        and feats == 16 * loads.shape[1]
        and query_keyvalue_lift.shape[1] % (48 * n) == 0
        and output_combiner.shape[1] % (48 * n) == 0
    )


def solution(mesh):
    def whole(*args):
        fused = fits_fused(mesh, args[0], args[1], args[2], args[3], args[6])
        return jax.shard_map(
            per_device_fused if fused else per_device,
            mesh=mesh,
            in_specs=(
                P("mem", None, "tile", None),
                P("mem", None),
                P(None, "mem"),
                P(None, "mem"),
                P(None, "mem"),
                P(),
                P(),
                P("mem", "tile", None),
                P("mem", "tile", None),
                P("mem", "tile", None),
                P("mem", "tile", None),
                P("mem", "tile", None),
            ),
            out_specs=P("mem", None, "tile", None),
            check_vma=False,
        )(*args)

    return whole
```

```python
import functools

import jax
import jax.numpy as jnp
from jax import lax
from jax.experimental import pallas as pl
from jax.experimental.pallas import tpu as pltpu
from jax.sharding import PartitionSpec as P

PANE_SIDE = 8
NS_ITERS = 5
KINDS = 17
MESH = pl.DeviceIdType.MESH


eps_norm = 1e-05
normalizing_guard = 1e-06


def passed_along(value, axis, by):
    devices = lax.axis_size(axis)
    return lax.ppermute(value, axis, [(i, (i + by) % devices) for i in range(devices)])


def layer_norm(values):
    values = values.astype(jnp.float32)
    center = values - jnp.mean(values, axis=-1, keepdims=True)
    spread = jnp.mean(center * center, axis=-1, keepdims=True)
    return center * lax.rsqrt(spread + eps_norm)


def unit_rows(values):
    values = values.astype(jnp.float32)
    return (
        values * lax.rsqrt(jnp.sum(values * values, axis=-1, keepdims=True) + normalizing_guard)
    ).astype(jnp.bfloat16)


def pane_cosine_mixer(padded_part, query_keyvalue_lift, cosine_logit_scale):
    members, rows, cols, attention_span = padded_part.shape
    focus_groups = cosine_logit_scale.shape[0]
    head_dim = attention_span // focus_groups
    qkv = jnp.dot(
        padded_part.reshape(-1, attention_span),
        query_keyvalue_lift,
        preferred_element_type=jnp.float32,
    ).astype(jnp.bfloat16)
    qkv = qkv.reshape(
        members, rows // PANE_SIDE, PANE_SIDE, cols // PANE_SIDE, PANE_SIDE, 3 * attention_span
    )
    qkv = qkv.transpose(0, 1, 3, 2, 4, 5).reshape(
        -1, PANE_SIDE * PANE_SIDE, 3, focus_groups, head_dim
    )
    query = unit_rows(qkv[:, :, 0])
    key_rows = unit_rows(qkv[:, :, 1])
    value_rows = qkv[:, :, 2]
    affinity_logits = jnp.einsum(
        "bihd,bjhd->bhij", query, key_rows, preferred_element_type=jnp.float32
    )
    affinity_logits = affinity_logits * cosine_logit_scale[None, :, None, None]
    weights = jnp.exp(affinity_logits)
    probs = (weights / jnp.sum(weights, axis=-1, keepdims=True)).astype(jnp.bfloat16)
    mixed_outcome = jnp.einsum(
        "bhij,bjhd->bihd", probs, value_rows, preferred_element_type=jnp.float32
    )
    mixed_outcome = mixed_outcome.astype(jnp.bfloat16).reshape(
        members, rows // PANE_SIDE, cols // PANE_SIDE, PANE_SIDE, PANE_SIDE, attention_span
    )
    return mixed_outcome.transpose(0, 1, 3, 2, 4, 5).reshape(members, rows, cols, attention_span)


def batched(left, right):
    return jnp.einsum("rij,rjk->rik", left, right, precision=lax.Precision.HIGHEST)


def local_analysis(
    embedded_patches,
    decoder_linear_map,
    sensor_gridpoint,
    sensor_domain_index,
    sensor_channel_list,
    sensor_reading,
    sensor_noise_deviation,
    sensor_variable_loadings,
):
    members, regions, attention_span = embedded_patches.shape
    feats = decoder_linear_map.shape[1]
    channels, variables = sensor_variable_loadings.shape
    points = feats // variables
    count = sensor_gridpoint.shape[0]
    prior_member_grids = jnp.dot(
        embedded_patches.reshape(-1, attention_span),
        decoder_linear_map,
        preferred_element_type=jnp.float32,
    ).astype(jnp.bfloat16)
    token = sensor_gridpoint // points
    point = sensor_gridpoint - token * points
    pick_point = (point[:, None] == jnp.arange(points, dtype=jnp.int32)[None, :]).astype(
        jnp.float32
    )
    pick_chan = (
        sensor_channel_list[:, None] == jnp.arange(channels, dtype=jnp.int32)[None, :]
    ).astype(jnp.float32)
    rows_h = jnp.dot(
        pick_chan, sensor_variable_loadings.astype(jnp.float32), precision=lax.Precision.HIGHEST
    )
    measurement_mapping = (
        (pick_point[:, :, None] * rows_h[:, None, :]).reshape(count, feats).astype(jnp.bfloat16)
    )
    mapped_samples = lax.dot_general(
        prior_member_grids,
        measurement_mapping,
        (((1,), (1,)), ((), ())),
        preferred_element_type=jnp.float32,
    )
    mapped_samples = mapped_samples.reshape(members, regions, count)
    pick_token = (token[None, :] == jnp.arange(regions, dtype=jnp.int32)[:, None]).astype(
        jnp.float32
    )
    ens_obs = jnp.sum(mapped_samples * pick_token[None], axis=1)
    mean_obs = jnp.mean(ens_obs, axis=0)
    pert_obs = ens_obs - mean_obs[None, :]
    innovation = sensor_reading - mean_obs
    distance = (token - sensor_domain_index).astype(jnp.float32)
    obs_weight = jnp.exp(-0.5 * distance * distance) / (
        sensor_noise_deviation * sensor_noise_deviation
    )
    pick_region = (
        sensor_domain_index[:, None] == jnp.arange(regions, dtype=jnp.int32)[None, :]
    ).astype(jnp.float32)
    weighted = pert_obs * obs_weight[None, :]
    gram = jnp.einsum(
        "kj,jr,lj->rkl", weighted, pick_region, pert_obs, precision=lax.Precision.HIGHEST
    )
    drive = jnp.einsum(
        "kj,jr,j->rk", weighted, pick_region, innovation, precision=lax.Precision.HIGHEST
    )
    eye = jnp.eye(members, dtype=jnp.float32)
    system = eye[None] + gram / (members - 1.0)
    bound = jnp.max(jnp.sum(jnp.abs(system), axis=2), axis=1)
    iterate = system / bound[:, None, None]
    inverse_root = jnp.broadcast_to(eye, system.shape)
    for step in range(NS_ITERS):
        factor = 1.5 * eye[None] - 0.5 * batched(inverse_root, iterate)
        iterate = batched(iterate, factor)
        inverse_root = batched(factor, inverse_root)
    root = inverse_root * lax.rsqrt(bound)[:, None, None]
    inner = jnp.einsum("rkl,rl->rk", root, drive, precision=lax.Precision.HIGHEST)
    mean_weight = jnp.einsum("rkl,rl->rk", root, inner, precision=lax.Precision.HIGHEST) / (
        members - 1.0
    )
    transform_matrix = root + mean_weight[:, :, None]
    values = embedded_patches.astype(jnp.float32)
    center = jnp.mean(values, axis=0)
    spread = values - center[None]
    posterior = center[None] + jnp.einsum(
        "ktf,tkm->mtf", spread, transform_matrix, precision=lax.Precision.HIGHEST
    )
    return posterior.astype(jnp.bfloat16)


def per_device(
    starting_ensemble,
    patch_lifting,
    query_keyvalue_lift,
    output_combiner,
    decoder_linear_map,
    cosine_logit_scale,
    sensor_variable_loadings,
    sensor_gridpoint,
    sensor_domain_index,
    sensor_channel_list,
    sensor_reading,
    sensor_noise_deviation,
):
    members, rows, cols, feats = starting_ensemble.shape
    full_embed, entire_triplet_product, full_out, full_head = (
        lax.all_gather(patch_lifting, "mem", axis=0, tiled=True),
        lax.all_gather(query_keyvalue_lift, "mem", axis=1, tiled=True),
        lax.all_gather(output_combiner, "mem", axis=1, tiled=True),
        lax.all_gather(decoder_linear_map, "mem", axis=1, tiled=True),
    )
    attention_span = full_embed.shape[1]
    hidden = jnp.dot(
        starting_ensemble.reshape(-1, feats), full_embed, preferred_element_type=jnp.float32
    )
    hidden = hidden.astype(jnp.bfloat16).reshape(members, rows, cols, attention_span)
    normed = layer_norm(hidden).astype(jnp.bfloat16)
    half = PANE_SIDE // 2
    incoming_rows = passed_along(normed[:, :, :half], "tile", -1)
    padded_sequence = jnp.concatenate([normed[:, :, half:], incoming_rows], axis=2)
    mixed_outcome_padded = pane_cosine_mixer(
        padded_sequence, entire_triplet_product, cosine_logit_scale
    )
    returned = passed_along(mixed_outcome_padded[:, :, cols - half :], "tile", 1)
    mixed_outcome = jnp.concatenate([returned, mixed_outcome_padded[:, :, : cols - half]], axis=2)
    mixed = hidden.astype(jnp.float32) + jnp.dot(
        mixed_outcome.reshape(-1, attention_span), full_out, preferred_element_type=jnp.float32
    ).reshape(members, rows, cols, attention_span)
    embedded_patches = layer_norm(mixed).astype(jnp.bfloat16)
    tile_tokens = rows * cols
    moved = lax.all_to_all(
        embedded_patches.reshape(members, tile_tokens, attention_span),
        "mem",
        split_axis=1,
        concat_axis=0,
        tiled=True,
    )
    ensemble, regions = (moved.shape[0], moved.shape[1])
    posterior = local_analysis(
        moved,
        full_head,
        sensor_gridpoint.reshape(-1),
        sensor_domain_index.reshape(-1),
        sensor_channel_list.reshape(-1),
        sensor_reading.reshape(-1),
        sensor_noise_deviation.reshape(-1),
        sensor_variable_loadings,
    )
    produced = jnp.dot(
        posterior.reshape(-1, attention_span), full_head, preferred_element_type=jnp.float32
    )
    produced = produced.astype(jnp.bfloat16).reshape(ensemble, regions, feats)
    analysed = lax.all_to_all(produced, "mem", split_axis=0, concat_axis=1, tiled=True)
    return analysed.reshape(members, rows, cols, feats)


def iota(shape, dim):
    return lax.broadcasted_iota(jnp.int32, shape, dim)


def dot(left, right):
    return jnp.dot(left, right, preferred_element_type=jnp.float32)


def dot_nt(left, right):
    return lax.dot_general(
        left, right, (((1,), (1,)), ((), ())), preferred_element_type=jnp.float32
    )


def two_terms(values):
    high = values.astype(jnp.bfloat16)
    return high, (values - high.astype(jnp.float32)).astype(jnp.bfloat16)


def fine(left, right):
    left_high, left_low = two_terms(left)
    right_high, right_low = two_terms(right)
    left_terms = jnp.concatenate([left_high, left_low], axis=1)
    if right.shape[1] > 128:
        return dot(left_terms, jnp.concatenate([right_high, right_high], axis=0)) + dot(
            left_high, right_low
        )
    both = dot(
        left_terms,
        jnp.concatenate(
            [
                jnp.concatenate([right_high, right_low], axis=1),
                jnp.concatenate([right_high, jnp.zeros_like(right_low)], axis=1),
            ],
            axis=0,
        ),
    )
    return both[:, : right.shape[1]] + both[:, right.shape[1] :]


def fine_nt(left, right):
    left_high, left_low = two_terms(left)
    right_high, right_low = two_terms(right)
    return (
        dot_nt(left_high, right_high) + dot_nt(left_low, right_high) + dot_nt(left_high, right_low)
    )


def one_hot(mask):
    return jnp.where(mask, 1.0, 0.0).astype(jnp.bfloat16)


def picked(rows, source):
    return one_hot(source == iota((rows, rows), 1))


def forecast_and_analyse(
    heads,
    x_hbm,
    embed_hbm,
    qkv_hbm,
    comb_hbm,
    dec_hbm,
    scale_hbm,
    load_hbm,
    grid_hbm,
    dom_hbm,
    chan_hbm,
    read_hbm,
    noise_hbm,
    out_ref,
    x_ref,
    embed_ref,
    dec_ref,
    scale_ref,
    load_ref,
    grid_ref,
    dom_ref,
    chan_ref,
    read_ref,
    noise_ref,
    g_embed,
    g_qkv,
    g_comb,
    g_dec,
    x_pad,
    to_west,
    window,
    qkv_buf,
    ctx,
    from_west,
    lat_send,
    lat_recv,
    pos_send,
    pos_recv,
    w_send,
    w_recv,
    t_send,
    t_recv,
    a_send,
    a_recv,
    l_sem,
):
    bf16, f32 = jnp.bfloat16, jnp.float32
    me = lax.axis_index("mem")
    tile = lax.axis_index("tile")
    tiles = lax.axis_size("tile")
    n = lax.axis_size("mem")
    core = me % 2
    along_x = (me // 2) % 2
    along_y = me // 4
    to_sib = 1 - 2 * core
    sib = me + to_sib
    x_nb = me + 2 - 4 * along_x
    y_nb = me + 4 - 8 * along_y
    diag = x_nb + 4 - 8 * along_y
    odd = tile % 2
    partner = tile + 1 - 2 * odd
    west = (tile + tiles - 1) % tiles
    east = (tile + 1) % tiles

    tokens, span = window.shape
    half = tokens // 2
    feats = x_ref.shape[1]
    piece = feats // n
    padded = g_embed.shape[0] // n
    width = padded * n
    count = grid_ref.shape[2]
    variables = load_ref.shape[1]

    def own_rows(held):
        rows = held.shape[0] // n
        return held.at[pl.ds(pl.multiple_of(me * rows, 16), rows)]

    local = [
        pltpu.make_async_copy(source, target, l_sem.at[i])
        for i, (source, target) in enumerate(
            (
                (embed_hbm, embed_ref),
                (qkv_hbm, own_rows(g_qkv)),
                (x_hbm, x_ref),
                (comb_hbm, own_rows(g_comb)),
                (dec_hbm, dec_ref),
                (load_hbm, load_ref),
                (grid_hbm, grid_ref),
                (chan_hbm, chan_ref),
                (dom_hbm, dom_ref),
                (read_hbm, read_ref),
                (noise_hbm, noise_ref),
                (scale_hbm, scale_ref),
            )
        )
    ]
    for fetched in local:
        fetched.start()

    barrier = pltpu.get_barrier_semaphore()
    for step in range(1, n):
        pl.semaphore_signal(
            barrier, inc=1, device_id=((me + step) % n, tile), device_id_type=MESH
        )
    for other in (west, east):
        pl.semaphore_signal(barrier, inc=1, device_id=(me, other), device_id_type=MESH)

    gathered = (g_embed, g_qkv, g_comb, g_dec)
    sends = []

    def copy(w, kind, owner, first, rows, target):
        held = gathered[w]
        block = held.shape[0] // n
        part = held.at[pl.ds(pl.multiple_of(owner * block + first, 16), rows)]
        return pltpu.make_async_remote_copy(
            src_ref=part,
            dst_ref=part,
            send_sem=w_send.at[w * KINDS + kind],
            recv_sem=w_recv.at[w * KINDS + kind],
            device_id=target,
            device_id_type=MESH,
        )

    here = {
        "sib": (sib, tile),
        "x": (x_nb, tile),
        "y": (y_nb, tile),
        "z": (me, partner),
    }

    def send(w, kind, owner, first, rows, way):
        sent = copy(w, kind, owner, first, rows, here[way])
        sent.start()
        sends.append(sent)

    def arrived(w, kind, owner, first, rows):
        copy(w, kind, owner, first, rows, here["sib"]).wait_recv()

    def third(w):
        return gathered[w].shape[0] // n // 3

    def own_first(w):
        t = third(w)
        send(w, 1, me, 2 * odd * t, t, "x")
        send(w, 2, me, 2 * odd * t, t, "y")

    def own_second(w):
        t = third(w)
        send(w, 15, me, t, t, "x")
        send(w, 16, me, t, t, "y")
        send(w, 0, me, 0, 3 * t, "sib")

    def pass_first(w):
        t = third(w)
        arrived(w, 1, x_nb, 2 * odd * t, t)
        send(w, 5, x_nb, 2 * odd * t, t, "y")
        send(w, 9, x_nb, 2 * odd * t, t, "z")
        arrived(w, 2, y_nb, 2 * odd * t, t)
        send(w, 10, y_nb, 2 * odd * t, t, "z")

    def pass_second(w):
        t = third(w)
        arrived(w, 16, y_nb, t, t)
        send(w, 6, y_nb, t, t, "x")
        send(w, 4, y_nb, odd * t, 2 * t, "sib")
        arrived(w, 15, x_nb, t, t)
        send(w, 3, x_nb, odd * t, 2 * t, "sib")

    def pass_diagonal(w):
        t = third(w)
        arrived(w, 5, diag, 2 * odd * t, t)
        send(w, 11, diag, 2 * odd * t, t, "z")
        send(w, 7, diag, 2 * odd * t, t, "sib")
        arrived(w, 6, diag, t, t)
        send(w, 8, diag, t, t, "sib")

    def pass_partner(w):
        t = third(w)
        for kind, owner in ((9, x_nb), (10, y_nb), (11, diag)):
            arrived(w, kind, owner, 2 * (1 - odd) * t, t)
            send(w, kind + 3, owner, 2 * (1 - odd) * t, t, "sib")

    def complete(w):
        t = third(w)
        arrived(w, 0, sib, 0, 3 * t)
        arrived(w, 3, x_nb + to_sib, odd * t, 2 * t)
        arrived(w, 4, y_nb + to_sib, odd * t, 2 * t)
        arrived(w, 7, diag + to_sib, 2 * odd * t, t)
        arrived(w, 8, diag + to_sib, t, t)
        for kind, owner in ((12, x_nb), (13, y_nb), (14, diag)):
            arrived(w, kind, owner + to_sib, 2 * (1 - odd) * t, t)

    def own_whole(w):
        rows = gathered[w].shape[0] // n
        send(w, 1, me, 0, rows, "x")
        send(w, 2, me, 0, rows, "y")
        send(w, 0, me, 0, rows, "sib")

    def pass_whole(w):
        rows = gathered[w].shape[0] // n
        upper = rows // 32 * 16
        arrived(w, 1, x_nb, 0, rows)
        send(w, 5, x_nb, 0, upper, "y")
        send(w, 3, x_nb, 0, rows, "sib")
        arrived(w, 2, y_nb, 0, rows)
        send(w, 6, y_nb, upper, rows - upper, "x")
        send(w, 4, y_nb, 0, rows, "sib")

    def pass_corner(w):
        rows = gathered[w].shape[0] // n
        upper = rows // 32 * 16
        arrived(w, 5, diag, 0, upper)
        arrived(w, 6, diag, upper, rows - upper)
        send(w, 7, diag, 0, rows, "sib")

    def complete_whole(w):
        rows = gathered[w].shape[0] // n
        for kind, owner in ((0, me), (3, x_nb), (4, y_nb), (7, diag)):
            arrived(w, kind, owner + to_sib, 0, rows)

    def keep_own(w, ref):
        block = gathered[w].shape[0] // n
        rows = ref.shape[0] // 16 * 16
        gathered[w][pl.ds(pl.multiple_of(me * block, 16), rows), :] = ref[:rows, :]
        if rows < block:
            left = ref.shape[0] - rows
            mask = one_hot(iota((block - rows, left), 0) == iota((block - rows, left), 1))
            gathered[w][pl.ds(pl.multiple_of(me * block + rows, 16), block - rows), :] = dot(
                mask, ref[rows:, :]
            ).astype(bf16)

    EMBED, QKV, COMB, DEC = 0, 1, 2, 3

    local[0].wait()
    keep_own(EMBED, embed_ref)
    pl.semaphore_wait(barrier, n + 1)
    own_whole(EMBED)
    local[1].wait()
    own_first(QKV)
    for fetched in local[2:]:
        fetched.wait()

    row = iota((tokens, tokens), 0)
    by_half = picked(
        tokens,
        ((row >> 5) & 1) * 64 + ((row >> 2) & 7) * 8 + (row >> 6) * 4 + (row & 3),
    )
    x_rows = dot(by_half, x_ref[...]).astype(bf16)
    x_pad[...] = jnp.zeros(x_pad.shape, bf16)
    for d in range(n):
        x_pad[:, padded * d : padded * d + piece] = x_rows[:, piece * d : piece * (d + 1)]

    pass_whole(EMBED)
    own_second(QKV)
    keep_own(DEC, dec_ref)
    within = iota((n, padded, variables), 1)
    within = within - jnp.where(within >= variables, variables, 0)
    pick_variable = one_hot(within == iota((n, padded, variables), 2)).reshape(width, variables)
    channels = load_ref.shape[0]
    loads = dot_nt(pick_variable, load_ref[...]).astype(bf16)
    chan_hot = one_hot(jnp.broadcast_to(chan_ref[0], (channels, count)) == iota((channels, count), 0))
    mapping = dot(loads, chan_hot)
    grid_point = grid_ref[0]
    points = feats // variables
    token_row = grid_point >> 4
    point_row = grid_point & (points - 1)
    dom_row = dom_ref[0]
    slot = iota((n, padded, count), 0) * 2 + jnp.where(
        iota((n, padded, count), 1) >= variables, 1, 0
    )
    mapping = jnp.where(
        slot.reshape(width, count) == jnp.broadcast_to(point_row, (width, count)), mapping, 0.0
    ).astype(bf16)

    pass_corner(EMBED)
    pass_first(QKV)
    own_whole(COMB)
    complete_whole(EMBED)

    hidden = dot(x_pad[...], g_embed[...]).astype(bf16)
    normed = layer_norm(hidden).astype(bf16)
    to_west[...] = normed[:half]
    window[half:, :] = normed[half:]

    def along_tile(index, source, target, way):
        return pltpu.make_async_remote_copy(
            src_ref=source,
            dst_ref=target,
            send_sem=t_send.at[index],
            recv_sem=t_recv.at[index],
            device_id=(me, way),
            device_id_type=MESH,
        )

    westward = along_tile(0, to_west, window.at[pl.ds(0, half)], west)
    westward.start()
    sends.append(westward)

    pass_second(QKV)

    pass_diagonal(QKV)
    own_whole(DEC)
    pass_partner(QKV)
    complete(QKV)
    westward.wait_recv()
    qkv_buf[...] = dot_nt(window[...], g_qkv[...]).astype(bf16)
    pass_whole(COMB)

    side = span // heads
    pair = 2 * side
    one_head = iota((pair, pair), 0) // side == iota((pair, pair), 1) // side
    head_sum = one_hot(one_head)
    head_sums = jnp.concatenate([head_sum, head_sum], axis=0)
    lane = iota((tokens, pair), 1)
    first = jnp.where(lane < side, 1.0, 0.0).astype(bf16)
    second = jnp.where(lane < side, 0.0, 1.0).astype(bf16)
    share = jnp.concatenate([first, second], axis=0)
    key_of = iota((half, 2 * tokens), 1)
    same_member = ((iota((half, 2 * tokens), 0) >> 5) & 1) == ((key_of >> 5) & 1)

    def unit_pair(rows, start):
        values = qkv_buf[rows, start : start + pair].astype(f32)
        squares = jnp.concatenate(two_terms(values * values), axis=1)
        return (values * lax.rsqrt(dot(squares, head_sums) + normalizing_guard)).astype(bf16)

    def attend(rows, pairs):
        for p in pairs:
            start = pair * p
            query = unit_pair(rows, start)
            key = keys[p]
            scales = jnp.where(
                key_of < tokens,
                scale_ref[:, 2 * p : 2 * p + 1],
                scale_ref[:, 2 * p + 1 : 2 * p + 2],
            )
            weights = jnp.where(same_member, jnp.exp(dot_nt(query, key) * scales), 0.0).astype(bf16)
            value = qkv_buf[:, 2 * span + start : 2 * span + start + pair]
            value = jnp.concatenate([value * first, value * second], axis=0)
            total = dot(weights, jnp.concatenate([value, share], axis=1))
            ctx[rows, start : start + pair] = (total[:, :pair] / total[:, pair:]).astype(bf16)

    keys = []
    for p in range(heads // 2):
        key = unit_pair(slice(None), span + pair * p)
        keys.append(jnp.concatenate([key * first, key * second], axis=0))
    attend(slice(0, half), range(heads // 2))
    eastward = along_tile(1, ctx.at[pl.ds(0, half)], from_west, east)
    eastward.start()
    sends.append(eastward)
    pass_corner(COMB)
    pass_whole(DEC)
    attend(slice(half, tokens), range(heads // 2))
    complete_whole(COMB)
    pass_corner(DEC)
    by_region = picked(
        tokens,
        ((row >> 2) & 1) * 64 + ((row >> 3) & 1) * 32 + (row >> 4) * 4 + (row & 3),
    )
    eastward.wait_recv()
    context = jnp.concatenate([from_west[...], ctx[half:, :]], axis=0)
    mixed = hidden.astype(f32) + dot_nt(context, g_comb[...])
    latent = layer_norm(mixed).astype(bf16)
    lat_send[...] = dot(by_region, latent).astype(bf16)

    block = tokens // n

    def exchange(index, source, target):
        mine = pl.ds(pl.multiple_of(me * block, 16), block)
        for step in range(1, n):
            to = (me + step) % n
            sent = pltpu.make_async_remote_copy(
                src_ref=source.at[pl.ds(pl.multiple_of(to * block, 16), block)],
                dst_ref=target.at[mine],
                send_sem=a_send.at[index * n + step],
                recv_sem=a_recv.at[index * n + step],
                device_id=(to, tile),
                device_id_type=MESH,
            )
            sent.start()
            sends.append(sent)
        target[mine, :] = source[mine, :]

    def exchanged(index, source, target):
        for step in range(1, n):
            origin = (me + n - step) % n
            part = pl.ds(pl.multiple_of(origin * block, 16), block)
            pltpu.make_async_remote_copy(
                src_ref=source.at[part],
                dst_ref=target.at[part],
                send_sem=a_send.at[index * n + step],
                recv_sem=a_recv.at[index * n + step],
                device_id=(origin, tile),
                device_id_type=MESH,
            ).wait_recv()

    exchange(0, lat_send, lat_recv)
    complete_whole(DEC)
    regions = n
    members = tokens // regions
    region3 = iota((members, regions, count), 1)
    on_token = jnp.where(region3 == token_row[None], 1.0, 0.0)
    in_region = jnp.where(region3 == dom_row[None], 1.0, 0.0).reshape(tokens, count)
    distance = (token_row - dom_row).astype(f32)
    noise = noise_ref[0]
    obs_weight = jnp.exp(-0.5 * distance * distance) / (noise * noise)
    in_region_weight = in_region * obs_weight
    reading = read_ref[0]
    unit = jnp.where(row == iota((tokens, tokens), 1), 1.0, 0.0)
    same_region = (row & (regions - 1)) == (iota((tokens, tokens), 1) & (regions - 1))
    by_member = picked(tokens, ((row >> 3) & 7) * 16 + (row >> 6) * 8 + (row & 7))
    exchanged(0, lat_send, lat_recv)

    values = lat_recv[...]
    prior = dot_nt(values, g_dec[...]).astype(bf16)
    samples = dot(prior, mapping).reshape(members, regions, count)
    ens_obs = jnp.sum(samples * on_token, axis=1, keepdims=True)
    mean_obs = jnp.mean(ens_obs, axis=0, keepdims=True)
    pert = jnp.broadcast_to(ens_obs - mean_obs, samples.shape).reshape(tokens, count)
    innovation = reading - mean_obs[0]
    weighted = pert * in_region_weight
    pert = pert * in_region
    gram = fine_nt(weighted, pert)
    drive = fine_nt(jnp.broadcast_to(innovation, (tokens, count)), weighted)
    system = unit + gram * (1.0 / (members - 1.0))
    sums = jnp.sum(jnp.abs(system), axis=1, keepdims=True).reshape(members, regions, 1)
    bound = jnp.broadcast_to(
        jnp.max(sums, axis=0, keepdims=True), (members, regions, 1)
    ).reshape(tokens, 1)
    iterate = system / bound
    inverse_root = None
    for step in range(NS_ITERS):
        if step == 0:
            factor = 1.5 * unit - 0.5 * iterate
            inverse_root = factor
        else:
            factor = 1.5 * unit - 0.5 * fine(inverse_root, iterate)
            inverse_root = fine(factor, inverse_root)
        if step < NS_ITERS - 1:
            iterate = fine(iterate, factor)
    root = inverse_root * lax.rsqrt(bound)
    inner = fine(drive, root)
    mean_weight = fine(inner, root) * (1.0 / (members - 1.0))
    transform_back = jnp.where(same_region, root + mean_weight, 0.0)
    latents = values.astype(f32).reshape(members, regions, span)
    center = jnp.mean(latents, axis=0, keepdims=True)
    spread = (latents - center).reshape(tokens, span)
    posterior = jnp.broadcast_to(center, latents.shape).reshape(tokens, span) + fine(
        transform_back, spread
    )
    pos_send[...] = posterior.astype(bf16)
    exchange(1, pos_send, pos_recv)
    for sent in sends[: 1 - n]:
        sent.wait_send()
    exchanged(1, pos_send, pos_recv)
    analysed = dot_nt(dot(by_member, pos_recv[...]).astype(bf16), g_dec[...])
    for d in range(n):
        out_ref[:, piece * d : piece * (d + 1)] = analysed[
            :, padded * d : padded * d + piece
        ].astype(bf16)
    for sent in sends[1 - n :]:
        sent.wait_send()


def per_device_fused(
    starting_ensemble,
    patch_lifting,
    query_keyvalue_lift,
    output_combiner,
    decoder_linear_map,
    cosine_logit_scale,
    sensor_variable_loadings,
    *sensors,
):
    n = lax.axis_size("mem")
    members, rows, cols, feats = starting_ensemble.shape
    tokens = members * rows * cols
    span = patch_lifting.shape[1]
    padded = -(-patch_lifting.shape[0] // 48) * 48
    vmem = pl.BlockSpec(memory_space=pltpu.VMEM)
    hbm = pl.BlockSpec(memory_space=pltpu.HBM)

    def held(*shape):
        return pltpu.VMEM(shape, jnp.bfloat16)

    out = pl.pallas_call(
        functools.partial(forecast_and_analyse, cosine_logit_scale.shape[0]),
        out_shape=jax.ShapeDtypeStruct((tokens, feats), jnp.bfloat16),
        in_specs=[hbm] * 12,
        out_specs=vmem,
        scratch_shapes=[
            held(tokens, feats),
            held(*patch_lifting.shape),
            held(decoder_linear_map.shape[1], span),
            pltpu.VMEM((1, cosine_logit_scale.shape[0]), jnp.float32),
            held(*sensor_variable_loadings.shape),
            *[pltpu.VMEM(sensor.shape, sensor.dtype) for sensor in sensors],
            held(padded * n, span),
            held(query_keyvalue_lift.shape[1] * n, span),
            held(output_combiner.shape[1] * n, span),
            held(padded * n, span),
            held(tokens, padded * n),
            held(tokens // 2, span),
            held(tokens, span),
            held(tokens, 3 * span),
            held(tokens, span),
            held(tokens // 2, span),
            held(tokens, span),
            held(tokens, span),
            held(tokens, span),
            held(tokens, span),
            pltpu.SemaphoreType.DMA((4 * KINDS,)),
            pltpu.SemaphoreType.DMA((4 * KINDS,)),
            pltpu.SemaphoreType.DMA((2,)),
            pltpu.SemaphoreType.DMA((2,)),
            pltpu.SemaphoreType.DMA((2 * n,)),
            pltpu.SemaphoreType.DMA((2 * n,)),
            pltpu.SemaphoreType.DMA((12,)),
        ],
        compiler_params=pltpu.CompilerParams(
            collective_id=0, has_side_effects=True, vmem_limit_bytes=63 * 1024 * 1024
        ),
        cost_estimate=pl.CostEstimate(
            flops=2 * tokens * span * (3 * feats + 4 * span),
            bytes_accessed=16 * 1024 * 1024,
            transcendentals=0,
        ),
    )(
        starting_ensemble.reshape(tokens, feats),
        patch_lifting,
        query_keyvalue_lift.T,
        output_combiner.T,
        decoder_linear_map.T,
        cosine_logit_scale.reshape(1, -1),
        sensor_variable_loadings,
        *sensors,
    )
    return out.reshape(members, rows, cols, feats)


def fits_fused(mesh, starting_ensemble, patch_lifting, query_keyvalue_lift, output_combiner, loads):
    n, tiles = mesh.shape["mem"], mesh.shape["tile"]
    members, rows, cols, feats = starting_ensemble.shape
    return (
        n == 8
        and tiles % 2 == 0
        and tiles > 2
        and (members // n, rows, cols // tiles) == (2, 8, 8)
        and feats == 16 * loads.shape[1]
        and query_keyvalue_lift.shape[1] % (48 * n) == 0
        and output_combiner.shape[1] % (48 * n) == 0
    )


def solution(mesh):
    def whole(*args):
        fused = fits_fused(mesh, args[0], args[1], args[2], args[3], args[6])
        return jax.shard_map(
            per_device_fused if fused else per_device,
            mesh=mesh,
            in_specs=(
                P("mem", None, "tile", None),
                P("mem", None),
                P(None, "mem"),
                P(None, "mem"),
                P(None, "mem"),
                P(),
                P(),
                P("mem", "tile", None),
                P("mem", "tile", None),
                P("mem", "tile", None),
                P("mem", "tile", None),
                P("mem", "tile", None),
            ),
            out_specs=P("mem", None, "tile", None),
            check_vma=False,
        )(*args)

    return whole
```

```python
import functools

import jax
import jax.numpy as jnp
from jax import lax
from jax.experimental import pallas as pl
from jax.experimental.pallas import tpu as pltpu
from jax.sharding import PartitionSpec as P

PANE_SIDE = 8
NS_ITERS = 5
KINDS = 17
MESH = pl.DeviceIdType.MESH


eps_norm = 1e-05
normalizing_guard = 1e-06


def passed_along(value, axis, by):
    devices = lax.axis_size(axis)
    return lax.ppermute(value, axis, [(i, (i + by) % devices) for i in range(devices)])


def layer_norm(values):
    values = values.astype(jnp.float32)
    center = values - jnp.mean(values, axis=-1, keepdims=True)
    spread = jnp.mean(center * center, axis=-1, keepdims=True)
    return center * lax.rsqrt(spread + eps_norm)


def unit_rows(values):
    values = values.astype(jnp.float32)
    return (
        values * lax.rsqrt(jnp.sum(values * values, axis=-1, keepdims=True) + normalizing_guard)
    ).astype(jnp.bfloat16)


def pane_cosine_mixer(padded_part, query_keyvalue_lift, cosine_logit_scale):
    members, rows, cols, attention_span = padded_part.shape
    focus_groups = cosine_logit_scale.shape[0]
    head_dim = attention_span // focus_groups
    qkv = jnp.dot(
        padded_part.reshape(-1, attention_span),
        query_keyvalue_lift,
        preferred_element_type=jnp.float32,
    ).astype(jnp.bfloat16)
    qkv = qkv.reshape(
        members, rows // PANE_SIDE, PANE_SIDE, cols // PANE_SIDE, PANE_SIDE, 3 * attention_span
    )
    qkv = qkv.transpose(0, 1, 3, 2, 4, 5).reshape(
        -1, PANE_SIDE * PANE_SIDE, 3, focus_groups, head_dim
    )
    query = unit_rows(qkv[:, :, 0])
    key_rows = unit_rows(qkv[:, :, 1])
    value_rows = qkv[:, :, 2]
    affinity_logits = jnp.einsum(
        "bihd,bjhd->bhij", query, key_rows, preferred_element_type=jnp.float32
    )
    affinity_logits = affinity_logits * cosine_logit_scale[None, :, None, None]
    weights = jnp.exp(affinity_logits)
    probs = (weights / jnp.sum(weights, axis=-1, keepdims=True)).astype(jnp.bfloat16)
    mixed_outcome = jnp.einsum(
        "bhij,bjhd->bihd", probs, value_rows, preferred_element_type=jnp.float32
    )
    mixed_outcome = mixed_outcome.astype(jnp.bfloat16).reshape(
        members, rows // PANE_SIDE, cols // PANE_SIDE, PANE_SIDE, PANE_SIDE, attention_span
    )
    return mixed_outcome.transpose(0, 1, 3, 2, 4, 5).reshape(members, rows, cols, attention_span)


def batched(left, right):
    return jnp.einsum("rij,rjk->rik", left, right, precision=lax.Precision.HIGHEST)


def local_analysis(
    embedded_patches,
    decoder_linear_map,
    sensor_gridpoint,
    sensor_domain_index,
    sensor_channel_list,
    sensor_reading,
    sensor_noise_deviation,
    sensor_variable_loadings,
):
    members, regions, attention_span = embedded_patches.shape
    feats = decoder_linear_map.shape[1]
    channels, variables = sensor_variable_loadings.shape
    points = feats // variables
    count = sensor_gridpoint.shape[0]
    prior_member_grids = jnp.dot(
        embedded_patches.reshape(-1, attention_span),
        decoder_linear_map,
        preferred_element_type=jnp.float32,
    ).astype(jnp.bfloat16)
    token = sensor_gridpoint // points
    point = sensor_gridpoint - token * points
    pick_point = (point[:, None] == jnp.arange(points, dtype=jnp.int32)[None, :]).astype(
        jnp.float32
    )
    pick_chan = (
        sensor_channel_list[:, None] == jnp.arange(channels, dtype=jnp.int32)[None, :]
    ).astype(jnp.float32)
    rows_h = jnp.dot(
        pick_chan, sensor_variable_loadings.astype(jnp.float32), precision=lax.Precision.HIGHEST
    )
    measurement_mapping = (
        (pick_point[:, :, None] * rows_h[:, None, :]).reshape(count, feats).astype(jnp.bfloat16)
    )
    mapped_samples = lax.dot_general(
        prior_member_grids,
        measurement_mapping,
        (((1,), (1,)), ((), ())),
        preferred_element_type=jnp.float32,
    )
    mapped_samples = mapped_samples.reshape(members, regions, count)
    pick_token = (token[None, :] == jnp.arange(regions, dtype=jnp.int32)[:, None]).astype(
        jnp.float32
    )
    ens_obs = jnp.sum(mapped_samples * pick_token[None], axis=1)
    mean_obs = jnp.mean(ens_obs, axis=0)
    pert_obs = ens_obs - mean_obs[None, :]
    innovation = sensor_reading - mean_obs
    distance = (token - sensor_domain_index).astype(jnp.float32)
    obs_weight = jnp.exp(-0.5 * distance * distance) / (
        sensor_noise_deviation * sensor_noise_deviation
    )
    pick_region = (
        sensor_domain_index[:, None] == jnp.arange(regions, dtype=jnp.int32)[None, :]
    ).astype(jnp.float32)
    weighted = pert_obs * obs_weight[None, :]
    gram = jnp.einsum(
        "kj,jr,lj->rkl", weighted, pick_region, pert_obs, precision=lax.Precision.HIGHEST
    )
    drive = jnp.einsum(
        "kj,jr,j->rk", weighted, pick_region, innovation, precision=lax.Precision.HIGHEST
    )
    eye = jnp.eye(members, dtype=jnp.float32)
    system = eye[None] + gram / (members - 1.0)
    bound = jnp.max(jnp.sum(jnp.abs(system), axis=2), axis=1)
    iterate = system / bound[:, None, None]
    inverse_root = jnp.broadcast_to(eye, system.shape)
    for step in range(NS_ITERS):
        factor = 1.5 * eye[None] - 0.5 * batched(inverse_root, iterate)
        iterate = batched(iterate, factor)
        inverse_root = batched(factor, inverse_root)
    root = inverse_root * lax.rsqrt(bound)[:, None, None]
    inner = jnp.einsum("rkl,rl->rk", root, drive, precision=lax.Precision.HIGHEST)
    mean_weight = jnp.einsum("rkl,rl->rk", root, inner, precision=lax.Precision.HIGHEST) / (
        members - 1.0
    )
    transform_matrix = root + mean_weight[:, :, None]
    values = embedded_patches.astype(jnp.float32)
    center = jnp.mean(values, axis=0)
    spread = values - center[None]
    posterior = center[None] + jnp.einsum(
        "ktf,tkm->mtf", spread, transform_matrix, precision=lax.Precision.HIGHEST
    )
    return posterior.astype(jnp.bfloat16)


def per_device(
    starting_ensemble,
    patch_lifting,
    query_keyvalue_lift,
    output_combiner,
    decoder_linear_map,
    cosine_logit_scale,
    sensor_variable_loadings,
    sensor_gridpoint,
    sensor_domain_index,
    sensor_channel_list,
    sensor_reading,
    sensor_noise_deviation,
):
    members, rows, cols, feats = starting_ensemble.shape
    full_embed, entire_triplet_product, full_out, full_head = (
        lax.all_gather(patch_lifting, "mem", axis=0, tiled=True),
        lax.all_gather(query_keyvalue_lift, "mem", axis=1, tiled=True),
        lax.all_gather(output_combiner, "mem", axis=1, tiled=True),
        lax.all_gather(decoder_linear_map, "mem", axis=1, tiled=True),
    )
    attention_span = full_embed.shape[1]
    hidden = jnp.dot(
        starting_ensemble.reshape(-1, feats), full_embed, preferred_element_type=jnp.float32
    )
    hidden = hidden.astype(jnp.bfloat16).reshape(members, rows, cols, attention_span)
    normed = layer_norm(hidden).astype(jnp.bfloat16)
    half = PANE_SIDE // 2
    incoming_rows = passed_along(normed[:, :, :half], "tile", -1)
    padded_sequence = jnp.concatenate([normed[:, :, half:], incoming_rows], axis=2)
    mixed_outcome_padded = pane_cosine_mixer(
        padded_sequence, entire_triplet_product, cosine_logit_scale
    )
    returned = passed_along(mixed_outcome_padded[:, :, cols - half :], "tile", 1)
    mixed_outcome = jnp.concatenate([returned, mixed_outcome_padded[:, :, : cols - half]], axis=2)
    mixed = hidden.astype(jnp.float32) + jnp.dot(
        mixed_outcome.reshape(-1, attention_span), full_out, preferred_element_type=jnp.float32
    ).reshape(members, rows, cols, attention_span)
    embedded_patches = layer_norm(mixed).astype(jnp.bfloat16)
    tile_tokens = rows * cols
    moved = lax.all_to_all(
        embedded_patches.reshape(members, tile_tokens, attention_span),
        "mem",
        split_axis=1,
        concat_axis=0,
        tiled=True,
    )
    ensemble, regions = (moved.shape[0], moved.shape[1])
    posterior = local_analysis(
        moved,
        full_head,
        sensor_gridpoint.reshape(-1),
        sensor_domain_index.reshape(-1),
        sensor_channel_list.reshape(-1),
        sensor_reading.reshape(-1),
        sensor_noise_deviation.reshape(-1),
        sensor_variable_loadings,
    )
    produced = jnp.dot(
        posterior.reshape(-1, attention_span), full_head, preferred_element_type=jnp.float32
    )
    produced = produced.astype(jnp.bfloat16).reshape(ensemble, regions, feats)
    analysed = lax.all_to_all(produced, "mem", split_axis=0, concat_axis=1, tiled=True)
    return analysed.reshape(members, rows, cols, feats)


def iota(shape, dim):
    return lax.broadcasted_iota(jnp.int32, shape, dim)


def dot(left, right):
    return jnp.dot(left, right, preferred_element_type=jnp.float32)


def dot_nt(left, right):
    return lax.dot_general(
        left, right, (((1,), (1,)), ((), ())), preferred_element_type=jnp.float32
    )


def two_terms(values):
    high = values.astype(jnp.bfloat16)
    return high, (values - high.astype(jnp.float32)).astype(jnp.bfloat16)


def fine(left, right):
    left_high, left_low = two_terms(left)
    right_high, right_low = two_terms(right)
    left_terms = jnp.concatenate([left_high, left_low], axis=1)
    if right.shape[1] > 128:
        return dot(left_terms, jnp.concatenate([right_high, right_high], axis=0)) + dot(
            left_high, right_low
        )
    both = dot(
        left_terms,
        jnp.concatenate(
            [
                jnp.concatenate([right_high, right_low], axis=1),
                jnp.concatenate([right_high, jnp.zeros_like(right_low)], axis=1),
            ],
            axis=0,
        ),
    )
    return both[:, : right.shape[1]] + both[:, right.shape[1] :]


def fine_nt(left, right):
    left_high, left_low = two_terms(left)
    right_high, right_low = two_terms(right)
    return (
        dot_nt(left_high, right_high) + dot_nt(left_low, right_high) + dot_nt(left_high, right_low)
    )


def one_hot(mask):
    return jnp.where(mask, 1.0, 0.0).astype(jnp.bfloat16)


def picked(rows, source):
    return one_hot(source == iota((rows, rows), 1))


def forecast_and_analyse(
    heads,
    x_hbm,
    embed_hbm,
    qkv_hbm,
    comb_hbm,
    dec_hbm,
    scale_hbm,
    load_hbm,
    grid_hbm,
    dom_hbm,
    chan_hbm,
    read_hbm,
    noise_hbm,
    out_ref,
    x_ref,
    embed_ref,
    dec_ref,
    scale_ref,
    load_ref,
    grid_ref,
    dom_ref,
    chan_ref,
    read_ref,
    noise_ref,
    g_embed,
    g_qkv,
    g_comb,
    g_dec,
    x_pad,
    to_west,
    window,
    qkv_buf,
    ctx,
    from_west,
    lat_send,
    lat_recv,
    pos_send,
    pos_recv,
    w_send,
    w_recv,
    t_send,
    t_recv,
    a_send,
    a_recv,
    l_sem,
):
    bf16, f32 = jnp.bfloat16, jnp.float32
    me = lax.axis_index("mem")
    tile = lax.axis_index("tile")
    tiles = lax.axis_size("tile")
    n = lax.axis_size("mem")
    core = me % 2
    along_x = (me // 2) % 2
    along_y = me // 4
    to_sib = 1 - 2 * core
    sib = me + to_sib
    x_nb = me + 2 - 4 * along_x
    y_nb = me + 4 - 8 * along_y
    diag = x_nb + 4 - 8 * along_y
    odd = tile % 2
    partner = tile + 1 - 2 * odd
    west = (tile + tiles - 1) % tiles
    east = (tile + 1) % tiles

    tokens, span = window.shape
    half = tokens // 2
    feats = x_ref.shape[1]
    piece = feats // n
    padded = g_embed.shape[0] // n
    width = padded * n
    count = grid_ref.shape[2]
    variables = load_ref.shape[1]

    def own_rows(held):
        rows = held.shape[0] // n
        return held.at[pl.ds(pl.multiple_of(me * rows, 16), rows)]

    local = [
        pltpu.make_async_copy(source, target, l_sem.at[i])
        for i, (source, target) in enumerate(
            (
                (embed_hbm, embed_ref),
                (qkv_hbm, own_rows(g_qkv)),
                (x_hbm, x_ref),
                (comb_hbm, own_rows(g_comb)),
                (dec_hbm, dec_ref),
                (load_hbm, load_ref),
                (grid_hbm, grid_ref),
                (chan_hbm, chan_ref),
                (dom_hbm, dom_ref),
                (read_hbm, read_ref),
                (noise_hbm, noise_ref),
                (scale_hbm, scale_ref),
            )
        )
    ]
    for fetched in local:
        fetched.start()

    barrier = pltpu.get_barrier_semaphore()
    for step in range(1, n):
        pl.semaphore_signal(
            barrier, inc=1, device_id=((me + step) % n, tile), device_id_type=MESH
        )
    for other in (west, east):
        pl.semaphore_signal(barrier, inc=1, device_id=(me, other), device_id_type=MESH)

    gathered = (g_embed, g_qkv, g_comb, g_dec)
    sends = []

    def copy(w, kind, owner, first, rows, target):
        held = gathered[w]
        block = held.shape[0] // n
        part = held.at[pl.ds(pl.multiple_of(owner * block + first, 16), rows)]
        return pltpu.make_async_remote_copy(
            src_ref=part,
            dst_ref=part,
            send_sem=w_send.at[w * KINDS + kind],
            recv_sem=w_recv.at[w * KINDS + kind],
            device_id=target,
            device_id_type=MESH,
        )

    here = {
        "sib": (sib, tile),
        "x": (x_nb, tile),
        "y": (y_nb, tile),
        "z": (me, partner),
    }

    def send(w, kind, owner, first, rows, way):
        sent = copy(w, kind, owner, first, rows, here[way])
        sent.start()
        sends.append(sent)

    def arrived(w, kind, owner, first, rows):
        copy(w, kind, owner, first, rows, here["sib"]).wait_recv()

    def third(w):
        return gathered[w].shape[0] // n // 3

    def own_first(w):
        t = third(w)
        send(w, 1, me, 2 * odd * t, t, "x")
        send(w, 2, me, 2 * odd * t, t, "y")

    def own_second(w):
        t = third(w)
        send(w, 15, me, t, t, "x")
        send(w, 16, me, t, t, "y")
        send(w, 0, me, 0, 3 * t, "sib")

    def pass_first(w):
        t = third(w)
        arrived(w, 1, x_nb, 2 * odd * t, t)
        send(w, 5, x_nb, 2 * odd * t, t, "y")
        send(w, 9, x_nb, 2 * odd * t, t, "z")
        arrived(w, 2, y_nb, 2 * odd * t, t)
        send(w, 10, y_nb, 2 * odd * t, t, "z")

    def pass_second(w):
        t = third(w)
        arrived(w, 16, y_nb, t, t)
        send(w, 6, y_nb, t, t, "x")
        send(w, 4, y_nb, odd * t, 2 * t, "sib")
        arrived(w, 15, x_nb, t, t)
        send(w, 3, x_nb, odd * t, 2 * t, "sib")

    def pass_diagonal(w):
        t = third(w)
        arrived(w, 5, diag, 2 * odd * t, t)
        send(w, 11, diag, 2 * odd * t, t, "z")
        send(w, 7, diag, 2 * odd * t, t, "sib")
        arrived(w, 6, diag, t, t)
        send(w, 8, diag, t, t, "sib")

    def pass_partner(w):
        t = third(w)
        for kind, owner in ((9, x_nb), (10, y_nb), (11, diag)):
            arrived(w, kind, owner, 2 * (1 - odd) * t, t)
            send(w, kind + 3, owner, 2 * (1 - odd) * t, t, "sib")

    def complete(w):
        t = third(w)
        arrived(w, 0, sib, 0, 3 * t)
        arrived(w, 3, x_nb + to_sib, odd * t, 2 * t)
        arrived(w, 4, y_nb + to_sib, odd * t, 2 * t)
        arrived(w, 7, diag + to_sib, 2 * odd * t, t)
        arrived(w, 8, diag + to_sib, t, t)
        for kind, owner in ((12, x_nb), (13, y_nb), (14, diag)):
            arrived(w, kind, owner + to_sib, 2 * (1 - odd) * t, t)

    def own_whole(w):
        rows = gathered[w].shape[0] // n
        send(w, 1, me, 0, rows, "x")
        send(w, 2, me, 0, rows, "y")
        send(w, 0, me, 0, rows, "sib")

    def pass_whole(w):
        rows = gathered[w].shape[0] // n
        upper = rows // 32 * 16
        arrived(w, 1, x_nb, 0, rows)
        send(w, 5, x_nb, 0, upper, "y")
        send(w, 3, x_nb, 0, rows, "sib")
        arrived(w, 2, y_nb, 0, rows)
        send(w, 6, y_nb, upper, rows - upper, "x")
        send(w, 4, y_nb, 0, rows, "sib")

    def pass_corner(w):
        rows = gathered[w].shape[0] // n
        upper = rows // 32 * 16
        arrived(w, 5, diag, 0, upper)
        arrived(w, 6, diag, upper, rows - upper)
        send(w, 7, diag, 0, rows, "sib")

    def complete_whole(w):
        rows = gathered[w].shape[0] // n
        for kind, owner in ((0, me), (3, x_nb), (4, y_nb), (7, diag)):
            arrived(w, kind, owner + to_sib, 0, rows)

    def keep_own(w, ref):
        block = gathered[w].shape[0] // n
        rows = ref.shape[0] // 16 * 16
        gathered[w][pl.ds(pl.multiple_of(me * block, 16), rows), :] = ref[:rows, :]
        if rows < block:
            left = ref.shape[0] - rows
            mask = one_hot(iota((block - rows, left), 0) == iota((block - rows, left), 1))
            gathered[w][pl.ds(pl.multiple_of(me * block + rows, 16), block - rows), :] = dot(
                mask, ref[rows:, :]
            ).astype(bf16)

    EMBED, QKV, COMB, DEC = 0, 1, 2, 3

    local[0].wait()
    keep_own(EMBED, embed_ref)
    pl.semaphore_wait(barrier, n + 1)
    own_whole(EMBED)
    local[1].wait()
    own_first(QKV)
    for fetched in local[2:]:
        fetched.wait()

    row = iota((tokens, tokens), 0)
    by_half = picked(
        tokens,
        ((row >> 5) & 1) * 64 + ((row >> 2) & 7) * 8 + (row >> 6) * 4 + (row & 3),
    )
    x_rows = dot(by_half, x_ref[...]).astype(bf16)
    x_pad[...] = jnp.zeros(x_pad.shape, bf16)
    for d in range(n):
        x_pad[:, padded * d : padded * d + piece] = x_rows[:, piece * d : piece * (d + 1)]

    pass_whole(EMBED)
    own_second(QKV)
    keep_own(DEC, dec_ref)
    within = iota((n, padded, variables), 1)
    within = within - jnp.where(within >= variables, variables, 0)
    pick_variable = one_hot(within == iota((n, padded, variables), 2)).reshape(width, variables)
    channels = load_ref.shape[0]
    loads = dot_nt(pick_variable, load_ref[...]).astype(bf16)
    chan_hot = one_hot(jnp.broadcast_to(chan_ref[0], (channels, count)) == iota((channels, count), 0))
    mapping = dot(loads, chan_hot)
    grid_point = grid_ref[0]
    points = feats // variables
    token_row = grid_point >> 4
    point_row = grid_point & (points - 1)
    dom_row = dom_ref[0]
    slot = iota((n, padded, count), 0) * 2 + jnp.where(
        iota((n, padded, count), 1) >= variables, 1, 0
    )
    mapping = jnp.where(
        slot.reshape(width, count) == jnp.broadcast_to(point_row, (width, count)), mapping, 0.0
    ).astype(bf16)

    pass_corner(EMBED)
    pass_first(QKV)
    own_whole(COMB)
    complete_whole(EMBED)

    hidden = dot(x_pad[...], g_embed[...]).astype(bf16)
    normed = layer_norm(hidden).astype(bf16)
    to_west[...] = normed[:half]
    window[half:, :] = normed[half:]

    def along_tile(index, source, target, way):
        return pltpu.make_async_remote_copy(
            src_ref=source,
            dst_ref=target,
            send_sem=t_send.at[index],
            recv_sem=t_recv.at[index],
            device_id=(me, way),
            device_id_type=MESH,
        )

    westward = along_tile(0, to_west, window.at[pl.ds(0, half)], west)
    westward.start()
    sends.append(westward)

    pass_second(QKV)

    pass_diagonal(QKV)
    pass_whole(COMB)
    own_whole(DEC)
    pass_partner(QKV)
    complete(QKV)
    westward.wait_recv()
    qkv_buf[...] = dot_nt(window[...], g_qkv[...]).astype(bf16)
    pass_corner(COMB)

    side = span // heads
    pair = 2 * side
    one_head = iota((pair, pair), 0) // side == iota((pair, pair), 1) // side
    head_sum = one_hot(one_head)
    head_sums = jnp.concatenate([head_sum, head_sum], axis=0)
    lane = iota((tokens, pair), 1)
    first = jnp.where(lane < side, 1.0, 0.0).astype(bf16)
    second = jnp.where(lane < side, 0.0, 1.0).astype(bf16)
    share = jnp.concatenate([first, second], axis=0)
    key_of = iota((half, 2 * tokens), 1)
    same_member = ((iota((half, 2 * tokens), 0) >> 5) & 1) == ((key_of >> 5) & 1)

    def unit_pair(rows, start):
        values = qkv_buf[rows, start : start + pair].astype(f32)
        squares = jnp.concatenate(two_terms(values * values), axis=1)
        return (values * lax.rsqrt(dot(squares, head_sums) + normalizing_guard)).astype(bf16)

    def attend(rows, pairs):
        for p in pairs:
            start = pair * p
            query = unit_pair(rows, start)
            key = keys[p]
            scales = jnp.where(
                key_of < tokens,
                scale_ref[:, 2 * p : 2 * p + 1],
                scale_ref[:, 2 * p + 1 : 2 * p + 2],
            )
            weights = jnp.where(same_member, jnp.exp(dot_nt(query, key) * scales), 0.0).astype(bf16)
            value = qkv_buf[:, 2 * span + start : 2 * span + start + pair]
            value = jnp.concatenate([value * first, value * second], axis=0)
            total = dot(weights, jnp.concatenate([value, share], axis=1))
            ctx[rows, start : start + pair] = (total[:, :pair] / total[:, pair:]).astype(bf16)

    keys = []
    for p in range(heads // 2):
        key = unit_pair(slice(None), span + pair * p)
        keys.append(jnp.concatenate([key * first, key * second], axis=0))
    attend(slice(0, half), range(heads // 2))
    eastward = along_tile(1, ctx.at[pl.ds(0, half)], from_west, east)
    eastward.start()
    sends.append(eastward)
    attend(slice(half, tokens), range(heads // 2))
    pass_whole(DEC)
    complete_whole(COMB)
    by_region = picked(
        tokens,
        ((row >> 2) & 1) * 64 + ((row >> 3) & 1) * 32 + (row >> 4) * 4 + (row & 3),
    )
    eastward.wait_recv()
    context = jnp.concatenate([from_west[...], ctx[half:, :]], axis=0)
    mixed = hidden.astype(f32) + dot_nt(context, g_comb[...])
    latent = layer_norm(mixed).astype(bf16)
    lat_send[...] = dot(by_region, latent).astype(bf16)

    block = tokens // n

    def exchange(index, source, target):
        mine = pl.ds(pl.multiple_of(me * block, 16), block)
        for step in range(1, n):
            to = (me + step) % n
            sent = pltpu.make_async_remote_copy(
                src_ref=source.at[pl.ds(pl.multiple_of(to * block, 16), block)],
                dst_ref=target.at[mine],
                send_sem=a_send.at[index * n + step],
                recv_sem=a_recv.at[index * n + step],
                device_id=(to, tile),
                device_id_type=MESH,
            )
            sent.start()
            sends.append(sent)
        target[mine, :] = source[mine, :]

    def exchanged(index, source, target):
        for step in range(1, n):
            origin = (me + n - step) % n
            part = pl.ds(pl.multiple_of(origin * block, 16), block)
            pltpu.make_async_remote_copy(
                src_ref=source.at[part],
                dst_ref=target.at[part],
                send_sem=a_send.at[index * n + step],
                recv_sem=a_recv.at[index * n + step],
                device_id=(origin, tile),
                device_id_type=MESH,
            ).wait_recv()

    exchange(0, lat_send, lat_recv)
    pass_corner(DEC)
    regions = n
    members = tokens // regions
    region3 = iota((members, regions, count), 1)
    on_token = jnp.where(region3 == token_row[None], 1.0, 0.0)
    in_region = jnp.where(region3 == dom_row[None], 1.0, 0.0).reshape(tokens, count)
    distance = (token_row - dom_row).astype(f32)
    noise = noise_ref[0]
    obs_weight = jnp.exp(-0.5 * distance * distance) / (noise * noise)
    in_region_weight = in_region * obs_weight
    reading = read_ref[0]
    unit = jnp.where(row == iota((tokens, tokens), 1), 1.0, 0.0)
    same_region = (row & (regions - 1)) == (iota((tokens, tokens), 1) & (regions - 1))
    by_member = picked(tokens, ((row >> 3) & 7) * 16 + (row >> 6) * 8 + (row & 7))
    complete_whole(DEC)
    exchanged(0, lat_send, lat_recv)

    values = lat_recv[...]
    prior = dot_nt(values, g_dec[...]).astype(bf16)
    samples = dot(prior, mapping).reshape(members, regions, count)
    ens_obs = jnp.sum(samples * on_token, axis=1, keepdims=True)
    mean_obs = jnp.mean(ens_obs, axis=0, keepdims=True)
    pert = jnp.broadcast_to(ens_obs - mean_obs, samples.shape).reshape(tokens, count)
    innovation = reading - mean_obs[0]
    weighted = pert * in_region_weight
    pert = pert * in_region
    gram = fine_nt(weighted, pert)
    drive = fine_nt(jnp.broadcast_to(innovation, (tokens, count)), weighted)
    system = unit + gram * (1.0 / (members - 1.0))
    sums = jnp.sum(jnp.abs(system), axis=1, keepdims=True).reshape(members, regions, 1)
    bound = jnp.broadcast_to(
        jnp.max(sums, axis=0, keepdims=True), (members, regions, 1)
    ).reshape(tokens, 1)
    iterate = system / bound
    inverse_root = None
    for step in range(NS_ITERS):
        if step == 0:
            factor = 1.5 * unit - 0.5 * iterate
            inverse_root = factor
        else:
            factor = 1.5 * unit - 0.5 * fine(inverse_root, iterate)
            inverse_root = fine(factor, inverse_root)
        if step < NS_ITERS - 1:
            iterate = fine(iterate, factor)
    root = inverse_root * lax.rsqrt(bound)
    inner = fine(drive, root)
    mean_weight = fine(inner, root) * (1.0 / (members - 1.0))
    transform_back = jnp.where(same_region, root + mean_weight, 0.0)
    latents = values.astype(f32).reshape(members, regions, span)
    center = jnp.mean(latents, axis=0, keepdims=True)
    spread = (latents - center).reshape(tokens, span)
    posterior = jnp.broadcast_to(center, latents.shape).reshape(tokens, span) + fine(
        transform_back, spread
    )
    pos_send[...] = posterior.astype(bf16)
    exchange(1, pos_send, pos_recv)
    for sent in sends[: 1 - n]:
        sent.wait_send()
    exchanged(1, pos_send, pos_recv)
    analysed = dot_nt(dot(by_member, pos_recv[...]).astype(bf16), g_dec[...])
    for d in range(n):
        out_ref[:, piece * d : piece * (d + 1)] = analysed[
            :, padded * d : padded * d + piece
        ].astype(bf16)
    for sent in sends[1 - n :]:
        sent.wait_send()


def per_device_fused(
    starting_ensemble,
    patch_lifting,
    query_keyvalue_lift,
    output_combiner,
    decoder_linear_map,
    cosine_logit_scale,
    sensor_variable_loadings,
    *sensors,
):
    n = lax.axis_size("mem")
    members, rows, cols, feats = starting_ensemble.shape
    tokens = members * rows * cols
    span = patch_lifting.shape[1]
    padded = -(-patch_lifting.shape[0] // 48) * 48
    vmem = pl.BlockSpec(memory_space=pltpu.VMEM)
    hbm = pl.BlockSpec(memory_space=pltpu.HBM)

    def held(*shape):
        return pltpu.VMEM(shape, jnp.bfloat16)

    out = pl.pallas_call(
        functools.partial(forecast_and_analyse, cosine_logit_scale.shape[0]),
        out_shape=jax.ShapeDtypeStruct((tokens, feats), jnp.bfloat16),
        in_specs=[hbm] * 12,
        out_specs=vmem,
        scratch_shapes=[
            held(tokens, feats),
            held(*patch_lifting.shape),
            held(decoder_linear_map.shape[1], span),
            pltpu.VMEM((1, cosine_logit_scale.shape[0]), jnp.float32),
            held(*sensor_variable_loadings.shape),
            *[pltpu.VMEM(sensor.shape, sensor.dtype) for sensor in sensors],
            held(padded * n, span),
            held(query_keyvalue_lift.shape[1] * n, span),
            held(output_combiner.shape[1] * n, span),
            held(padded * n, span),
            held(tokens, padded * n),
            held(tokens // 2, span),
            held(tokens, span),
            held(tokens, 3 * span),
            held(tokens, span),
            held(tokens // 2, span),
            held(tokens, span),
            held(tokens, span),
            held(tokens, span),
            held(tokens, span),
            pltpu.SemaphoreType.DMA((4 * KINDS,)),
            pltpu.SemaphoreType.DMA((4 * KINDS,)),
            pltpu.SemaphoreType.DMA((2,)),
            pltpu.SemaphoreType.DMA((2,)),
            pltpu.SemaphoreType.DMA((2 * n,)),
            pltpu.SemaphoreType.DMA((2 * n,)),
            pltpu.SemaphoreType.DMA((12,)),
        ],
        compiler_params=pltpu.CompilerParams(
            collective_id=0, has_side_effects=True, vmem_limit_bytes=63 * 1024 * 1024
        ),
        cost_estimate=pl.CostEstimate(
            flops=2 * tokens * span * (3 * feats + 4 * span),
            bytes_accessed=16 * 1024 * 1024,
            transcendentals=0,
        ),
    )(
        starting_ensemble.reshape(tokens, feats),
        patch_lifting,
        query_keyvalue_lift.T,
        output_combiner.T,
        decoder_linear_map.T,
        cosine_logit_scale.reshape(1, -1),
        sensor_variable_loadings,
        *sensors,
    )
    return out.reshape(members, rows, cols, feats)


def fits_fused(mesh, starting_ensemble, patch_lifting, query_keyvalue_lift, output_combiner, loads):
    n, tiles = mesh.shape["mem"], mesh.shape["tile"]
    members, rows, cols, feats = starting_ensemble.shape
    return (
        n == 8
        and tiles % 2 == 0
        and tiles > 2
        and (members // n, rows, cols // tiles) == (2, 8, 8)
        and feats == 16 * loads.shape[1]
        and query_keyvalue_lift.shape[1] % (48 * n) == 0
        and output_combiner.shape[1] % (48 * n) == 0
    )


def solution(mesh):
    def whole(*args):
        fused = fits_fused(mesh, args[0], args[1], args[2], args[3], args[6])
        return jax.shard_map(
            per_device_fused if fused else per_device,
            mesh=mesh,
            in_specs=(
                P("mem", None, "tile", None),
                P("mem", None),
                P(None, "mem"),
                P(None, "mem"),
                P(None, "mem"),
                P(),
                P(),
                P("mem", "tile", None),
                P("mem", "tile", None),
                P("mem", "tile", None),
                P("mem", "tile", None),
                P("mem", "tile", None),
            ),
            out_specs=P("mem", None, "tile", None),
            check_vma=False,
        )(*args)

    return whole
```

```python
import functools

import jax
import jax.numpy as jnp
from jax import lax
from jax.experimental import pallas as pl
from jax.experimental.pallas import tpu as pltpu
from jax.sharding import PartitionSpec as P

PANE_SIDE = 8
NS_ITERS = 5
KINDS = 17
MESH = pl.DeviceIdType.MESH


eps_norm = 1e-05
normalizing_guard = 1e-06


def passed_along(value, axis, by):
    devices = lax.axis_size(axis)
    return lax.ppermute(value, axis, [(i, (i + by) % devices) for i in range(devices)])


def layer_norm(values):
    values = values.astype(jnp.float32)
    center = values - jnp.mean(values, axis=-1, keepdims=True)
    spread = jnp.mean(center * center, axis=-1, keepdims=True)
    return center * lax.rsqrt(spread + eps_norm)


def unit_rows(values):
    values = values.astype(jnp.float32)
    return (
        values * lax.rsqrt(jnp.sum(values * values, axis=-1, keepdims=True) + normalizing_guard)
    ).astype(jnp.bfloat16)


def pane_cosine_mixer(padded_part, query_keyvalue_lift, cosine_logit_scale):
    members, rows, cols, attention_span = padded_part.shape
    focus_groups = cosine_logit_scale.shape[0]
    head_dim = attention_span // focus_groups
    qkv = jnp.dot(
        padded_part.reshape(-1, attention_span),
        query_keyvalue_lift,
        preferred_element_type=jnp.float32,
    ).astype(jnp.bfloat16)
    qkv = qkv.reshape(
        members, rows // PANE_SIDE, PANE_SIDE, cols // PANE_SIDE, PANE_SIDE, 3 * attention_span
    )
    qkv = qkv.transpose(0, 1, 3, 2, 4, 5).reshape(
        -1, PANE_SIDE * PANE_SIDE, 3, focus_groups, head_dim
    )
    query = unit_rows(qkv[:, :, 0])
    key_rows = unit_rows(qkv[:, :, 1])
    value_rows = qkv[:, :, 2]
    affinity_logits = jnp.einsum(
        "bihd,bjhd->bhij", query, key_rows, preferred_element_type=jnp.float32
    )
    affinity_logits = affinity_logits * cosine_logit_scale[None, :, None, None]
    weights = jnp.exp(affinity_logits)
    probs = (weights / jnp.sum(weights, axis=-1, keepdims=True)).astype(jnp.bfloat16)
    mixed_outcome = jnp.einsum(
        "bhij,bjhd->bihd", probs, value_rows, preferred_element_type=jnp.float32
    )
    mixed_outcome = mixed_outcome.astype(jnp.bfloat16).reshape(
        members, rows // PANE_SIDE, cols // PANE_SIDE, PANE_SIDE, PANE_SIDE, attention_span
    )
    return mixed_outcome.transpose(0, 1, 3, 2, 4, 5).reshape(members, rows, cols, attention_span)


def batched(left, right):
    return jnp.einsum("rij,rjk->rik", left, right, precision=lax.Precision.HIGHEST)


def local_analysis(
    embedded_patches,
    decoder_linear_map,
    sensor_gridpoint,
    sensor_domain_index,
    sensor_channel_list,
    sensor_reading,
    sensor_noise_deviation,
    sensor_variable_loadings,
):
    members, regions, attention_span = embedded_patches.shape
    feats = decoder_linear_map.shape[1]
    channels, variables = sensor_variable_loadings.shape
    points = feats // variables
    count = sensor_gridpoint.shape[0]
    prior_member_grids = jnp.dot(
        embedded_patches.reshape(-1, attention_span),
        decoder_linear_map,
        preferred_element_type=jnp.float32,
    ).astype(jnp.bfloat16)
    token = sensor_gridpoint // points
    point = sensor_gridpoint - token * points
    pick_point = (point[:, None] == jnp.arange(points, dtype=jnp.int32)[None, :]).astype(
        jnp.float32
    )
    pick_chan = (
        sensor_channel_list[:, None] == jnp.arange(channels, dtype=jnp.int32)[None, :]
    ).astype(jnp.float32)
    rows_h = jnp.dot(
        pick_chan, sensor_variable_loadings.astype(jnp.float32), precision=lax.Precision.HIGHEST
    )
    measurement_mapping = (
        (pick_point[:, :, None] * rows_h[:, None, :]).reshape(count, feats).astype(jnp.bfloat16)
    )
    mapped_samples = lax.dot_general(
        prior_member_grids,
        measurement_mapping,
        (((1,), (1,)), ((), ())),
        preferred_element_type=jnp.float32,
    )
    mapped_samples = mapped_samples.reshape(members, regions, count)
    pick_token = (token[None, :] == jnp.arange(regions, dtype=jnp.int32)[:, None]).astype(
        jnp.float32
    )
    ens_obs = jnp.sum(mapped_samples * pick_token[None], axis=1)
    mean_obs = jnp.mean(ens_obs, axis=0)
    pert_obs = ens_obs - mean_obs[None, :]
    innovation = sensor_reading - mean_obs
    distance = (token - sensor_domain_index).astype(jnp.float32)
    obs_weight = jnp.exp(-0.5 * distance * distance) / (
        sensor_noise_deviation * sensor_noise_deviation
    )
    pick_region = (
        sensor_domain_index[:, None] == jnp.arange(regions, dtype=jnp.int32)[None, :]
    ).astype(jnp.float32)
    weighted = pert_obs * obs_weight[None, :]
    gram = jnp.einsum(
        "kj,jr,lj->rkl", weighted, pick_region, pert_obs, precision=lax.Precision.HIGHEST
    )
    drive = jnp.einsum(
        "kj,jr,j->rk", weighted, pick_region, innovation, precision=lax.Precision.HIGHEST
    )
    eye = jnp.eye(members, dtype=jnp.float32)
    system = eye[None] + gram / (members - 1.0)
    bound = jnp.max(jnp.sum(jnp.abs(system), axis=2), axis=1)
    iterate = system / bound[:, None, None]
    inverse_root = jnp.broadcast_to(eye, system.shape)
    for step in range(NS_ITERS):
        factor = 1.5 * eye[None] - 0.5 * batched(inverse_root, iterate)
        iterate = batched(iterate, factor)
        inverse_root = batched(factor, inverse_root)
    root = inverse_root * lax.rsqrt(bound)[:, None, None]
    inner = jnp.einsum("rkl,rl->rk", root, drive, precision=lax.Precision.HIGHEST)
    mean_weight = jnp.einsum("rkl,rl->rk", root, inner, precision=lax.Precision.HIGHEST) / (
        members - 1.0
    )
    transform_matrix = root + mean_weight[:, :, None]
    values = embedded_patches.astype(jnp.float32)
    center = jnp.mean(values, axis=0)
    spread = values - center[None]
    posterior = center[None] + jnp.einsum(
        "ktf,tkm->mtf", spread, transform_matrix, precision=lax.Precision.HIGHEST
    )
    return posterior.astype(jnp.bfloat16)


def per_device(
    starting_ensemble,
    patch_lifting,
    query_keyvalue_lift,
    output_combiner,
    decoder_linear_map,
    cosine_logit_scale,
    sensor_variable_loadings,
    sensor_gridpoint,
    sensor_domain_index,
    sensor_channel_list,
    sensor_reading,
    sensor_noise_deviation,
):
    members, rows, cols, feats = starting_ensemble.shape
    full_embed, entire_triplet_product, full_out, full_head = (
        lax.all_gather(patch_lifting, "mem", axis=0, tiled=True),
        lax.all_gather(query_keyvalue_lift, "mem", axis=1, tiled=True),
        lax.all_gather(output_combiner, "mem", axis=1, tiled=True),
        lax.all_gather(decoder_linear_map, "mem", axis=1, tiled=True),
    )
    attention_span = full_embed.shape[1]
    hidden = jnp.dot(
        starting_ensemble.reshape(-1, feats), full_embed, preferred_element_type=jnp.float32
    )
    hidden = hidden.astype(jnp.bfloat16).reshape(members, rows, cols, attention_span)
    normed = layer_norm(hidden).astype(jnp.bfloat16)
    half = PANE_SIDE // 2
    incoming_rows = passed_along(normed[:, :, :half], "tile", -1)
    padded_sequence = jnp.concatenate([normed[:, :, half:], incoming_rows], axis=2)
    mixed_outcome_padded = pane_cosine_mixer(
        padded_sequence, entire_triplet_product, cosine_logit_scale
    )
    returned = passed_along(mixed_outcome_padded[:, :, cols - half :], "tile", 1)
    mixed_outcome = jnp.concatenate([returned, mixed_outcome_padded[:, :, : cols - half]], axis=2)
    mixed = hidden.astype(jnp.float32) + jnp.dot(
        mixed_outcome.reshape(-1, attention_span), full_out, preferred_element_type=jnp.float32
    ).reshape(members, rows, cols, attention_span)
    embedded_patches = layer_norm(mixed).astype(jnp.bfloat16)
    tile_tokens = rows * cols
    moved = lax.all_to_all(
        embedded_patches.reshape(members, tile_tokens, attention_span),
        "mem",
        split_axis=1,
        concat_axis=0,
        tiled=True,
    )
    ensemble, regions = (moved.shape[0], moved.shape[1])
    posterior = local_analysis(
        moved,
        full_head,
        sensor_gridpoint.reshape(-1),
        sensor_domain_index.reshape(-1),
        sensor_channel_list.reshape(-1),
        sensor_reading.reshape(-1),
        sensor_noise_deviation.reshape(-1),
        sensor_variable_loadings,
    )
    produced = jnp.dot(
        posterior.reshape(-1, attention_span), full_head, preferred_element_type=jnp.float32
    )
    produced = produced.astype(jnp.bfloat16).reshape(ensemble, regions, feats)
    analysed = lax.all_to_all(produced, "mem", split_axis=0, concat_axis=1, tiled=True)
    return analysed.reshape(members, rows, cols, feats)


def iota(shape, dim):
    return lax.broadcasted_iota(jnp.int32, shape, dim)


def dot(left, right):
    return jnp.dot(left, right, preferred_element_type=jnp.float32)


def dot_nt(left, right):
    return lax.dot_general(
        left, right, (((1,), (1,)), ((), ())), preferred_element_type=jnp.float32
    )


def two_terms(values):
    high = values.astype(jnp.bfloat16)
    return high, (values - high.astype(jnp.float32)).astype(jnp.bfloat16)


def fine(left, right):
    left_high, left_low = two_terms(left)
    right_high, right_low = two_terms(right)
    left_terms = jnp.concatenate([left_high, left_low], axis=1)
    if right.shape[1] > 128:
        return dot(left_terms, jnp.concatenate([right_high, right_high], axis=0)) + dot(
            left_high, right_low
        )
    both = dot(
        left_terms,
        jnp.concatenate(
            [
                jnp.concatenate([right_high, right_low], axis=1),
                jnp.concatenate([right_high, jnp.zeros_like(right_low)], axis=1),
            ],
            axis=0,
        ),
    )
    return both[:, : right.shape[1]] + both[:, right.shape[1] :]


def fine_nt(left, right):
    left_high, left_low = two_terms(left)
    right_high, right_low = two_terms(right)
    return (
        dot_nt(left_high, right_high) + dot_nt(left_low, right_high) + dot_nt(left_high, right_low)
    )


def one_hot(mask):
    return jnp.where(mask, 1.0, 0.0).astype(jnp.bfloat16)


def picked(rows, source):
    return one_hot(source == iota((rows, rows), 1))


def forecast_and_analyse(
    heads,
    x_hbm,
    embed_hbm,
    qkv_hbm,
    comb_hbm,
    dec_hbm,
    scale_hbm,
    load_hbm,
    grid_hbm,
    dom_hbm,
    chan_hbm,
    read_hbm,
    noise_hbm,
    out_ref,
    x_ref,
    embed_ref,
    dec_ref,
    scale_ref,
    load_ref,
    grid_ref,
    dom_ref,
    chan_ref,
    read_ref,
    noise_ref,
    g_embed,
    g_qkv,
    g_comb,
    g_dec,
    x_pad,
    to_west,
    window,
    qkv_buf,
    ctx,
    from_west,
    lat_send,
    lat_recv,
    pos_send,
    pos_recv,
    w_send,
    w_recv,
    t_send,
    t_recv,
    a_send,
    a_recv,
    l_sem,
):
    bf16, f32 = jnp.bfloat16, jnp.float32
    me = lax.axis_index("mem")
    tile = lax.axis_index("tile")
    tiles = lax.axis_size("tile")
    n = lax.axis_size("mem")
    core = me % 2
    along_x = (me // 2) % 2
    along_y = me // 4
    to_sib = 1 - 2 * core
    sib = me + to_sib
    x_nb = me + 2 - 4 * along_x
    y_nb = me + 4 - 8 * along_y
    diag = x_nb + 4 - 8 * along_y
    odd = tile % 2
    partner = tile + 1 - 2 * odd
    west = (tile + tiles - 1) % tiles
    east = (tile + 1) % tiles

    tokens, span = window.shape
    half = tokens // 2
    feats = x_ref.shape[1]
    piece = feats // n
    padded = g_embed.shape[0] // n
    width = padded * n
    count = grid_ref.shape[2]
    variables = load_ref.shape[1]

    def own_rows(held):
        rows = held.shape[0] // n
        return held.at[pl.ds(pl.multiple_of(me * rows, 16), rows)]

    local = [
        pltpu.make_async_copy(source, target, l_sem.at[i])
        for i, (source, target) in enumerate(
            (
                (embed_hbm, embed_ref),
                (qkv_hbm, own_rows(g_qkv)),
                (x_hbm, x_ref),
                (comb_hbm, own_rows(g_comb)),
                (dec_hbm, dec_ref),
                (load_hbm, load_ref),
                (grid_hbm, grid_ref),
                (chan_hbm, chan_ref),
                (dom_hbm, dom_ref),
                (read_hbm, read_ref),
                (noise_hbm, noise_ref),
                (scale_hbm, scale_ref),
            )
        )
    ]
    for fetched in local:
        fetched.start()

    barrier = pltpu.get_barrier_semaphore()
    for step in range(1, n):
        pl.semaphore_signal(
            barrier, inc=1, device_id=((me + step) % n, tile), device_id_type=MESH
        )
    for other in (west, east):
        pl.semaphore_signal(barrier, inc=1, device_id=(me, other), device_id_type=MESH)

    gathered = (g_embed, g_qkv, g_comb, g_dec)
    sends = []

    def copy(w, kind, owner, first, rows, target):
        held = gathered[w]
        block = held.shape[0] // n
        part = held.at[pl.ds(pl.multiple_of(owner * block + first, 16), rows)]
        return pltpu.make_async_remote_copy(
            src_ref=part,
            dst_ref=part,
            send_sem=w_send.at[w * KINDS + kind],
            recv_sem=w_recv.at[w * KINDS + kind],
            device_id=target,
            device_id_type=MESH,
        )

    here = {
        "sib": (sib, tile),
        "x": (x_nb, tile),
        "y": (y_nb, tile),
        "z": (me, partner),
    }

    def send(w, kind, owner, first, rows, way):
        sent = copy(w, kind, owner, first, rows, here[way])
        sent.start()
        sends.append(sent)

    def arrived(w, kind, owner, first, rows):
        copy(w, kind, owner, first, rows, here["sib"]).wait_recv()

    def third(w):
        return gathered[w].shape[0] // n // 3

    def own_first(w):
        t = third(w)
        send(w, 1, me, 2 * odd * t, t, "x")
        send(w, 2, me, 2 * odd * t, t, "y")

    def own_second(w):
        t = third(w)
        send(w, 15, me, t, t, "x")
        send(w, 16, me, t, t, "y")
        send(w, 0, me, 0, 3 * t, "sib")

    def pass_first(w):
        t = third(w)
        arrived(w, 1, x_nb, 2 * odd * t, t)
        send(w, 5, x_nb, 2 * odd * t, t, "y")
        send(w, 9, x_nb, 2 * odd * t, t, "z")
        arrived(w, 2, y_nb, 2 * odd * t, t)
        send(w, 10, y_nb, 2 * odd * t, t, "z")

    def pass_second(w):
        t = third(w)
        arrived(w, 16, y_nb, t, t)
        send(w, 6, y_nb, t, t, "x")
        send(w, 4, y_nb, odd * t, 2 * t, "sib")
        arrived(w, 15, x_nb, t, t)
        send(w, 3, x_nb, odd * t, 2 * t, "sib")

    def pass_diagonal(w):
        t = third(w)
        arrived(w, 5, diag, 2 * odd * t, t)
        send(w, 11, diag, 2 * odd * t, t, "z")
        send(w, 7, diag, 2 * odd * t, t, "sib")
        arrived(w, 6, diag, t, t)
        send(w, 8, diag, t, t, "sib")

    def pass_partner(w):
        t = third(w)
        for kind, owner in ((9, x_nb), (10, y_nb), (11, diag)):
            arrived(w, kind, owner, 2 * (1 - odd) * t, t)
            send(w, kind + 3, owner, 2 * (1 - odd) * t, t, "sib")

    def complete(w):
        t = third(w)
        arrived(w, 0, sib, 0, 3 * t)
        arrived(w, 3, x_nb + to_sib, odd * t, 2 * t)
        arrived(w, 4, y_nb + to_sib, odd * t, 2 * t)
        arrived(w, 7, diag + to_sib, 2 * odd * t, t)
        arrived(w, 8, diag + to_sib, t, t)
        for kind, owner in ((12, x_nb), (13, y_nb), (14, diag)):
            arrived(w, kind, owner + to_sib, 2 * (1 - odd) * t, t)

    def own_whole(w):
        rows = gathered[w].shape[0] // n
        send(w, 1, me, 0, rows, "x")
        send(w, 2, me, 0, rows, "y")
        send(w, 0, me, 0, rows, "sib")

    def pass_whole(w):
        rows = gathered[w].shape[0] // n
        upper = rows // 32 * 16
        arrived(w, 1, x_nb, 0, rows)
        send(w, 5, x_nb, 0, upper, "y")
        send(w, 3, x_nb, 0, rows, "sib")
        arrived(w, 2, y_nb, 0, rows)
        send(w, 6, y_nb, upper, rows - upper, "x")
        send(w, 4, y_nb, 0, rows, "sib")

    def pass_corner(w):
        rows = gathered[w].shape[0] // n
        upper = rows // 32 * 16
        arrived(w, 5, diag, 0, upper)
        arrived(w, 6, diag, upper, rows - upper)
        send(w, 7, diag, 0, rows, "sib")

    def complete_whole(w):
        rows = gathered[w].shape[0] // n
        for kind, owner in ((0, me), (3, x_nb), (4, y_nb), (7, diag)):
            arrived(w, kind, owner + to_sib, 0, rows)

    def keep_own(w, ref):
        block = gathered[w].shape[0] // n
        rows = ref.shape[0] // 16 * 16
        gathered[w][pl.ds(pl.multiple_of(me * block, 16), rows), :] = ref[:rows, :]
        if rows < block:
            left = ref.shape[0] - rows
            mask = one_hot(iota((block - rows, left), 0) == iota((block - rows, left), 1))
            gathered[w][pl.ds(pl.multiple_of(me * block + rows, 16), block - rows), :] = dot(
                mask, ref[rows:, :]
            ).astype(bf16)

    EMBED, QKV, COMB, DEC = 0, 1, 2, 3

    local[0].wait()
    keep_own(EMBED, embed_ref)
    pl.semaphore_wait(barrier, n + 1)
    own_first(EMBED)
    own_second(EMBED)
    local[1].wait()
    own_first(QKV)
    for fetched in local[2:]:
        fetched.wait()

    row = iota((tokens, tokens), 0)
    by_half = picked(
        tokens,
        ((row >> 5) & 1) * 64 + ((row >> 2) & 7) * 8 + (row >> 6) * 4 + (row & 3),
    )
    x_rows = dot(by_half, x_ref[...]).astype(bf16)
    x_pad[...] = jnp.zeros(x_pad.shape, bf16)
    for d in range(n):
        x_pad[:, padded * d : padded * d + piece] = x_rows[:, piece * d : piece * (d + 1)]

    pass_first(EMBED)
    pass_second(EMBED)
    own_second(QKV)
    keep_own(DEC, dec_ref)
    within = iota((n, padded, variables), 1)
    within = within - jnp.where(within >= variables, variables, 0)
    pick_variable = one_hot(within == iota((n, padded, variables), 2)).reshape(width, variables)
    channels = load_ref.shape[0]
    loads = dot_nt(pick_variable, load_ref[...]).astype(bf16)
    chan_hot = one_hot(jnp.broadcast_to(chan_ref[0], (channels, count)) == iota((channels, count), 0))
    mapping = dot(loads, chan_hot)
    grid_point = grid_ref[0]
    points = feats // variables
    token_row = grid_point >> 4
    point_row = grid_point & (points - 1)
    dom_row = dom_ref[0]
    slot = iota((n, padded, count), 0) * 2 + jnp.where(
        iota((n, padded, count), 1) >= variables, 1, 0
    )
    mapping = jnp.where(
        slot.reshape(width, count) == jnp.broadcast_to(point_row, (width, count)), mapping, 0.0
    ).astype(bf16)

    pass_diagonal(EMBED)
    pass_first(QKV)
    pass_partner(EMBED)
    own_whole(COMB)
    complete(EMBED)

    hidden = dot(x_pad[...], g_embed[...]).astype(bf16)
    normed = layer_norm(hidden).astype(bf16)
    to_west[...] = normed[:half]
    window[half:, :] = normed[half:]

    def along_tile(index, source, target, way):
        return pltpu.make_async_remote_copy(
            src_ref=source,
            dst_ref=target,
            send_sem=t_send.at[index],
            recv_sem=t_recv.at[index],
            device_id=(me, way),
            device_id_type=MESH,
        )

    westward = along_tile(0, to_west, window.at[pl.ds(0, half)], west)
    westward.start()
    sends.append(westward)

    pass_second(QKV)

    pass_diagonal(QKV)
    pass_whole(COMB)
    own_whole(DEC)
    pass_partner(QKV)
    complete(QKV)
    westward.wait_recv()
    qkv_buf[...] = dot_nt(window[...], g_qkv[...]).astype(bf16)
    pass_corner(COMB)

    side = span // heads
    pair = 2 * side
    one_head = iota((pair, pair), 0) // side == iota((pair, pair), 1) // side
    head_sum = one_hot(one_head)
    head_sums = jnp.concatenate([head_sum, head_sum], axis=0)
    lane = iota((tokens, pair), 1)
    first = jnp.where(lane < side, 1.0, 0.0).astype(bf16)
    second = jnp.where(lane < side, 0.0, 1.0).astype(bf16)
    share = jnp.concatenate([first, second], axis=0)
    key_of = iota((half, 2 * tokens), 1)
    same_member = ((iota((half, 2 * tokens), 0) >> 5) & 1) == ((key_of >> 5) & 1)

    def unit_pair(rows, start):
        values = qkv_buf[rows, start : start + pair].astype(f32)
        squares = jnp.concatenate(two_terms(values * values), axis=1)
        return (values * lax.rsqrt(dot(squares, head_sums) + normalizing_guard)).astype(bf16)

    def attend(rows, pairs):
        for p in pairs:
            start = pair * p
            query = unit_pair(rows, start)
            key = keys[p]
            scales = jnp.where(
                key_of < tokens,
                scale_ref[:, 2 * p : 2 * p + 1],
                scale_ref[:, 2 * p + 1 : 2 * p + 2],
            )
            weights = jnp.where(same_member, jnp.exp(dot_nt(query, key) * scales), 0.0).astype(bf16)
            value = qkv_buf[:, 2 * span + start : 2 * span + start + pair]
            value = jnp.concatenate([value * first, value * second], axis=0)
            total = dot(weights, jnp.concatenate([value, share], axis=1))
            ctx[rows, start : start + pair] = (total[:, :pair] / total[:, pair:]).astype(bf16)

    keys = []
    for p in range(heads // 2):
        key = unit_pair(slice(None), span + pair * p)
        keys.append(jnp.concatenate([key * first, key * second], axis=0))
    attend(slice(0, half), range(heads // 2))
    eastward = along_tile(1, ctx.at[pl.ds(0, half)], from_west, east)
    eastward.start()
    sends.append(eastward)
    attend(slice(half, tokens), range(heads // 2))
    pass_whole(DEC)
    complete_whole(COMB)
    by_region = picked(
        tokens,
        ((row >> 2) & 1) * 64 + ((row >> 3) & 1) * 32 + (row >> 4) * 4 + (row & 3),
    )
    eastward.wait_recv()
    context = jnp.concatenate([from_west[...], ctx[half:, :]], axis=0)
    mixed = hidden.astype(f32) + dot_nt(context, g_comb[...])
    latent = layer_norm(mixed).astype(bf16)
    lat_send[...] = dot(by_region, latent).astype(bf16)

    block = tokens // n

    def exchange(index, source, target):
        mine = pl.ds(pl.multiple_of(me * block, 16), block)
        for step in range(1, n):
            to = (me + step) % n
            sent = pltpu.make_async_remote_copy(
                src_ref=source.at[pl.ds(pl.multiple_of(to * block, 16), block)],
                dst_ref=target.at[mine],
                send_sem=a_send.at[index * n + step],
                recv_sem=a_recv.at[index * n + step],
                device_id=(to, tile),
                device_id_type=MESH,
            )
            sent.start()
            sends.append(sent)
        target[mine, :] = source[mine, :]

    def exchanged(index, source, target):
        for step in range(1, n):
            origin = (me + n - step) % n
            part = pl.ds(pl.multiple_of(origin * block, 16), block)
            pltpu.make_async_remote_copy(
                src_ref=source.at[part],
                dst_ref=target.at[part],
                send_sem=a_send.at[index * n + step],
                recv_sem=a_recv.at[index * n + step],
                device_id=(origin, tile),
                device_id_type=MESH,
            ).wait_recv()

    exchange(0, lat_send, lat_recv)
    pass_corner(DEC)
    regions = n
    members = tokens // regions
    region3 = iota((members, regions, count), 1)
    on_token = jnp.where(region3 == token_row[None], 1.0, 0.0)
    in_region = jnp.where(region3 == dom_row[None], 1.0, 0.0).reshape(tokens, count)
    distance = (token_row - dom_row).astype(f32)
    noise = noise_ref[0]
    obs_weight = jnp.exp(-0.5 * distance * distance) / (noise * noise)
    in_region_weight = in_region * obs_weight
    reading = read_ref[0]
    unit = jnp.where(row == iota((tokens, tokens), 1), 1.0, 0.0)
    same_region = (row & (regions - 1)) == (iota((tokens, tokens), 1) & (regions - 1))
    by_member = picked(tokens, ((row >> 3) & 7) * 16 + (row >> 6) * 8 + (row & 7))
    complete_whole(DEC)
    exchanged(0, lat_send, lat_recv)

    values = lat_recv[...]
    prior = dot_nt(values, g_dec[...]).astype(bf16)
    samples = dot(prior, mapping).reshape(members, regions, count)
    ens_obs = jnp.sum(samples * on_token, axis=1, keepdims=True)
    mean_obs = jnp.mean(ens_obs, axis=0, keepdims=True)
    pert = jnp.broadcast_to(ens_obs - mean_obs, samples.shape).reshape(tokens, count)
    innovation = reading - mean_obs[0]
    weighted = pert * in_region_weight
    pert = pert * in_region
    gram = fine_nt(weighted, pert)
    drive = fine_nt(jnp.broadcast_to(innovation, (tokens, count)), weighted)
    system = unit + gram * (1.0 / (members - 1.0))
    sums = jnp.sum(jnp.abs(system), axis=1, keepdims=True).reshape(members, regions, 1)
    bound = jnp.broadcast_to(
        jnp.max(sums, axis=0, keepdims=True), (members, regions, 1)
    ).reshape(tokens, 1)
    iterate = system / bound
    inverse_root = None
    for step in range(NS_ITERS):
        if step == 0:
            factor = 1.5 * unit - 0.5 * iterate
            inverse_root = factor
        else:
            factor = 1.5 * unit - 0.5 * fine(inverse_root, iterate)
            inverse_root = fine(factor, inverse_root)
        if step < NS_ITERS - 1:
            iterate = fine(iterate, factor)
    root = inverse_root * lax.rsqrt(bound)
    inner = fine(drive, root)
    mean_weight = fine(inner, root) * (1.0 / (members - 1.0))
    transform_back = jnp.where(same_region, root + mean_weight, 0.0)
    latents = values.astype(f32).reshape(members, regions, span)
    center = jnp.mean(latents, axis=0, keepdims=True)
    spread = (latents - center).reshape(tokens, span)
    posterior = jnp.broadcast_to(center, latents.shape).reshape(tokens, span) + fine(
        transform_back, spread
    )
    pos_send[...] = posterior.astype(bf16)
    exchange(1, pos_send, pos_recv)
    for sent in sends[: 1 - n]:
        sent.wait_send()
    exchanged(1, pos_send, pos_recv)
    analysed = dot_nt(dot(by_member, pos_recv[...]).astype(bf16), g_dec[...])
    for d in range(n):
        out_ref[:, piece * d : piece * (d + 1)] = analysed[
            :, padded * d : padded * d + piece
        ].astype(bf16)
    for sent in sends[1 - n :]:
        sent.wait_send()


def per_device_fused(
    starting_ensemble,
    patch_lifting,
    query_keyvalue_lift,
    output_combiner,
    decoder_linear_map,
    cosine_logit_scale,
    sensor_variable_loadings,
    *sensors,
):
    n = lax.axis_size("mem")
    members, rows, cols, feats = starting_ensemble.shape
    tokens = members * rows * cols
    span = patch_lifting.shape[1]
    padded = -(-patch_lifting.shape[0] // 48) * 48
    vmem = pl.BlockSpec(memory_space=pltpu.VMEM)
    hbm = pl.BlockSpec(memory_space=pltpu.HBM)

    def held(*shape):
        return pltpu.VMEM(shape, jnp.bfloat16)

    out = pl.pallas_call(
        functools.partial(forecast_and_analyse, cosine_logit_scale.shape[0]),
        out_shape=jax.ShapeDtypeStruct((tokens, feats), jnp.bfloat16),
        in_specs=[hbm] * 12,
        out_specs=vmem,
        scratch_shapes=[
            held(tokens, feats),
            held(*patch_lifting.shape),
            held(decoder_linear_map.shape[1], span),
            pltpu.VMEM((1, cosine_logit_scale.shape[0]), jnp.float32),
            held(*sensor_variable_loadings.shape),
            *[pltpu.VMEM(sensor.shape, sensor.dtype) for sensor in sensors],
            held(padded * n, span),
            held(query_keyvalue_lift.shape[1] * n, span),
            held(output_combiner.shape[1] * n, span),
            held(padded * n, span),
            held(tokens, padded * n),
            held(tokens // 2, span),
            held(tokens, span),
            held(tokens, 3 * span),
            held(tokens, span),
            held(tokens // 2, span),
            held(tokens, span),
            held(tokens, span),
            held(tokens, span),
            held(tokens, span),
            pltpu.SemaphoreType.DMA((4 * KINDS,)),
            pltpu.SemaphoreType.DMA((4 * KINDS,)),
            pltpu.SemaphoreType.DMA((2,)),
            pltpu.SemaphoreType.DMA((2,)),
            pltpu.SemaphoreType.DMA((2 * n,)),
            pltpu.SemaphoreType.DMA((2 * n,)),
            pltpu.SemaphoreType.DMA((12,)),
        ],
        compiler_params=pltpu.CompilerParams(
            collective_id=0, has_side_effects=True, vmem_limit_bytes=63 * 1024 * 1024
        ),
        cost_estimate=pl.CostEstimate(
            flops=2 * tokens * span * (3 * feats + 4 * span),
            bytes_accessed=16 * 1024 * 1024,
            transcendentals=0,
        ),
    )(
        starting_ensemble.reshape(tokens, feats),
        patch_lifting,
        query_keyvalue_lift.T,
        output_combiner.T,
        decoder_linear_map.T,
        cosine_logit_scale.reshape(1, -1),
        sensor_variable_loadings,
        *sensors,
    )
    return out.reshape(members, rows, cols, feats)


def fits_fused(mesh, starting_ensemble, patch_lifting, query_keyvalue_lift, output_combiner, loads):
    n, tiles = mesh.shape["mem"], mesh.shape["tile"]
    members, rows, cols, feats = starting_ensemble.shape
    return (
        n == 8
        and tiles % 2 == 0
        and tiles > 2
        and (members // n, rows, cols // tiles) == (2, 8, 8)
        and feats == 16 * loads.shape[1]
        and query_keyvalue_lift.shape[1] % (48 * n) == 0
        and output_combiner.shape[1] % (48 * n) == 0
    )


def solution(mesh):
    def whole(*args):
        fused = fits_fused(mesh, args[0], args[1], args[2], args[3], args[6])
        return jax.shard_map(
            per_device_fused if fused else per_device,
            mesh=mesh,
            in_specs=(
                P("mem", None, "tile", None),
                P("mem", None),
                P(None, "mem"),
                P(None, "mem"),
                P(None, "mem"),
                P(),
                P(),
                P("mem", "tile", None),
                P("mem", "tile", None),
                P("mem", "tile", None),
                P("mem", "tile", None),
                P("mem", "tile", None),
            ),
            out_specs=P("mem", None, "tile", None),
            check_vma=False,
        )(*args)

    return whole
```
